128 devices in a mesh: dp: 16 (over x_lo, z, core), sp: 8 (over y, x_hi).
Axes of the slice: x: 4 (x_hi: 2, x_lo: 2; x = x_hi * 2 + x_lo), y: 4, z: 4, core: 2. Of those that a mesh axis runs over, the one named last changes fastest.
Arguments:
- tokens: bfloat16 [16384, 2048], P(('dp', 'sp')), may hold values from -6 to 6
- cotangent: bfloat16 [16384, 2048], P(('dp', 'sp')), may hold values from -6 to 6
- seq_lengths: int32 [16, 2], P('dp'), may hold values from 1 to 1023, as said below
- adapter_ids: int32 [16, 2], P('dp'), may hold values from 0 to 7
- norm_gain: float32 [2048], replicated, may hold values from 0.5 to 1.5
- ffn_gain: float32 [2048], replicated, may hold values from 0.5 to 1.5
- gate_gain: float32 [3072], replicated, may hold values from 0.5 to 1.5
- conv_weight: float32 [4, 3584], replicated, may hold values from -3 to 3
- conv_bias: float32 [3584], replicated, may hold values from -3 to 3
- dt_bias: float32 [48], replicated, may hold values from -3 to 0.5
- decay_log: float32 [48], replicated, may hold values from -7 to -2
- skip_gain: float32 [48], replicated, may hold values from 0.5 to 1.5
- frozen_input_weight: bfloat16 [2048, 8240], P('dp'), may hold values from -0.125 to 0.125
- input_adapter_lower: bfloat16 [2048, 128], P('dp'), may hold values from -0.125 to 0.125
- input_adapter_upper: bfloat16 [128, 8240], P('dp'), may hold values from -1.5 to 1.5
- frozen_output_weight: bfloat16 [4096, 2048], P('dp'), may hold values from -0.1875 to 0.1875
- output_adapter_lower: bfloat16 [4096, 128], P('dp'), may hold values from -0.09375 to 0.09375
- output_adapter_upper: bfloat16 [128, 2048], P('dp'), may hold values from -1.5 to 1.5
- frozen_gate_up_weight: bfloat16 [2048, 8192], P('dp'), may hold values from -0.125 to 0.125
- gate_up_adapter_lower: bfloat16 [2048, 128], P('dp'), may hold values from -0.125 to 0.125
- gate_up_adapter_upper: bfloat16 [128, 8192], P('dp'), may hold values from -1.5 to 1.5
- frozen_down_weight: bfloat16 [4096, 2048], P('dp'), may hold values from -0.09375 to 0.09375
- down_adapter_lower: bfloat16 [4096, 128], P('dp'), may hold values from -0.09375 to 0.09375
- down_adapter_upper: bfloat16 [128, 2048], P('dp'), may hold values from -1.5 to 1.5
Outputs:
- layer_out: bfloat16 [16384, 2048], P(('dp', 'sp'))
- grad_tokens: bfloat16 [16384, 2048], P(('dp', 'sp'))
- grad_a_in: float32 [2048, 128], P('dp')
- grad_b_in: float32 [128, 8240], P('dp')
- grad_a_out: float32 [4096, 128], P('dp')
- grad_b_out: float32 [128, 2048], P('dp')
- grad_a_gu: float32 [2048, 128], P('dp')
- grad_b_gu: float32 [128, 8192], P('dp')
- grad_a_down: float32 [4096, 128], P('dp')
- grad_b_down: float32 [128, 2048], P('dp')
The draws below stay inside these ranges and needn't reach their ends.
Inputs may be any that keep to these rules, and one draw needn't show every extreme that they name: `seq_lengths`: each row sums to 1024; one of its two lengths is at most 64.
All inputs are finite; a program needn't handle non-finite values.
Results may differ from the reference program's by a relative error of at most 0.023.
Values may be sent and summed in bfloat16 or wider, within the bound.
No kernel may reach another device: no remote copies, remote signals or barrier semaphores. Data moves between devices by JAX's collectives and lax.ppermute only.
A program may use at most 320 MiB of HBM per device.

```python
import jax
import jax.numpy as jnp
from jax import lax

MODEL_WIDTH = 2048
H_Q = 8
H_KV = 2
HEAD = 128
M_HEADS = 48
CONV = 4
HIDDEN_UNITS = 4096
ADAPTER_RANK = 16
ADAPTER_SETS = 8
SEQS = 2
GROUP_TOK = 1024
SPAN = 128
ATT_BLOCK = 512
GROUPS = 16
TOKENS = 16384
SHORT_MAX = 64
D_SSM = 3072
SHARED = 1024
INPUT_COLUMNS = 8240
MIXER_ROWS = 4096
CONV_CH = 3584
ADAPTER_COLUMNS = 128


def draw_seq_lengths(key, part):
    key = jax.random.fold_in(key, 11)
    short_key, order_key = jax.random.split(key)
    short_drawn = jax.random.randint(short_key, (GROUPS,), 1, SHORT_MAX + 1)
    short_length = jnp.where(jnp.arange(GROUPS) == 0, 1, short_drawn)
    order_bits = jax.random.randint(order_key, (GROUPS,), 0, 2)
    first_length = jnp.where(order_bits == 1, short_length, GROUP_TOK - short_length)
    return jnp.stack([first_length, GROUP_TOK - first_length], axis=1).astype(jnp.int32)


def set_ends(entries, own_key, low, high):
    longest = entries.shape.index(max(entries.shape))
    spots = []
    for shift in (0, 1):
        where = [jax.random.randint(jax.random.fold_in(own_key, axis), (), 0, length) for axis, length in enumerate(entries.shape)]
        where[longest] = (where[longest] + shift) % entries.shape[longest]
        spots.append(tuple(where))
    return entries.at[spots[0]].set(low).at[spots[1]].set(high)


def steps_of(own_key, dims, cuts, least, largest):
    def one(axis_at, shards_of):
        steps = jax.random.uniform(jax.random.fold_in(jax.random.fold_in(own_key, 6), axis_at), (shards_of,), jnp.float32, least / len(cuts), largest / len(cuts))
        return jnp.repeat(jnp.exp(steps), dims[axis_at] // shards_of).reshape((-1,) + (1,) * (len(dims) - axis_at - 1))

    gain = one(*cuts[0])
    for cut in cuts[1:]:
        gain = gain * one(*cut)
    return gain


def gaussian(rng, shape, scale, limit, cuts=(), held_as=jnp.bfloat16):
    values = scale * jax.random.normal(rng, shape, jnp.float32)
    if cuts:
        values = values * steps_of(rng, shape, cuts, -0.22, 0.18)
    return jnp.clip(values, -limit, limit).astype(held_as)


def setup_inputs(seed: int = 0) -> dict:
    streams_of = jax.random.split(jax.random.key(seed), 25)
    tokens = gaussian(streams_of[0], (TOKENS, MODEL_WIDTH), 1.0, 6.0, ((0, 128),))
    cotangent = gaussian(streams_of[1], (TOKENS, MODEL_WIDTH), 1.0, 6.0, ((0, 128),))
    seq_lengths = draw_seq_lengths(jax.random.fold_in(streams_of[24], 71), 0)
    adapter_ids = set_ends(jax.random.randint(streams_of[3], (GROUPS, SEQS), 0, ADAPTER_SETS), jax.random.fold_in(streams_of[3], 1), 0, ADAPTER_SETS - 1).astype(jnp.int32)
    norm_gain = jnp.clip(1.0 + 0.1 * jax.random.normal(streams_of[4], (MODEL_WIDTH,), jnp.float32), 0.5, 1.5)
    ffn_gain = jnp.clip(1.0 + 0.1 * jax.random.normal(streams_of[5], (MODEL_WIDTH,), jnp.float32), 0.5, 1.5)
    gate_gain = jnp.clip(1.0 + 0.1 * jax.random.normal(streams_of[6], (D_SSM,), jnp.float32), 0.5, 1.5)
    conv_weight = gaussian(streams_of[7], (CONV, CONV_CH), CONV ** -0.5, 3.0, (), jnp.float32)
    conv_bias = gaussian(streams_of[8], (CONV_CH,), 0.5, 3.0, (), jnp.float32)
    dt_bias = jnp.clip(jax.random.uniform(streams_of[9], (M_HEADS,), jnp.float32, -3.0, 0.5), -3.0, 0.5)
    decay_log = jnp.clip(jax.random.uniform(streams_of[10], (M_HEADS,), jnp.float32, -7.0, -2.0), -7.0, -2.0)
    skip_gain = jnp.clip(jax.random.uniform(streams_of[11], (M_HEADS,), jnp.float32, 0.5, 1.5), 0.5, 1.5)
    frozen_input_weight = gaussian(streams_of[12], (MODEL_WIDTH, INPUT_COLUMNS), MODEL_WIDTH ** -0.5, 0.125, ((0, 16),))
    input_adapter_lower = gaussian(streams_of[13], (MODEL_WIDTH, ADAPTER_COLUMNS), MODEL_WIDTH ** -0.5, 0.125, ((0, 16),))
    input_adapter_upper = gaussian(streams_of[14], (ADAPTER_COLUMNS, INPUT_COLUMNS), ADAPTER_RANK ** -0.5, 1.5, ((0, 16),))
    frozen_output_weight = gaussian(streams_of[15], (MIXER_ROWS, MODEL_WIDTH), (H_Q * HEAD) ** -0.5, 0.1875, ((0, 16),))
    output_adapter_lower = gaussian(streams_of[16], (MIXER_ROWS, ADAPTER_COLUMNS), MIXER_ROWS ** -0.5, 0.09375, ((0, 16),))
    output_adapter_upper = gaussian(streams_of[17], (ADAPTER_COLUMNS, MODEL_WIDTH), ADAPTER_RANK ** -0.5, 1.5, ((0, 16),))
    frozen_gate_up_weight = gaussian(streams_of[18], (MODEL_WIDTH, 2 * HIDDEN_UNITS), MODEL_WIDTH ** -0.5, 0.125, ((0, 16),))
    gate_up_adapter_lower = gaussian(streams_of[19], (MODEL_WIDTH, ADAPTER_COLUMNS), MODEL_WIDTH ** -0.5, 0.125, ((0, 16),))
    gate_up_adapter_upper = gaussian(streams_of[20], (ADAPTER_COLUMNS, 2 * HIDDEN_UNITS), ADAPTER_RANK ** -0.5, 1.5, ((0, 16),))
    frozen_down_weight = gaussian(streams_of[21], (HIDDEN_UNITS, MODEL_WIDTH), HIDDEN_UNITS ** -0.5, 0.09375, ((0, 16),))
    down_adapter_lower = gaussian(streams_of[22], (HIDDEN_UNITS, ADAPTER_COLUMNS), HIDDEN_UNITS ** -0.5, 0.09375, ((0, 16),))
    down_adapter_upper = gaussian(streams_of[23], (ADAPTER_COLUMNS, MODEL_WIDTH), ADAPTER_RANK ** -0.5, 1.5, ((0, 16),))
    return {"tokens": tokens, "cotangent": cotangent, "seq_lengths": seq_lengths, "adapter_ids": adapter_ids, "norm_gain": norm_gain, "ffn_gain": ffn_gain, "gate_gain": gate_gain, "conv_weight": conv_weight, "conv_bias": conv_bias, "dt_bias": dt_bias, "decay_log": decay_log, "skip_gain": skip_gain, "frozen_input_weight": frozen_input_weight, "input_adapter_lower": input_adapter_lower, "input_adapter_upper": input_adapter_upper, "frozen_output_weight": frozen_output_weight, "output_adapter_lower": output_adapter_lower, "output_adapter_upper": output_adapter_upper, "frozen_gate_up_weight": frozen_gate_up_weight, "gate_up_adapter_lower": gate_up_adapter_lower, "gate_up_adapter_upper": gate_up_adapter_upper, "frozen_down_weight": frozen_down_weight, "down_adapter_lower": down_adapter_lower, "down_adapter_upper": down_adapter_upper}


epsilon = 1e-05
rope_base = 100000000000.0
masked_score = -1e+30
highest = lax.Precision.HIGHEST

@jax.custom_vjp
def reduced_rank(v):
    return lax.optimization_barrier(v.astype(jnp.bfloat16)).astype(jnp.float32)

@jax.custom_vjp
def reduced_rank_gradient(v):
    return v

def low_keep(v):
    return (reduced_rank(v), None)

def low_pass(kept, grad):
    return (grad,)

def back_keep(v):
    return (v, None)

def back_low(kept, grad):
    return (reduced_rank(grad),)
reduced_rank.defvjp(low_keep, low_pass)
reduced_rank_gradient.defvjp(back_keep, back_low)

def matrix_product(product_operand, weight_matrix):
    return jnp.dot(product_operand, weight_matrix, precision=highest, preferred_element_type=jnp.float32)

def rms_scale(vectors, scale_gain):
    return vectors * lax.rsqrt(lax.optimization_barrier(jnp.mean(vectors * vectors, axis=-1, keepdims=True)) + epsilon) * scale_gain

def silu_value(vectors):
    return vectors * jax.nn.sigmoid(vectors)

def softplus_value(vectors):
    return jnp.log1p(jnp.exp(-jnp.abs(vectors))) + jnp.maximum(vectors, 0.0)

def rotary_tables(position, width):
    half_width = width // 2
    frequency = rope_base ** (-(jnp.arange(half_width).astype(jnp.float32) * 2.0 / width))
    angle = position.astype(jnp.float32)[:, None] * frequency[None, :]
    return (jnp.cos(angle), jnp.sin(angle))

def rotate(vectors, cosine_table, sine_table):
    half_width = vectors.shape[-1] // 2
    first_half = vectors[..., :half_width]
    second_half = vectors[..., half_width:]
    return jnp.concatenate([first_half * cosine_table - second_half * sine_table, second_half * cosine_table + first_half * sine_table], axis=-1)

def causal_conv(signal, weight_matrix, bias_row, segment):
    length_all = signal.shape[0]
    summed_conv = bias_row[None, :] + weight_matrix[CONV - 1][None, :] * signal
    for offset in range(1, CONV):
        moved_rows = jnp.pad(signal, ((offset, 0), (0, 0)))[:length_all]
        earlier = jnp.pad(segment, (offset, 0), constant_values=-1)[:length_all]
        summed_conv = summed_conv + weight_matrix[CONV - 1 - offset][None, :] * jnp.where((earlier == segment)[:, None], moved_rows, 0.0)
    return summed_conv

def state_scan(inner_heads, step_rates, log_decay, inputs_b, outputs_c, segment, skip_gain):
    length_all, head_count, head_dim = inner_heads.shape
    span_total = length_all // SPAN
    span_index = jnp.arange(SPAN)
    causal = span_index[:, None] >= span_index[None, :]

    def span_step(running, pieces):
        state_now, previous = running
        span_inner, span_rate, span_decay, span_in, span_out, span_seg = pieces
        cumulative = jnp.cumsum(span_decay, axis=0)
        same_seq = ((span_seg[:, None] == span_seg[None, :]) & causal)[:, :, None]
        gap_log = cumulative[:, None, :] - cumulative[None, :, :]
        decay_mask = jnp.where(same_seq, jnp.exp(jnp.where(same_seq, gap_log, 0.0)), 0.0)
        mixing = jnp.einsum('in,jn->ij', span_out, span_in, precision=highest)
        weighted = span_inner * span_rate[:, :, None]
        within_span = jnp.einsum('ij,ijh,jhp->ihp', mixing, decay_mask, weighted, precision=highest)
        carried = (span_seg == previous).astype(jnp.float32)
        from_state = jnp.einsum('in,hpn->ihp', span_out, state_now, precision=highest)
        from_state = from_state * (jnp.exp(cumulative) * carried[:, None])[:, :, None]
        result = within_span + from_state + skip_gain[None, :, None] * span_inner
        last_seg = span_seg[-1]
        tail_weight = jnp.where((span_seg == last_seg)[:, None], jnp.exp(cumulative[-1][None, :] - cumulative), 0.0) * span_rate
        keep_state = jnp.exp(cumulative[-1]) * (last_seg == previous).astype(jnp.float32)
        new_state = state_now * keep_state[:, None, None] + jnp.einsum('jh,jhp,jn->hpn', tail_weight, span_inner, span_in, precision=highest)
        return ((new_state, last_seg), result)
    state_start = jnp.zeros((head_count, head_dim, inputs_b.shape[1]), jnp.float32)
    pieces = (inner_heads.reshape(span_total, SPAN, head_count, head_dim), step_rates.reshape(span_total, SPAN, head_count), log_decay.reshape(span_total, SPAN, head_count), inputs_b.reshape(span_total, SPAN, -1), outputs_c.reshape(span_total, SPAN, -1), segment.reshape(span_total, SPAN))
    running, results = lax.scan(jax.checkpoint(span_step), (state_start, jnp.int32(-1)), pieces)
    return results.reshape(length_all, head_count, head_dim)

def mamba_local(inner_part, step_part, shared_bc, conv_x, bias_x, conv_bc, bias_bc, dt_shift, decay_rate, skip_gain, segment):
    length_all = inner_part.shape[0]
    head_count = dt_shift.shape[0]
    x_in = silu_value(causal_conv(inner_part, conv_x, bias_x, segment)).reshape(length_all, head_count, -1)
    states_in = silu_value(causal_conv(shared_bc, conv_bc, bias_bc, segment))
    state_cols = states_in.shape[1] // 2
    step_rates = softplus_value(step_part + dt_shift[None, :])
    log_decay = -step_rates * jnp.exp(decay_rate)[None, :]
    scanned = state_scan(x_in, step_rates, log_decay, states_in[:, :state_cols], states_in[:, state_cols:], segment, skip_gain)
    return scanned.reshape(length_all, -1)

def merge_branches(attended, scanned, gate_input, scale_gain):
    gated = scanned * silu_value(gate_input)
    return jnp.concatenate([attended, rms_scale(gated, scale_gain)], axis=1)

def adapted_output(product_operand, weight_matrix, lowering_matrix, raising_matrix, adapter_column_mask):
    lowered_portion = reduced_rank_gradient(reduced_rank(matrix_product(product_operand, lowering_matrix)) * adapter_column_mask)
    return reduced_rank_gradient(matrix_product(product_operand, weight_matrix) + matrix_product(lowered_portion, raising_matrix))

def attention_group(queries, keys, values, segment, position):
    cosine_table, sine_table = rotary_tables(position, HEAD)
    query_rot = reduced_rank(rotate(queries, cosine_table[:, None, :], sine_table[:, None, :]))
    key_rot = reduced_rank(rotate(keys, cosine_table[:, None, :], sine_table[:, None, :]))
    key_full = jnp.repeat(key_rot, H_Q // H_KV, axis=1)
    value_full = jnp.repeat(values, H_Q // H_KV, axis=1)
    score_scale = HEAD ** (-0.5)
    group_index = jnp.arange(GROUP_TOK)

    def score_block(first_row):
        query_block = lax.dynamic_slice_in_dim(query_rot, first_row, ATT_BLOCK, 0)
        rows_block = first_row + jnp.arange(ATT_BLOCK)
        seg_block = lax.dynamic_slice_in_dim(segment, first_row, ATT_BLOCK, 0)
        scores = reduced_rank_gradient(jnp.einsum('bhd,khd->hbk', query_block, key_full, precision=highest) * score_scale)
        allowed = (group_index[None, :] <= rows_block[:, None]) & (segment[None, :] == seg_block[:, None])
        scores = jnp.where(allowed[None], scores, masked_score)
        row_peak = lax.optimization_barrier(jnp.max(scores, axis=-1, keepdims=True))
        exponent = jnp.exp(scores - row_peak)
        probability = exponent / lax.optimization_barrier(jnp.sum(exponent, axis=-1, keepdims=True))
        return jnp.einsum('hbk,khd->bhd', reduced_rank(probability), value_full, precision=highest)
    blocks = lax.map(jax.checkpoint(score_block), jnp.arange(GROUP_TOK // ATT_BLOCK) * ATT_BLOCK)
    return blocks.reshape(GROUP_TOK, H_Q * HEAD)

def layer_forward(hidden, adapters, lengths, set_ids, frozen, small_params):
    frozen_input_weight, frozen_output_weight, frozen_gate_up_weight, frozen_down_weight = frozen
    input_adapter_lower, input_adapter_upper, output_adapter_lower, output_adapter_upper, gate_up_adapter_lower, gate_up_adapter_upper, down_adapter_lower, down_adapter_upper = adapters
    norm_gain, ffn_gain, gate_gain, conv_weight, conv_bias, dt_bias, decay_log, skip_gain = small_params
    group_index = jnp.arange(GROUP_TOK)
    segment = (group_index >= lengths[0]).astype(jnp.int32)
    position = group_index - lengths[0] * segment
    token_adapter_set = jnp.where(segment == 1, set_ids[1], set_ids[0])
    adapter_column_mask = (jnp.arange(ADAPTER_SETS * ADAPTER_RANK)[None, :] // ADAPTER_RANK == token_adapter_set[:, None]).astype(jnp.float32)
    input_reduced = reduced_rank(rms_scale(hidden, norm_gain))
    projected_input = adapted_output(input_reduced, frozen_input_weight, input_adapter_lower, input_adapter_upper, adapter_column_mask)
    edge_one = H_Q * HEAD
    edge_two = edge_one + D_SSM
    edge_three = edge_two + SHARED
    edge_four = edge_three + D_SSM
    queries = reduced_rank(projected_input[:, :edge_one])
    inner_part = reduced_rank(projected_input[:, edge_one:edge_two])
    shared = reduced_rank(projected_input[:, edge_two:edge_three])
    gate_input = projected_input[:, edge_three:edge_four]
    step_part = reduced_rank(projected_input[:, edge_four:])
    kv_cols = 2 * H_KV * HEAD
    keys = shared[:, :H_KV * HEAD].reshape(GROUP_TOK, H_KV, HEAD)
    values = shared[:, H_KV * HEAD:kv_cols].reshape(GROUP_TOK, H_KV, HEAD)
    attended = reduced_rank_gradient(reduced_rank(attention_group(queries.reshape(GROUP_TOK, H_Q, HEAD), keys, values, segment, position)))
    scanned = reduced_rank_gradient(reduced_rank(mamba_local(inner_part, step_part, shared[:, kv_cols:], conv_weight[:, :D_SSM], conv_bias[:D_SSM], conv_weight[:, D_SSM:], conv_bias[D_SSM:], dt_bias, decay_log, skip_gain, segment)))
    mixer_output = merge_branches(attended, scanned, gate_input, gate_gain)
    adapter_branch = adapted_output(reduced_rank(mixer_output), frozen_output_weight, output_adapter_lower, output_adapter_upper, adapter_column_mask)
    residual = hidden + adapter_branch
    gate_up_reduced = reduced_rank(rms_scale(residual, ffn_gain))
    gate_and_up = adapted_output(gate_up_reduced, frozen_gate_up_weight, gate_up_adapter_lower, gate_up_adapter_upper, adapter_column_mask)
    activated_hidden = silu_value(gate_and_up[:, :HIDDEN_UNITS]) * gate_and_up[:, HIDDEN_UNITS:]
    feedforward_output = adapted_output(reduced_rank(activated_hidden), frozen_down_weight, down_adapter_lower, down_adapter_upper, adapter_column_mask)
    return residual + feedforward_output

def reference(tokens, cotangent, seq_lengths, adapter_ids, norm_gain, ffn_gain, gate_gain, conv_weight, conv_bias, dt_bias, decay_log, skip_gain, frozen_input_weight, input_adapter_lower, input_adapter_upper, frozen_output_weight, output_adapter_lower, output_adapter_upper, frozen_gate_up_weight, gate_up_adapter_lower, gate_up_adapter_upper, frozen_down_weight, down_adapter_lower, down_adapter_upper):
    frozen = tuple((matrix.astype(jnp.float32) for matrix in (frozen_input_weight, frozen_output_weight, frozen_gate_up_weight, frozen_down_weight)))
    adapters = tuple((matrix.astype(jnp.float32) for matrix in (input_adapter_lower, input_adapter_upper, output_adapter_lower, output_adapter_upper, gate_up_adapter_lower, gate_up_adapter_upper, down_adapter_lower, down_adapter_upper)))
    small_params = (norm_gain, ffn_gain, gate_gain, conv_weight, conv_bias, dt_bias, decay_log, skip_gain)
    hidden_all = tokens.astype(jnp.float32).reshape(GROUPS, GROUP_TOK, MODEL_WIDTH)
    upstream_all = cotangent.astype(jnp.float32).reshape(GROUPS, GROUP_TOK, MODEL_WIDTH)

    def one_group(totals, inputs):
        hidden, upstream, lengths, set_ids = inputs

        def forward_group(hidden_in, adapter_in):
            return layer_forward(hidden_in, adapter_in, lengths, set_ids, frozen, small_params)
        result, pullback = jax.vjp(forward_group, hidden, adapters)
        grad_hidden, grad_adapters = pullback(upstream)
        totals = tuple((running + addend for running, addend in zip(totals, grad_adapters)))
        return (totals, (result.astype(jnp.bfloat16), grad_hidden.astype(jnp.bfloat16)))
    start_totals = tuple((jnp.zeros(matrix.shape, jnp.float32) for matrix in adapters))
    totals, (outputs, grads_in) = lax.scan(one_group, start_totals, (hidden_all, upstream_all, seq_lengths, adapter_ids))
    return (outputs.reshape(TOKENS, MODEL_WIDTH), grads_in.reshape(TOKENS, MODEL_WIDTH), totals[0], totals[1], totals[2], totals[3], totals[4], totals[5], totals[6], totals[7])
```

```python
from functools import partial

import jax
import jax.numpy as jnp
from jax import lax
from jax.sharding import PartitionSpec as P

H_Q = 8
H_KV = 2
HEAD = 128
M_HEADS = 48
M_HEAD = 64
CONV = 4
ADAPTER_RANK = 16
ADAPTER_SETS = 8
SPAN = 128
ATT_BLOCK = 512
D_SSM = 3072
SHARED = 1024
ADAPTERS = ADAPTER_RANK * ADAPTER_SETS

Y_RING = 4
X_PAIR = 2
SEQ = 8
DP = 16
HEADS_DEV = 6
INNER = HEADS_DEV * M_HEAD
SLICE = HEAD + INNER
MIX = X_PAIR * SLICE
UNITS = 1024

COL_Q = 0
COL_INNER = COL_Q + HEAD
COL_GATE = COL_INNER + INNER
COL_K = COL_GATE + INNER
COL_V = COL_K + HEAD
COL_BC = COL_V + HEAD
COL_STEP = COL_BC + 512
IN_COLS = COL_STEP + 128

EDGE_INNER = H_Q * HEAD
EDGE_SHARED = EDGE_INNER + D_SSM
EDGE_GATE = EDGE_SHARED + SHARED
EDGE_STEP = EDGE_GATE + D_SSM

epsilon = 1e-05
rope_base = 100000000000.0
masked_score = -1e30
highest = lax.Precision.HIGHEST
bf16 = jnp.bfloat16
f32 = jnp.float32


def rms_scale(vectors, scale_gain):
    return (
        vectors
        * lax.rsqrt(jnp.mean(vectors * vectors, axis=-1, keepdims=True) + epsilon)
        * scale_gain
    )


def silu_value(vectors):
    return vectors * jax.nn.sigmoid(vectors)


def softplus_value(vectors):
    return jnp.log1p(jnp.exp(-jnp.abs(vectors))) + jnp.maximum(vectors, 0.0)


def swiglu(gate_and_up):
    half_width = gate_and_up.shape[1] // 2
    return silu_value(gate_and_up[:, :half_width]) * gate_and_up[:, half_width:]


def rotary_tables(position, width):
    half_width = width // 2
    frequency = rope_base ** (-(jnp.arange(half_width).astype(f32) * 2.0 / width))
    angle = position.astype(f32)[:, None] * frequency[None, :]
    return (jnp.cos(angle), jnp.sin(angle))


def rotate(vectors, cosine_table, sine_table):
    half_width = vectors.shape[-1] // 2
    first_half = vectors[..., :half_width]
    second_half = vectors[..., half_width:]
    return jnp.concatenate(
        [
            first_half * cosine_table - second_half * sine_table,
            second_half * cosine_table + first_half * sine_table,
        ],
        axis=-1,
    )


def rotate_back(grads_rot, cosine_table, sine_table):
    return rotate(grads_rot, cosine_table, -sine_table)


def causal_conv(signal, weight_matrix, bias_row, segment):
    length_all = signal.shape[0]
    summed_conv = bias_row[None, :] + weight_matrix[CONV - 1][None, :] * signal
    for offset in range(1, CONV):
        moved_rows = jnp.pad(signal, ((offset, 0), (0, 0)))[:length_all]
        earlier = jnp.pad(segment, (offset, 0), constant_values=-1)[:length_all]
        summed_conv = summed_conv + weight_matrix[CONV - 1 - offset][None, :] * jnp.where(
            (earlier == segment)[:, None], moved_rows, 0.0
        )
    return summed_conv


def state_scan(inner_heads, step_rates, log_decay, inputs_b, outputs_c, segment, skip_gain):
    length_all, head_count, head_dim = inner_heads.shape
    span_total = length_all // SPAN
    span_index = jnp.arange(SPAN)
    causal = span_index[:, None] >= span_index[None, :]

    def span_step(running, pieces):
        state_now, previous = running
        span_inner, span_rate, span_decay, span_in, span_out, span_seg = pieces
        cumulative = jnp.cumsum(span_decay, axis=0)
        same_seq = ((span_seg[:, None] == span_seg[None, :]) & causal)[:, :, None]
        gap_log = cumulative[:, None, :] - cumulative[None, :, :]
        decay_mask = jnp.where(same_seq, jnp.exp(jnp.where(same_seq, gap_log, 0.0)), 0.0)
        mixing = jnp.einsum("in,jn->ij", span_out, span_in, precision=highest)
        weighted = span_inner * span_rate[:, :, None]
        within_span = jnp.einsum("ij,ijh,jhp->ihp", mixing, decay_mask, weighted, precision=highest)
        carried = (span_seg == previous).astype(f32)
        from_state = jnp.einsum("in,hpn->ihp", span_out, state_now, precision=highest)
        from_state = from_state * (jnp.exp(cumulative) * carried[:, None])[:, :, None]
        result = within_span + from_state + skip_gain[None, :, None] * span_inner
        last_seg = span_seg[-1]
        tail_weight = (
            jnp.where(
                (span_seg == last_seg)[:, None], jnp.exp(cumulative[-1][None, :] - cumulative), 0.0
            )
            * span_rate
        )
        keep_state = jnp.exp(cumulative[-1]) * (last_seg == previous).astype(f32)
        new_state = state_now * keep_state[:, None, None] + jnp.einsum(
            "jh,jhp,jn->hpn", tail_weight, span_inner, span_in, precision=highest
        )
        return ((new_state, last_seg), result)

    state_start = jnp.zeros((head_count, head_dim, inputs_b.shape[1]), f32)
    pieces = (
        inner_heads.reshape(span_total, SPAN, head_count, head_dim),
        step_rates.reshape(span_total, SPAN, head_count),
        log_decay.reshape(span_total, SPAN, head_count),
        inputs_b.reshape(span_total, SPAN, -1),
        outputs_c.reshape(span_total, SPAN, -1),
        segment.reshape(span_total, SPAN),
    )
    running, results = lax.scan(jax.checkpoint(span_step), (state_start, jnp.int32(-1)), pieces)
    return results.reshape(length_all, head_count, head_dim)


def mamba_local(
    inner_part,
    step_part,
    shared_bc,
    conv_x,
    bias_x,
    conv_bc,
    bias_bc,
    dt_shift,
    decay_rate,
    skip_gain,
    segment,
):
    length_all = inner_part.shape[0]
    head_count = dt_shift.shape[0]
    x_in = silu_value(causal_conv(inner_part, conv_x, bias_x, segment)).reshape(
        length_all, head_count, -1
    )
    states_in = silu_value(causal_conv(shared_bc, conv_bc, bias_bc, segment))
    state_cols = states_in.shape[1] // 2
    step_rates = softplus_value(step_part + dt_shift[None, :])
    log_decay = -step_rates * jnp.exp(decay_rate)[None, :]
    scanned = state_scan(
        x_in,
        step_rates,
        log_decay,
        states_in[:, :state_cols],
        states_in[:, state_cols:],
        segment,
        skip_gain,
    )
    return scanned.reshape(length_all, -1)


def product(left, right):
    return jnp.dot(left, right, preferred_element_type=f32)


def contract_last(left, right):
    return lax.dot_general(left, right, (((1,), (1,)), ((), ())), preferred_element_type=f32)


def contract_first(left, right):
    return lax.dot_general(left, right, (((0,), (0,)), ((), ())), preferred_element_type=f32)


def hop(value, target):
    return lax.ppermute(value, "sp", [(i, target(i)) for i in range(SEQ)])


def up(i):
    return (i + X_PAIR) % SEQ


def down(i):
    return (i - X_PAIR) % SEQ


def side(i):
    return i ^ 1


def gather_ring(block):
    half = block.shape[0] // 2
    below = hop(block, up)
    above = hop(block, down)
    far_first = hop(below[:half], up)
    far_second = hop(above[half:], down)
    return jnp.concatenate([block, above, far_first, far_second, below], axis=0)


def scatter_ring(partial_rows):
    n = partial_rows.shape[0] // Y_RING
    half = n // 2
    far = partial_rows[2 * n : 3 * n].astype(bf16)
    from_below = hop(far[:half], up).astype(f32)
    from_above = hop(far[half:], down).astype(f32)
    to_up = partial_rows[n : 2 * n]
    to_up = jnp.concatenate([to_up[:half] + from_below, to_up[half:]], axis=0).astype(bf16)
    to_down = partial_rows[3 * n :]
    to_down = jnp.concatenate([to_down[:half], to_down[half:] + from_above], axis=0).astype(bf16)
    low = hop(to_up, up).astype(f32)
    high = hop(to_down, down).astype(f32)
    return partial_rows[:n] + low + high


def gather_seq(block):
    copies = jnp.broadcast_to(block[None], (SEQ,) + block.shape)
    return lax.all_to_all(copies, "sp", split_axis=0, concat_axis=0).reshape(
        (SEQ * block.shape[0],) + block.shape[1:]
    )


def scatter_seq(partial_rows):
    n = partial_rows.shape[0] // SEQ
    pieces = partial_rows.astype(bf16).reshape((SEQ, n) + partial_rows.shape[1:])
    return jnp.sum(
        lax.all_to_all(pieces, "sp", split_axis=0, concat_axis=0).astype(f32), axis=0
    )


def sum_seq_small(value):
    total = value
    for offset in range(1, SEQ):
        total = total + hop(value, lambda i, offset=offset: (i + offset) % SEQ)
    return total


def per_device(
    tokens,
    cotangent,
    seq_lengths,
    adapter_ids,
    norm_gain,
    ffn_gain,
    gate_gain,
    conv_weight,
    conv_bias,
    dt_bias,
    decay_log,
    skip_gain,
    frozen_input_weight,
    input_adapter_lower,
    input_adapter_upper,
    frozen_output_weight,
    output_adapter_lower,
    output_adapter_upper,
    frozen_gate_up_weight,
    gate_up_adapter_lower,
    gate_up_adapter_upper,
    frozen_down_weight,
    down_adapter_lower,
    down_adapter_upper,
):
    s = lax.axis_index("sp")
    d = lax.axis_index("dp")
    y = s // X_PAIR
    x = s % X_PAIR
    tok_count = tokens.shape[0]
    group_len = tok_count * SEQ
    first_len = seq_lengths[0, 0]
    set_ids = adapter_ids[0]

    def adapter_mask(token_index):
        resident = jnp.where(token_index >= first_len, set_ids[1], set_ids[0])
        return jnp.arange(ADAPTERS)[None, :] // ADAPTER_RANK == resident[:, None]

    group_index = jnp.arange(group_len)
    segment = (group_index >= first_len).astype(jnp.int32)
    position = group_index - first_len * segment
    mask_all = adapter_mask(group_index)
    ring_blocks = X_PAIR * ((y + jnp.arange(Y_RING)) % Y_RING) + x
    ring_index = (ring_blocks[:, None] * tok_count + jnp.arange(tok_count)[None, :]).reshape(-1)
    mask_ring = adapter_mask(ring_index)

    def head_columns(values):
        lead = values.shape[:-1]
        grouped = values.reshape(lead + (12, Y_RING, M_HEAD))
        grouped = lax.dynamic_slice_in_dim(grouped, HEADS_DEV * x, HEADS_DEV, len(lead))
        grouped = lax.dynamic_index_in_dim(grouped, y, len(lead) + 1, keepdims=False)
        return grouped.reshape(lead + (INNER,))

    def head_items(values):
        lead = values.shape[:-1]
        grouped = values.reshape(lead + (12, Y_RING))
        grouped = lax.dynamic_slice_in_dim(grouped, HEADS_DEV * x, HEADS_DEV, len(lead))
        return lax.dynamic_index_in_dim(grouped, y, len(lead) + 1, keepdims=False)

    kv_head = s // (H_Q // H_KV)

    def input_columns(rows):
        return jnp.concatenate(
            [
                lax.dynamic_slice_in_dim(rows, s * HEAD, HEAD, 1),
                head_columns(rows[:, EDGE_INNER:EDGE_SHARED]),
                head_columns(rows[:, EDGE_GATE:EDGE_STEP]),
                lax.dynamic_slice_in_dim(rows, EDGE_SHARED + kv_head * HEAD, HEAD, 1),
                lax.dynamic_slice_in_dim(rows, EDGE_SHARED + (H_KV + kv_head) * HEAD, HEAD, 1),
                rows[:, EDGE_SHARED + 2 * H_KV * HEAD : EDGE_GATE],
                jnp.pad(head_items(rows[:, EDGE_STEP:]), ((0, 0), (0, 128 - HEADS_DEV))),
            ],
            axis=1,
        )

    def unit_columns(rows):
        grouped = rows.reshape(rows.shape[0], 2, DP, Y_RING, 64)
        return lax.dynamic_index_in_dim(grouped, y, 3, keepdims=False).reshape(rows.shape[0], -1)

    def gather_rows(rows):
        return lax.all_gather(rows, "dp", axis=0, tiled=True)

    in_upper = input_columns(input_adapter_upper)
    in_all = gather_rows(
        jnp.concatenate(
            [
                input_columns(frozen_input_weight),
                input_adapter_lower,
                in_upper.reshape(128, -1),
            ],
            axis=1,
        )
    )
    in_weight = in_all[:, : IN_COLS + ADAPTERS]
    in_raise = in_all[:, IN_COLS + ADAPTERS :].reshape(ADAPTERS, IN_COLS)

    out_rows = jnp.concatenate([frozen_output_weight, output_adapter_lower], axis=1)
    piece = lax.dynamic_slice_in_dim(out_rows, 64 * y, 64, 0)
    spread = jnp.zeros_like(piece)
    for k in range(1, Y_RING):
        block = lax.dynamic_slice_in_dim(out_rows, 64 * ((y + k) % Y_RING), 64, 0)
        pairs = [((i // 2) * SEQ + i, ((i // 2 + k) % Y_RING) * SEQ + i) for i in range(SEQ)]
        spread = spread + lax.ppermute(block, ("dp", "sp"), pairs)
    own_rows = (d >= Y_RING) | (d == y)
    out_all = gather_rows(
        jnp.concatenate(
            [jnp.where(own_rows, piece, spread), output_adapter_upper.reshape(64, -1)], axis=1
        )
    )
    model = frozen_output_weight.shape[1]
    out_weight = out_all[:, : model + ADAPTERS]
    out_raise = out_all[:, model + ADAPTERS :].reshape(ADAPTERS, model)

    down_rows = lax.dynamic_slice_in_dim(frozen_down_weight, 64 * y, 64, 0)
    down_lower = lax.dynamic_slice_in_dim(down_adapter_lower, 64 * y, 64, 0)
    ffn_all = gather_rows(
        jnp.concatenate(
            [
                unit_columns(frozen_gate_up_weight),
                gate_up_adapter_lower,
                unit_columns(gate_up_adapter_upper).reshape(128, -1),
                jnp.concatenate([down_rows[:, : model // 2], down_rows[:, model // 2 :]], axis=0),
                down_adapter_upper.reshape(128, -1),
                jnp.concatenate([down_lower, jnp.zeros_like(down_lower)], axis=0),
            ],
            axis=1,
        )
    )
    gu_weight = ffn_all[:, : 2 * UNITS + ADAPTERS]
    edge = 2 * UNITS + ADAPTERS
    gu_raise = ffn_all[:, edge : edge + 128].reshape(ADAPTERS, 2 * UNITS)
    edge += 128
    folded = ffn_all[:, edge : edge + model // 2].reshape(DP, 2, 64, model // 2)
    edge += model // 2
    down_raise = ffn_all[:, edge : edge + 128].reshape(ADAPTERS, model)
    edge += 128
    lowers = ffn_all[:, edge:].reshape(DP, 2, 64, ADAPTERS)
    down_weight = jnp.concatenate(
        [
            folded[:, 0].reshape(UNITS, -1),
            folded[:, 1].reshape(UNITS, -1),
            lowers[:, 0].reshape(UNITS, -1),
        ],
        axis=1,
    )

    def masked(lowered, mask):
        return jnp.where(mask, lowered, 0.0).astype(bf16)

    def forward(left, weight, raising, mask):
        both = product(left, weight)
        width = raising.shape[1]
        lowered = masked(both[:, width:], mask)
        return both[:, :width] + product(lowered, raising), lowered

    def backward(left, lowered, upstream, weight, raising, mask):
        gradient_lowered = masked(contract_last(upstream, raising), mask)
        grad_raise = contract_first(lowered, upstream)
        grad_lower = contract_first(left, gradient_lowered)
        grad_left = contract_last(jnp.concatenate([upstream, gradient_lowered], axis=1), weight)
        return grad_left, grad_lower, grad_raise

    hidden = tokens.astype(f32)
    normed, norm_back = jax.vjp(partial(rms_scale, scale_gain=norm_gain), hidden)
    left_in = gather_seq(normed.astype(bf16))
    cot_ring = gather_ring(cotangent)
    projected, lower_in = forward(left_in, in_weight, in_raise, mask_all)

    gate_input = projected[:, COL_GATE:COL_K]
    mamba_fn = partial(
        mamba_local,
        conv_x=head_columns(conv_weight[:, :D_SSM]),
        bias_x=head_columns(conv_bias[:D_SSM]),
        conv_bc=conv_weight[:, D_SSM:],
        bias_bc=conv_bias[D_SSM:],
        dt_shift=head_items(dt_bias),
        decay_rate=head_items(decay_log),
        skip_gain=head_items(skip_gain),
        segment=segment,
    )
    scanned, scan_back = jax.vjp(
        mamba_fn,
        projected[:, COL_INNER:COL_GATE].astype(bf16).astype(f32),
        projected[:, COL_STEP : COL_STEP + HEADS_DEV].astype(bf16).astype(f32),
        projected[:, COL_BC:COL_STEP].astype(bf16).astype(f32),
    )
    scanned = scanned.astype(bf16).astype(f32)
    key_one = projected[:, COL_K:COL_V].astype(bf16)
    value_one = projected[:, COL_V:COL_BC].astype(bf16)
    cosine_table, sine_table = rotary_tables(position, HEAD)
    query_rot = rotate(
        projected[:, COL_Q:COL_INNER].astype(bf16).astype(f32), cosine_table, sine_table
    ).astype(bf16)
    key_rot = rotate(key_one.astype(f32), cosine_table, sine_table).astype(bf16)
    score_scale = HEAD ** (-0.5)
    block_count = group_len // ATT_BLOCK
    block_starts = jnp.arange(block_count) * ATT_BLOCK

    def block_scores(first_row):
        query_block = lax.dynamic_slice_in_dim(query_rot, first_row, ATT_BLOCK, 0)
        rows_block = first_row + jnp.arange(ATT_BLOCK)
        seg_block = lax.dynamic_slice_in_dim(segment, first_row, ATT_BLOCK, 0)
        scores = contract_last(query_block, key_rot) * score_scale
        allowed = (group_index[None, :] <= rows_block[:, None]) & (
            segment[None, :] == seg_block[:, None]
        )
        return (query_block, jnp.where(allowed, scores, masked_score))

    def attend_block(first_row):
        query_block, scores = block_scores(first_row)
        row_peak = jnp.max(scores, axis=-1, keepdims=True)
        exponent = jnp.exp(scores - row_peak)
        row_total = jnp.sum(exponent, axis=-1, keepdims=True)
        probability = (exponent / row_total).astype(bf16)
        block_out = product(probability, value_one)
        return (block_out.astype(bf16), row_peak[..., 0] + jnp.log(row_total[..., 0]))

    attended_blocks, log_totals = lax.map(attend_block, block_starts)
    attended = attended_blocks.reshape(group_len, HEAD)

    gate_silu, gate_back = jax.vjp(silu_value, gate_input)
    gated = scanned * gate_silu
    squares = sum_seq_small(jnp.sum(gated * gated, axis=1).reshape(SEQ, tok_count)).reshape(-1)
    inverse = lax.rsqrt(squares / D_SSM + epsilon)[:, None]
    gain_part = head_columns(gate_gain)[None, :]
    normed_gated = gated * inverse * gain_part
    mixed = jnp.concatenate([attended, normed_gated.astype(bf16)], axis=1)

    def to_ring(values):
        doubled = jnp.concatenate([values, values], axis=0)
        rolled = lax.dynamic_slice_in_dim(doubled, X_PAIR * tok_count * y, group_len, 0)
        return rolled.reshape(Y_RING, X_PAIR, tok_count, -1)

    def from_ring(values):
        flat = values.reshape(group_len, -1)
        doubled = jnp.concatenate([flat, flat], axis=0)
        start = X_PAIR * tok_count * ((Y_RING - y) % Y_RING)
        return lax.dynamic_slice_in_dim(doubled, start, group_len, 0)

    ring_len = Y_RING * tok_count
    mixed_ring = to_ring(mixed)
    kept = lax.dynamic_index_in_dim(mixed_ring, x, 1, keepdims=False).reshape(ring_len, SLICE)
    other = lax.dynamic_index_in_dim(mixed_ring, 1 - x, 1, keepdims=False).reshape(ring_len, SLICE)
    received = hop(other, side)
    low = jnp.where(x == 0, kept, received)
    high = jnp.where(x == 0, received, kept)
    left_out = jnp.concatenate([low[:, :HEAD], high[:, :HEAD], low[:, HEAD:], high[:, HEAD:]], axis=1)
    branch_part, lower_out = forward(left_out, out_weight, out_raise, mask_ring)
    residual = hidden + scatter_ring(branch_part)
    normed_ffn, ffn_norm_back = jax.vjp(partial(rms_scale, scale_gain=ffn_gain), residual)
    left_gu = gather_ring(normed_ffn.astype(bf16))
    gate_and_up, lower_gu = forward(left_gu, gu_weight, gu_raise, mask_ring)
    activated_hidden, act_back = jax.vjp(swiglu, gate_and_up)
    left_down = activated_hidden.astype(bf16)
    ffn_part, lower_down = forward(left_down, down_weight, down_raise, mask_ring)
    layer_out = (residual + scatter_ring(ffn_part)).astype(bf16)

    grad_act, grad_a_down, grad_b_down = backward(
        left_down, lower_down, cot_ring, down_weight, down_raise, mask_ring
    )
    (grad_gate_up,) = act_back(grad_act)
    grad_gu_part, grad_a_gu, grad_b_gu = backward(
        left_gu, lower_gu, grad_gate_up.astype(bf16), gu_weight, gu_raise, mask_ring
    )
    (grad_resid_norm,) = ffn_norm_back(scatter_ring(grad_gu_part))
    grad_residual = cotangent.astype(f32) + grad_resid_norm
    grad_ring = gather_ring(grad_residual.astype(bf16))
    grad_mixed, grad_a_out, grad_b_out = backward(
        left_out, lower_out, grad_ring, out_weight, out_raise, mask_ring
    )
    grad_mixed = grad_mixed.astype(bf16)
    low = jnp.concatenate([grad_mixed[:, :HEAD], grad_mixed[:, 2 * HEAD : 2 * HEAD + INNER]], axis=1)
    high = jnp.concatenate([grad_mixed[:, HEAD : 2 * HEAD], grad_mixed[:, 2 * HEAD + INNER :]], axis=1)
    kept = jnp.where(x == 0, low, high)
    received = hop(jnp.where(x == 0, high, low), side)
    first = jnp.where(x == 0, kept, received).reshape(Y_RING, 1, tok_count, SLICE)
    second = jnp.where(x == 0, received, kept).reshape(Y_RING, 1, tok_count, SLICE)
    head_grads = from_ring(jnp.concatenate([first, second], axis=1))
    grad_attended = head_grads[:, :HEAD]
    grad_normed = head_grads[:, HEAD:].astype(f32) * gain_part
    slope = sum_seq_small(
        jnp.sum(grad_normed * gated, axis=1).reshape(SEQ, tok_count)
    ).reshape(-1, 1)
    grad_gated = inverse * grad_normed - gated * (inverse * inverse * inverse * slope / D_SSM)
    (grad_gate,) = gate_back(grad_gated * scanned)
    grad_scanned = (grad_gated * gate_silu).astype(bf16).astype(f32)
    grad_inner, grad_steps, grad_bc = scan_back(grad_scanned)

    grad_out_blocks = grad_attended.reshape(block_count, ATT_BLOCK, HEAD)

    def back_block(running, pieces):
        first_row, grad_block, log_block = pieces
        query_block, scores = block_scores(first_row)
        probability = jnp.exp(scores - log_block[..., None])
        grad_prob = contract_last(grad_block, value_one)
        row_delta = jnp.sum(probability * grad_prob, axis=-1, keepdims=True)
        dscore = (probability * (grad_prob - row_delta)).astype(bf16)
        grad_query_block = product(dscore, key_rot) * score_scale
        grad_key_block = contract_first(dscore, query_block) * score_scale
        grad_value_block = contract_first(probability.astype(bf16), grad_block)
        return ((running[0] + grad_key_block, running[1] + grad_value_block), grad_query_block)

    start_kv = (jnp.zeros((group_len, HEAD), f32), jnp.zeros((group_len, HEAD), f32))
    (grad_key_rot, grad_value), grad_query_rot = lax.scan(
        back_block, start_kv, (block_starts, grad_out_blocks, log_totals)
    )
    grad_query = rotate_back(grad_query_rot.reshape(group_len, HEAD), cosine_table, sine_table)
    grad_key = rotate_back(grad_key_rot, cosine_table, sine_table)
    grad_projected = jnp.concatenate(
        [
            grad_query.astype(bf16),
            grad_inner.astype(bf16),
            grad_gate.astype(bf16),
            grad_key.astype(bf16),
            grad_value.astype(bf16),
            grad_bc.astype(bf16),
            jnp.pad(grad_steps.astype(bf16), ((0, 0), (0, 128 - HEADS_DEV))),
        ],
        axis=1,
    )
    grad_left_part, grad_a_in, grad_b_in = backward(
        left_in, lower_in, grad_projected, in_weight, in_raise, mask_all
    )
    (grad_hidden_norm,) = norm_back(scatter_seq(grad_left_part))
    grad_tokens = (grad_residual + grad_hidden_norm).astype(bf16)

    def lanes(matrix):
        return matrix.astype(bf16).reshape(DP, -1, 128)

    early = jnp.concatenate(
        [
            lanes(grad_a_out),
            lanes(grad_b_out),
            lanes(grad_a_gu),
            lanes(grad_b_gu),
            lanes(grad_a_down),
            lanes(grad_b_down),
        ],
        axis=1,
    )
    early = lax.psum_scatter(
        early.reshape(-1, 128), "dp", scatter_dimension=0, tiled=True
    )
    a_out_block = early[:64]
    b_out_own = early[64:192]
    a_gu_own = early[192:320]
    b_gu_own = early[320:448]
    a_down_own = early[448:512]
    b_down_own = early[512:640]
    zero_rows = jnp.zeros((256, 128), bf16)
    a_out_own = lax.dynamic_update_slice_in_dim(
        zero_rows, jnp.where(own_rows, a_out_block, jnp.zeros_like(a_out_block)), 64 * y, 0
    )
    for k in range(1, Y_RING):
        pairs = [(((i // 2 + k) % Y_RING) * SEQ + i, (i // 2) * SEQ + i) for i in range(SEQ)]
        moved = lax.ppermute(a_out_block, ("dp", "sp"), pairs)
        a_out_own = a_out_own + lax.dynamic_update_slice_in_dim(
            zero_rows, moved, 64 * ((y + k) % Y_RING), 0
        )
    a_down_own = lax.dynamic_update_slice_in_dim(zero_rows, a_down_own, 64 * y, 0)
    b_gu_full = lax.dynamic_update_slice_in_dim(
        jnp.zeros((8, 2, DP, Y_RING, 64), bf16), b_gu_own.reshape(8, 2, DP, 1, 64), y, 3
    ).reshape(512, 128)
    early_full = lax.psum(
        jnp.concatenate([a_out_own, b_out_own, a_gu_own, b_gu_full, a_down_own, b_down_own], axis=0),
        "sp",
    ).astype(f32)
    out_a_out = early_full[:256]
    out_b_out = early_full[256:384].reshape(8, -1)
    out_a_gu = early_full[384:512]
    out_b_gu = early_full[512:1024].reshape(8, -1)
    out_a_down = early_full[1024:1280]
    out_b_down = early_full[1280:].reshape(8, -1)

    late = jnp.concatenate([lanes(grad_a_in), lanes(grad_b_in)], axis=1)
    late = jnp.sum(
        lax.all_to_all(late, "dp", split_axis=0, concat_axis=0).astype(f32), axis=0
    )
    a_in_own = late[:128]
    b_in_own = late[128:].reshape(8, IN_COLS)

    def spread_heads(part, width):
        return lax.dynamic_update_slice(
            jnp.zeros((8, 12, Y_RING, width), f32),
            part.reshape(8, HEADS_DEV, 1, width),
            (0, HEADS_DEV * x, y, 0),
        ).reshape(8, -1)

    kv_width = H_KV * HEAD
    b_in_full = jnp.concatenate(
        [
            lax.dynamic_update_slice_in_dim(
                jnp.zeros((8, EDGE_INNER), f32), b_in_own[:, COL_Q:COL_INNER], s * HEAD, 1
            ),
            spread_heads(b_in_own[:, COL_INNER:COL_GATE], M_HEAD),
            lax.dynamic_update_slice_in_dim(
                jnp.zeros((8, kv_width), f32), b_in_own[:, COL_K:COL_V], kv_head * HEAD, 1
            ),
            lax.dynamic_update_slice_in_dim(
                jnp.zeros((8, kv_width), f32), b_in_own[:, COL_V:COL_BC], kv_head * HEAD, 1
            ),
            b_in_own[:, COL_BC:COL_STEP],
            spread_heads(b_in_own[:, COL_GATE:COL_K], M_HEAD),
            spread_heads(b_in_own[:, COL_STEP : COL_STEP + HEADS_DEV], 1),
            jnp.zeros((8, 80), f32),
        ],
        axis=1,
    )
    late_full = jnp.concatenate([a_in_own, b_in_full.reshape(-1, 128)], axis=0)
    pad = (-late_full.shape[0]) % 128
    late_full = jnp.pad(late_full, ((0, pad), (0, 0)))
    late_full = gather_seq(scatter_seq(late_full).astype(bf16)).astype(f32)
    out_a_in = late_full[:128]
    out_b_in = late_full[128 : 128 + 520].reshape(8, -1)[:, : EDGE_STEP + M_HEADS]
    return (
        layer_out,
        grad_tokens,
        out_a_in,
        out_b_in,
        out_a_out,
        out_b_out,
        out_a_gu,
        out_b_gu,
        out_a_down,
        out_b_down,
    )


def solution(mesh):
    rows = P("dp", None)
    both = P(("dp", "sp"), None)
    in_specs = (both, both) + (rows,) * 2 + (P(),) * 8 + (rows,) * 12
    out_specs = (both, both) + (rows,) * 8
    return jax.shard_map(
        per_device, mesh=mesh, in_specs=in_specs, out_specs=out_specs, check_vma=False
    )
```

```python
from functools import partial

import jax
import jax.numpy as jnp
from jax import lax
from jax.experimental import pallas as pl
from jax.experimental.pallas import tpu as pltpu
from jax.sharding import PartitionSpec as P

H_Q = 8
H_KV = 2
HEAD = 128
M_HEADS = 48
M_HEAD = 64
CONV = 4
ADAPTER_RANK = 16
ADAPTER_SETS = 8
SPAN = 128
STATE = 256
D_SSM = 3072
SHARED = 1024
ADAPTERS = ADAPTER_RANK * ADAPTER_SETS

Y_RING = 4
X_PAIR = 2
SEQ = 8
DP = 16
HEADS_DEV = 6
INNER = HEADS_DEV * M_HEAD
SLICE = HEAD + INNER
MIX = X_PAIR * SLICE
UNITS = 1024

COL_Q = 0
COL_INNER = COL_Q + HEAD
COL_GATE = COL_INNER + INNER
COL_K = COL_GATE + INNER
COL_V = COL_K + HEAD
COL_BC = COL_V + HEAD
COL_STEP = COL_BC + 2 * STATE
IN_COLS = COL_STEP + 128

EDGE_INNER = H_Q * HEAD
EDGE_SHARED = EDGE_INNER + D_SSM
EDGE_GATE = EDGE_SHARED + SHARED
EDGE_STEP = EDGE_GATE + D_SSM

CONVOLVED = INNER + 2 * STATE

epsilon = 1e-05
rope_base = 100000000000.0
masked_score = -1e30
highest = lax.Precision.HIGHEST
bf16 = jnp.bfloat16
f32 = jnp.float32


def rms_scale(vectors, scale_gain):
    return (
        vectors
        * lax.rsqrt(jnp.mean(vectors * vectors, axis=-1, keepdims=True) + epsilon)
        * scale_gain
    )


def silu_value(vectors):
    return vectors * jax.nn.sigmoid(vectors)


def swiglu(gate_and_up):
    half_width = gate_and_up.shape[1] // 2
    return silu_value(gate_and_up[:, :half_width]) * gate_and_up[:, half_width:]


def rotary_tables(position):
    lanes = jnp.arange(HEAD)
    half_width = HEAD // 2
    frequency = rope_base ** (-((lanes % half_width).astype(f32) * 2.0 / HEAD))
    angle = position.astype(f32)[:, None] * frequency[None, :]
    return jnp.cos(angle), jnp.where(lanes < half_width, -1.0, 1.0) * jnp.sin(angle)


def product(left, right):
    return jnp.dot(left, right, preferred_element_type=f32)


def contract_last(left, right):
    return lax.dot_general(left, right, (((1,), (1,)), ((), ())), preferred_element_type=f32)


def contract_first(left, right):
    return lax.dot_general(left, right, (((0,), (0,)), ((), ())), preferred_element_type=f32)


def hop(value, target):
    return lax.ppermute(value, "sp", [(i, target(i)) for i in range(SEQ)])


def up(i):
    return (i + X_PAIR) % SEQ


def down(i):
    return (i - X_PAIR) % SEQ


def side(i):
    return i ^ 1


def gather_ring(block):
    half = block.shape[0] // 2
    below = hop(block, up)
    above = hop(block, down)
    far_first = hop(below[:half], up)
    far_second = hop(above[half:], down)
    return jnp.concatenate([block, above, far_first, far_second, below], axis=0)


def scatter_ring(partial_rows):
    n = partial_rows.shape[0] // Y_RING
    half = n // 2
    far = partial_rows[2 * n : 3 * n].astype(bf16)
    from_below = hop(far[:half], up).astype(f32)
    from_above = hop(far[half:], down).astype(f32)
    to_up = partial_rows[n : 2 * n]
    to_up = jnp.concatenate([to_up[:half] + from_below, to_up[half:]], axis=0).astype(bf16)
    to_down = partial_rows[3 * n :]
    to_down = jnp.concatenate([to_down[:half], to_down[half:] + from_above], axis=0).astype(bf16)
    low = hop(to_up, up).astype(f32)
    high = hop(to_down, down).astype(f32)
    return partial_rows[:n] + low + high


def gather_seq(block):
    copies = jnp.broadcast_to(block[None], (SEQ,) + block.shape)
    return lax.all_to_all(copies, "sp", split_axis=0, concat_axis=0).reshape(
        (SEQ * block.shape[0],) + block.shape[1:]
    )


def scatter_seq(partial_rows):
    n = partial_rows.shape[0] // SEQ
    pieces = partial_rows.astype(bf16).reshape((SEQ, n) + partial_rows.shape[1:])
    return jnp.sum(
        lax.all_to_all(pieces, "sp", split_axis=0, concat_axis=0).astype(f32), axis=0
    )


def sum_seq_small(value):
    total = value
    for offset in range(1, SEQ):
        total = total + hop(value, lambda i, offset=offset: (i + offset) % SEQ)
    return total


def blocks_of(matrix):
    n = matrix.shape[1] // 128
    return matrix.reshape(DP, 8, n, 128).transpose(0, 2, 1, 3).reshape(DP, 8 * n, 128)


def row_from_blocks(stacked):
    n = stacked.shape[0] // 8
    return stacked.reshape(n, 8, 128).transpose(1, 0, 2).reshape(8, 128 * n)


def sixteen_rows(rows):
    return jnp.pad(rows, ((0, 16 - rows.shape[0]), (0, 0)))


def pick_columns(block, y):
    rows = lax.broadcasted_iota(jnp.int32, (512, 128), 0)
    lanes = lax.broadcasted_iota(jnp.int32, (512, 128), 1)
    wanted = jnp.where(lanes < M_HEAD, lanes, lanes + 256 - M_HEAD) + M_HEAD * y
    return product(block, (rows == wanted).astype(bf16))


def pack_input_kernel(place_ref, weight_ref, lower_ref, upper_ref, out_ref):
    s = place_ref[0]
    y = s // X_PAIR
    x = s % X_PAIR
    kv_head = s // (H_Q // H_KV)

    def at(column):
        return pl.ds(pl.multiple_of(column, 128), 128)

    def share(ref):
        def heads(edge):
            return [
                pick_columns(
                    ref[:, pl.ds(pl.multiple_of(edge + 256 * (HEADS_DEV * x + 2 * pair), 128), 512)], y
                )
                for pair in range(HEADS_DEV // 2)
            ]

        step_rows = lax.broadcasted_iota(jnp.int32, (M_HEADS, 128), 0)
        step_lanes = lax.broadcasted_iota(jnp.int32, (M_HEADS, 128), 1)
        picked = (step_rows == Y_RING * (HEADS_DEV * x + step_lanes) + y) & (step_lanes < HEADS_DEV)
        return (
            [ref[:, at(HEAD * s)].astype(f32)]
            + heads(EDGE_INNER)
            + heads(EDGE_GATE)
            + [
                ref[:, at(EDGE_SHARED + HEAD * kv_head)].astype(f32),
                ref[:, at(EDGE_SHARED + HEAD * (H_KV + kv_head))].astype(f32),
            ]
            + [
                ref[:, EDGE_SHARED + 2 * H_KV * HEAD + 128 * i : EDGE_SHARED + 2 * H_KV * HEAD + 128 * i + 128].astype(f32)
                for i in range(2 * STATE // 128)
            ]
            + [product(ref[:, EDGE_STEP:], picked.astype(bf16))]
        )

    for i, piece in enumerate(share(weight_ref)):
        out_ref[:, 128 * i : 128 * i + 128] = piece.astype(bf16)
    out_ref[:, IN_COLS : IN_COLS + ADAPTERS] = lower_ref[...]
    upper = [piece[:8] for piece in share(upper_ref)]
    upper.append(jnp.zeros((128 - 8 * len(upper), 128), f32))
    out_ref[:, IN_COLS + ADAPTERS :] = jnp.concatenate(upper, axis=0).astype(bf16)


def pack_ffn_kernel(
    place_ref, gu_ref, gu_lower_ref, gu_upper_ref, down_ref, down_lower_ref, down_upper_ref, out_ref
):
    y = place_ref[0] // X_PAIR
    pairs = 2 * UNITS // 128
    for i in range(pairs):
        out_ref[:, 128 * i : 128 * i + 128] = pick_columns(
            gu_ref[:, 512 * i : 512 * i + 512], y
        ).astype(bf16)
    edge = 2 * UNITS
    out_ref[:, edge : edge + 128] = gu_lower_ref[...]
    edge += 128
    out_ref[:, edge : edge + 128] = jnp.concatenate(
        [pick_columns(gu_upper_ref[:, 512 * i : 512 * i + 512], y)[:8] for i in range(pairs)], axis=0
    ).astype(bf16)
    edge += 128
    model = down_ref.shape[1]
    rows = pl.ds(pl.multiple_of(64 * y, 64), 64)
    out_ref[:64, edge : edge + model // 2] = down_ref[rows, : model // 2]
    out_ref[64:, edge : edge + model // 2] = down_ref[rows, model // 2 :]
    edge += model // 2
    out_ref[:, edge : edge + 128] = jnp.concatenate(
        [down_upper_ref[:, 128 * i : 128 * i + 128].astype(f32)[:8] for i in range(model // 128)], axis=0
    ).astype(bf16)
    edge += 128
    out_ref[:64, edge:] = down_lower_ref[rows, :]
    out_ref[64:, edge:] = jnp.zeros((64, 128), bf16)


def pack_output_kernel(rows_ref, upper_ref, out_ref):
    width = rows_ref.shape[1]
    out_ref[:, :width] = rows_ref[...]
    for c in range(2):
        out_ref[:, width + 128 * c : width + 128 * c + 128] = jnp.concatenate(
            [
                upper_ref[:, 1024 * c + 128 * i : 1024 * c + 128 * i + 128].astype(f32)[:8]
                for i in range(8)
            ],
            axis=0,
        ).astype(bf16)


def raising_kernel(*refs):
    out_ref = refs[-1]
    column = 0
    for ref in refs[:-1]:
        stacked = ref[...].astype(f32)
        depth = stacked.shape[0] // DP
        for block in range(min(depth // 8, out_ref.shape[1] // 128)):
            out_ref[:, column : column + 128] = jnp.concatenate(
                [
                    stacked[depth * shard + 8 * block : depth * shard + 8 * block + 8]
                    for shard in range(DP)
                ],
                axis=0,
            ).astype(bf16)
            column += 128


def raising(gathered, columns, width):
    depth = gathered.shape[0]
    return pl.pallas_call(
        raising_kernel,
        grid=(1,),
        in_specs=[
            pl.BlockSpec((depth, 128), lambda i, c=column: (0, c // 128)) for column in columns
        ],
        out_specs=pl.BlockSpec((ADAPTERS, width), lambda i: (0, 0)),
        out_shape=jax.ShapeDtypeStruct((ADAPTERS, width), bf16),
        compiler_params=pltpu.CompilerParams(vmem_limit_bytes=32 * 1024 * 1024),
    )(*[gathered] * len(columns))


def pack(kernel, arrays, shape):
    return pl.pallas_call(
        kernel,
        in_specs=[
            pl.BlockSpec(memory_space=pltpu.SMEM if a.ndim == 1 else pltpu.VMEM) for a in arrays
        ],
        out_specs=pl.BlockSpec(memory_space=pltpu.VMEM),
        out_shape=jax.ShapeDtypeStruct(shape, bf16),
        compiler_params=pltpu.CompilerParams(vmem_limit_bytes=32 * 1024 * 1024),
    )(*arrays)


def lane_index(shape):
    return lax.broadcasted_iota(jnp.int32, shape, 1)


def row_index(shape):
    return lax.broadcasted_iota(jnp.int32, shape, 0)


def over_heads(per_head):
    rows = per_head.shape[0]
    low = lane_index((rows, 128)) < M_HEAD
    return jnp.concatenate(
        [
            jnp.where(low, per_head[:, 2 * pair : 2 * pair + 1], per_head[:, 2 * pair + 1 : 2 * pair + 2])
            for pair in range(HEADS_DEV // 2)
        ],
        axis=1,
    )


def head_sums(values):
    member = (row_index((INNER, 128)) // M_HEAD == lane_index((INNER, 128))).astype(bf16)
    coarse = values.astype(bf16)
    fine = (values - coarse.astype(f32)).astype(bf16)
    return product(coarse, member) + product(fine, member)


def span_terms(convolved, step_block, rate_rows, first_len, start):
    shifted = step_block + rate_rows[0:1]
    rates = jnp.log1p(jnp.exp(-jnp.abs(shifted))) + jnp.maximum(shifted, 0.0)
    log_decay = rates * rate_rows[1:2]
    rows = row_index((SPAN, SPAN))
    lanes = lane_index((SPAN, SPAN))
    below = rows >= lanes
    cumulative = jnp.dot(
        below.astype(f32), log_decay, precision=highest, preferred_element_type=f32
    )
    seg_rows = (rows + start >= first_len).astype(jnp.int32)
    seg_lanes = (lanes + start >= first_len).astype(jnp.int32)
    allowed = below & (seg_rows == seg_lanes)
    last_seg = (start + SPAN - 1 >= first_len).astype(jnp.int32)
    previous = (start - 1 >= first_len).astype(jnp.int32)
    total = cumulative[SPAN - 1 : SPAN]
    entry = jnp.where(seg_rows == previous, jnp.exp(cumulative), 0.0)
    tail = jnp.where(seg_rows == last_seg, jnp.exp(total - cumulative), 0.0)
    keep = jnp.where(last_seg == previous, jnp.exp(total), 0.0)
    activated = convolved * jax.nn.sigmoid(convolved)
    x_in = activated[:, :INNER]
    in_state = activated[:, INNER : INNER + STATE]
    out_state = activated[:, INNER + STATE :]
    return shifted, rates, cumulative, allowed, entry, tail, keep, x_in, in_state, out_state


def decay_of(cumulative, across, allowed, head):
    gap = cumulative[:, head : head + 1] - across[head : head + 1]
    return jnp.exp(jnp.where(allowed, gap, masked_score))


def scan_forward_kernel(
    lengths_ref,
    proj_ref,
    taps_ref,
    rate_rows_ref,
    skip_ref,
    gated_ref,
    scanned_ref,
    squares_ref,
    convolved_ref,
    states_ref,
    state,
    last_rows,
):
    step = pl.program_id(0)
    start = step * SPAN
    first_len = lengths_ref[0, 0]

    @pl.when(step == 0)
    def _():
        state[...] = jnp.zeros_like(state)
        last_rows[...] = jnp.zeros_like(last_rows)

    signal = jnp.concatenate(
        [proj_ref[:, COL_INNER:COL_GATE], proj_ref[:, COL_BC:COL_STEP]], axis=1
    ).astype(f32)
    row = start + row_index((SPAN, 1))
    position = row - jnp.where(row >= first_len, first_len, 0)
    convolved = taps_ref[4:5] + taps_ref[3:4] * signal
    before = last_rows[...]
    top = row_index((8, 1))
    for offset in range(1, CONV):
        moved = pltpu.roll(signal, offset, 0)
        edge = jnp.where(top < offset, pltpu.roll(before, offset, 0), moved[:8])
        moved = jnp.concatenate([edge, moved[8:]], axis=0)
        convolved = convolved + taps_ref[3 - offset : 4 - offset] * jnp.where(
            position >= offset, moved, 0.0
        )
    last_rows[...] = signal[SPAN - 8 :]
    convolved_ref[...] = convolved
    step_block = proj_ref[:, COL_STEP:].astype(f32)
    _, rates, cumulative, allowed, entry, tail, keep, x_in, in_state, out_state = span_terms(
        convolved, step_block, rate_rows_ref[...], first_len, start
    )
    across = cumulative.T
    in_half = in_state.astype(bf16)
    out_half = out_state.astype(bf16)
    state_now = state[...]
    state_half = state_now.astype(bf16)
    states_ref[0] = state_half
    mixing = contract_last(out_half, in_half)
    rates_wide = over_heads(rates)
    weighted = (x_in * rates_wide).astype(bf16)
    low = lane_index((SPAN, 128)) < M_HEAD
    within = []
    for pair in range(HEADS_DEV // 2):
        block = weighted[:, 128 * pair : 128 * pair + 128]
        sides = [
            product(
                (mixing * decay_of(cumulative, across, allowed, 2 * pair + i)).astype(bf16), block
            )
            for i in range(2)
        ]
        within.append(jnp.where(low, sides[0], sides[1]))
    result = (
        jnp.concatenate(within, axis=1)
        + product(out_half, state_half) * over_heads(entry)
        + skip_ref[0:1] * x_in
    )
    scanned = result.astype(bf16)
    scanned_ref[...] = scanned
    gate = proj_ref[:, COL_GATE:COL_K].astype(f32)
    gated = scanned.astype(f32) * (gate * jax.nn.sigmoid(gate))
    gated_ref[...] = gated.astype(bf16)
    squares_ref[...] = lax.dot_general(
        jnp.ones((8, INNER), f32),
        gated * gated,
        (((1,), (1,)), ((), ())),
        precision=highest,
        preferred_element_type=f32,
    )
    state[...] = state_now * over_heads(keep) + contract_first(
        in_half, (x_in * over_heads(tail * rates)).astype(bf16)
    )


def scan_backward_kernel(
    lengths_ref,
    proj_ref,
    convolved_ref,
    scanned_ref,
    states_ref,
    upstream_ref,
    scales_ref,
    grad_query_ref,
    grad_key_ref,
    grad_value_ref,
    taps_ref,
    rate_rows_ref,
    skip_ref,
    out_ref,
    grad_state,
    next_rows,
):
    step = pl.num_programs(0) - 1 - pl.program_id(0)
    start = step * SPAN
    first_len = lengths_ref[0, 0]

    @pl.when(pl.program_id(0) == 0)
    def _():
        grad_state[...] = jnp.zeros_like(grad_state)
        next_rows[...] = jnp.zeros_like(next_rows)

    convolved = convolved_ref[...]
    step_block = proj_ref[:, COL_STEP:].astype(f32)
    rate_rows = rate_rows_ref[...]
    shifted, rates, cumulative, allowed, entry, tail, keep, x_in, in_state, out_state = span_terms(
        convolved, step_block, rate_rows, first_len, start
    )
    across = cumulative.T
    in_half = in_state.astype(bf16)
    out_half = out_state.astype(bf16)
    state_half = states_ref[0]

    gate = proj_ref[:, COL_GATE:COL_K].astype(f32)
    gate_sigmoid = jax.nn.sigmoid(gate)
    gate_silu = gate * gate_sigmoid
    scanned = scanned_ref[...].astype(f32)
    upstream = upstream_ref[...].astype(f32) * skip_ref[1:2]
    grad_gated = scales_ref[:, 0:1] * upstream - scales_ref[:, 1:2] * (scanned * gate_silu)
    out_ref[:, COL_GATE:COL_K] = (
        grad_gated * scanned * (gate_sigmoid * (1.0 + gate * (1.0 - gate_sigmoid)))
    ).astype(bf16)
    grad_half = (grad_gated * gate_silu).astype(bf16)
    grad_result = grad_half.astype(f32)

    mixing = contract_last(out_half, in_half)
    rates_wide = over_heads(rates)
    entry_wide = over_heads(entry)
    tail_wide = over_heads(tail)
    keep_wide = over_heads(keep)
    weighted = (x_in * rates_wide).astype(bf16)
    lane = lane_index((SPAN, 128))
    low = lane < M_HEAD
    grad_mixing = jnp.zeros((SPAN, SPAN), f32)
    grad_cumulative = jnp.zeros((SPAN, 128), f32)
    grad_across = jnp.zeros((SPAN, 128), f32)
    head_row = row_index((SPAN, 128))
    grad_weighted = []
    for pair in range(HEADS_DEV // 2):
        block = weighted[:, 128 * pair : 128 * pair + 128]
        grad_block = grad_half[:, 128 * pair : 128 * pair + 128]
        sides = []
        for i in range(2):
            head = 2 * pair + i
            decay = decay_of(cumulative, across, allowed, head)
            spread = mixing * decay
            sides.append(contract_first(spread.astype(bf16), grad_block))
            mine = low if i == 0 else jnp.logical_not(low)
            grad_spread = contract_last(jnp.where(mine, grad_block, jnp.zeros_like(grad_block)), block)
            grad_mixing = grad_mixing + grad_spread * decay
            grad_gap = grad_spread * spread
            grad_cumulative = jnp.where(
                lane == head, jnp.sum(grad_gap, axis=1, keepdims=True), grad_cumulative
            )
            grad_across = jnp.where(
                head_row == head, jnp.sum(grad_gap, axis=0, keepdims=True), grad_across
            )
        grad_weighted.append(jnp.where(low, sides[0], sides[1]))
    grad_weighted = jnp.concatenate(grad_weighted, axis=1)
    grad_cumulative = grad_cumulative - grad_across.T

    grad_next = grad_state[...]
    grad_next_half = grad_next.astype(bf16)
    grad_entered = (grad_result * entry_wide).astype(bf16)
    from_state = product(out_half, state_half)
    to_state = product(in_half, grad_next_half)
    tail_rates = tail_wide * rates_wide
    grad_mixing_half = grad_mixing.astype(bf16)
    grad_out_state = product(grad_mixing_half, in_half) + contract_last(grad_entered, state_half)
    grad_in_state = contract_first(grad_mixing_half, out_half) + contract_last(
        (x_in * tail_rates).astype(bf16), grad_next_half
    )
    sums = head_sums(
        jnp.concatenate(
            [
                grad_result * from_state,
                to_state * x_in,
                grad_weighted * x_in,
                jnp.broadcast_to(
                    jnp.sum(grad_next * state_half.astype(f32), axis=0, keepdims=True), (8, INNER)
                ),
            ],
            axis=0,
        )
    )
    grad_entry = sums[:SPAN]
    grad_tail = sums[SPAN : 2 * SPAN]
    grad_rates = sums[2 * SPAN : 3 * SPAN] + grad_tail * tail
    from_tail = grad_tail * tail * rates
    grad_total = (
        jnp.sum(from_tail, axis=0, keepdims=True) + sums[3 * SPAN : 3 * SPAN + 1] * keep
    )
    grad_cumulative = grad_cumulative + grad_entry * entry - from_tail
    grad_cumulative = grad_cumulative + jnp.where(head_row == SPAN - 1, grad_total, 0.0)
    above = (row_index((SPAN, SPAN)) <= lane_index((SPAN, SPAN))).astype(f32)
    grad_decay = jnp.dot(above, grad_cumulative, precision=highest, preferred_element_type=f32)
    grad_rates = grad_rates + grad_decay * rate_rows[1:2]
    out_ref[:, COL_STEP:] = jnp.where(
        lane < HEADS_DEV, grad_rates * jax.nn.sigmoid(shifted), 0.0
    ).astype(bf16)
    grad_x = grad_weighted * rates_wide + to_state * tail_rates + skip_ref[0:1] * grad_result
    grad_state[...] = grad_next * keep_wide + contract_first(out_half, grad_entered)

    conv_sigmoid = jax.nn.sigmoid(convolved)
    grad_conv = jnp.concatenate([grad_x, grad_in_state, grad_out_state], axis=1) * (
        conv_sigmoid * (1.0 + convolved * (1.0 - conv_sigmoid))
    )
    row = start + row_index((SPAN, 1))
    position = row - jnp.where(row >= first_len, first_len, 0)
    later_row = start + SPAN + row_index((8, 1))
    later_position = later_row - jnp.where(later_row >= first_len, first_len, 0)
    later = next_rows[...]
    bottom = row_index((8, 1))
    grad_signal = taps_ref[3:4] * grad_conv
    for offset in range(1, CONV):
        moved = pltpu.roll(jnp.where(position >= offset, grad_conv, 0.0), SPAN - offset, 0)
        edge = pltpu.roll(jnp.where(later_position >= offset, later, 0.0), 8 - offset, 0)
        edge = jnp.where(bottom >= 8 - offset, edge, moved[SPAN - 8 :])
        moved = jnp.concatenate([moved[: SPAN - 8], edge], axis=0)
        grad_signal = grad_signal + taps_ref[3 - offset : 4 - offset] * moved
    next_rows[...] = grad_conv[:8]
    out_ref[:, COL_INNER:COL_GATE] = grad_signal[:, :INNER].astype(bf16)
    out_ref[:, COL_BC:COL_STEP] = grad_signal[:, INNER:].astype(bf16)
    out_ref[:, :COL_INNER] = grad_query_ref[...]
    out_ref[:, COL_K:COL_V] = grad_key_ref[...]
    out_ref[:, COL_V:COL_BC] = grad_value_ref[...]


def whole(shape):
    return pl.BlockSpec(shape, lambda i: (0,) * len(shape))


smem = pl.BlockSpec(memory_space=pltpu.SMEM)


def scan_forward(lengths, proj, taps, rate_rows, skip_rows):
    length_all = proj.shape[0]
    spans = length_all // SPAN

    def rows(width):
        return pl.BlockSpec((SPAN, width), lambda i: (i, 0))

    return pl.pallas_call(
        scan_forward_kernel,
        grid=(spans,),
        in_specs=[smem, rows(IN_COLS), whole(taps.shape), whole(rate_rows.shape), whole(skip_rows.shape)],
        out_specs=[
            rows(INNER),
            rows(INNER),
            pl.BlockSpec((8, SPAN), lambda i: (i, 0)),
            rows(CONVOLVED),
            pl.BlockSpec((1, STATE, INNER), lambda i: (i, 0, 0)),
        ],
        out_shape=[
            jax.ShapeDtypeStruct((length_all, INNER), bf16),
            jax.ShapeDtypeStruct((length_all, INNER), bf16),
            jax.ShapeDtypeStruct((8 * spans, SPAN), f32),
            jax.ShapeDtypeStruct((length_all, CONVOLVED), f32),
            jax.ShapeDtypeStruct((spans, STATE, INNER), bf16),
        ],
        scratch_shapes=[pltpu.VMEM((STATE, INNER), f32), pltpu.VMEM((8, CONVOLVED), f32)],
        compiler_params=pltpu.CompilerParams(vmem_limit_bytes=32 * 1024 * 1024),
        name="scan_forward",
    )(lengths, proj, taps, rate_rows, skip_rows)


def scan_backward(
    lengths, proj, convolved, scanned, states, upstream, scales, grad_qkv, taps, rate_rows, skip_rows
):
    length_all = proj.shape[0]
    spans = length_all // SPAN

    def rows(width):
        return pl.BlockSpec((SPAN, width), lambda i: (spans - 1 - i, 0))

    return pl.pallas_call(
        scan_backward_kernel,
        grid=(spans,),
        in_specs=[
            smem,
            rows(IN_COLS),
            rows(CONVOLVED),
            rows(INNER),
            pl.BlockSpec((1, STATE, INNER), lambda i: (spans - 1 - i, 0, 0)),
            rows(INNER),
            rows(2),
            rows(HEAD),
            rows(HEAD),
            rows(HEAD),
            whole(taps.shape),
            whole(rate_rows.shape),
            whole(skip_rows.shape),
        ],
        out_specs=rows(IN_COLS),
        out_shape=jax.ShapeDtypeStruct((length_all, IN_COLS), bf16),
        scratch_shapes=[pltpu.VMEM((STATE, INNER), f32), pltpu.VMEM((8, CONVOLVED), f32)],
        compiler_params=pltpu.CompilerParams(vmem_limit_bytes=32 * 1024 * 1024),
        name="scan_backward",
    )(lengths, proj, convolved, scanned, states, upstream, scales, *grad_qkv, taps, rate_rows, skip_rows)


QUERY_ROWS = 256
score_scale = HEAD ** (-0.5)


def turn(values, cosine, sine):
    return values * cosine + pltpu.roll(values, HEAD // 2, 1) * sine


def allowed_scores(query_rot, key_rot, first_row, first_len):
    scores = contract_last(query_rot, key_rot) * score_scale
    rows = first_row + row_index(scores.shape)
    lanes = lane_index(scores.shape)
    allowed = (lanes <= rows) & ((lanes >= first_len) | (rows < first_len))
    return jnp.where(allowed, scores, masked_score)


def attention_forward_kernel(
    lengths_ref, query_ref, key_ref, value_ref, cosine_ref, sine_ref, out_ref, totals_ref
):
    first_len = lengths_ref[0, 0]
    length_all = query_ref.shape[0]
    key_rot = turn(key_ref[...].astype(f32), cosine_ref[...], sine_ref[...]).astype(bf16)
    for first in range(0, length_all, QUERY_ROWS):
        block = slice(first, first + QUERY_ROWS)
        seen = first + QUERY_ROWS
        query_rot = turn(
            query_ref[block].astype(f32), cosine_ref[block], sine_ref[block]
        ).astype(bf16)
        scores = allowed_scores(query_rot, key_rot[:seen], first, first_len)
        peak = jnp.max(scores, axis=1, keepdims=True)
        exponent = jnp.exp(scores - peak)
        total = jnp.sum(exponent, axis=1, keepdims=True)
        probs = (exponent * (1.0 / total)).astype(bf16)
        out_ref[block] = product(probs, value_ref[:seen]).astype(bf16)
        totals_ref[block] = peak + jnp.log(total)


def attention_backward_kernel(
    lengths_ref,
    query_ref,
    key_ref,
    value_ref,
    cosine_ref,
    sine_ref,
    upstream_ref,
    totals_ref,
    grad_query_ref,
    grad_key_ref,
    grad_value_ref,
    key_sum,
    value_sum,
):
    first_len = lengths_ref[0, 0]
    length_all = query_ref.shape[0]
    key_rot = turn(key_ref[...].astype(f32), cosine_ref[...], sine_ref[...]).astype(bf16)
    key_sum[...] = jnp.zeros_like(key_sum)
    value_sum[...] = jnp.zeros_like(value_sum)
    for first in range(0, length_all, QUERY_ROWS):
        block = slice(first, first + QUERY_ROWS)
        seen = first + QUERY_ROWS
        cosine = cosine_ref[block]
        sine = sine_ref[block]
        query_rot = turn(query_ref[block].astype(f32), cosine, sine).astype(bf16)
        probs = jnp.exp(
            allowed_scores(query_rot, key_rot[:seen], first, first_len) - totals_ref[block]
        )
        upstream = upstream_ref[block]
        grad_probs = contract_last(upstream, value_ref[:seen])
        delta = jnp.sum(probs * grad_probs, axis=1, keepdims=True)
        grad_scores = (probs * (grad_probs - delta)).astype(bf16)
        grad_query_ref[block] = turn(
            product(grad_scores, key_rot[:seen]) * score_scale, cosine, -sine
        ).astype(bf16)
        key_sum[:seen] += contract_first(grad_scores, query_rot)
        value_sum[:seen] += contract_first(probs.astype(bf16), upstream)
    grad_key_ref[...] = turn(
        key_sum[...] * score_scale, cosine_ref[...], -sine_ref[...]
    ).astype(bf16)
    grad_value_ref[...] = value_sum[...].astype(bf16)


def head_block(length_all, column):
    return pl.BlockSpec((length_all, HEAD), lambda i: (0, column // HEAD))


def attention_forward(lengths, proj, cosine, sine):
    length_all = proj.shape[0]
    block = head_block(length_all, 0)
    return pl.pallas_call(
        attention_forward_kernel,
        grid=(1,),
        in_specs=[
            smem,
            block,
            head_block(length_all, COL_K),
            head_block(length_all, COL_V),
            block,
            block,
        ],
        out_specs=[block, pl.BlockSpec((length_all, 1), lambda i: (0, 0))],
        out_shape=[
            jax.ShapeDtypeStruct((length_all, HEAD), bf16),
            jax.ShapeDtypeStruct((length_all, 1), f32),
        ],
        compiler_params=pltpu.CompilerParams(vmem_limit_bytes=40 * 1024 * 1024),
        name="attention_forward",
    )(lengths, proj, proj, proj, cosine, sine)


def attention_backward(lengths, proj, cosine, sine, upstream, totals):
    length_all = proj.shape[0]
    block = head_block(length_all, 0)
    return pl.pallas_call(
        attention_backward_kernel,
        grid=(1,),
        in_specs=[
            smem,
            block,
            head_block(length_all, COL_K),
            head_block(length_all, COL_V),
            block,
            block,
            block,
            pl.BlockSpec((length_all, 1), lambda i: (0, 0)),
        ],
        out_specs=[block, block, block],
        out_shape=[jax.ShapeDtypeStruct((length_all, HEAD), bf16)] * 3,
        scratch_shapes=[pltpu.VMEM((length_all, HEAD), f32)] * 2,
        compiler_params=pltpu.CompilerParams(vmem_limit_bytes=40 * 1024 * 1024),
        name="attention_backward",
    )(lengths, proj, proj, proj, cosine, sine, upstream, totals)


def per_device(
    tokens,
    cotangent,
    seq_lengths,
    adapter_ids,
    norm_gain,
    ffn_gain,
    gate_gain,
    conv_weight,
    conv_bias,
    dt_bias,
    decay_log,
    skip_gain,
    frozen_input_weight,
    input_adapter_lower,
    input_adapter_upper,
    frozen_output_weight,
    output_adapter_lower,
    output_adapter_upper,
    frozen_gate_up_weight,
    gate_up_adapter_lower,
    gate_up_adapter_upper,
    frozen_down_weight,
    down_adapter_lower,
    down_adapter_upper,
):
    s = lax.axis_index("sp")
    d = lax.axis_index("dp")
    y = s // X_PAIR
    x = s % X_PAIR
    tok_count = tokens.shape[0]
    group_len = tok_count * SEQ
    first_len = seq_lengths[0, 0]
    set_ids = adapter_ids[0]

    def adapter_mask(token_index):
        resident = jnp.where(token_index >= first_len, set_ids[1], set_ids[0])
        return jnp.arange(ADAPTERS)[None, :] // ADAPTER_RANK == resident[:, None]

    group_index = jnp.arange(group_len)
    segment = (group_index >= first_len).astype(jnp.int32)
    position = group_index - first_len * segment
    mask_all = adapter_mask(group_index)
    ring_blocks = X_PAIR * ((y + jnp.arange(Y_RING)) % Y_RING) + x
    ring_index = (ring_blocks[:, None] * tok_count + jnp.arange(tok_count)[None, :]).reshape(-1)
    mask_ring = adapter_mask(ring_index)

    def head_columns(values):
        lead = values.shape[:-1]
        grouped = values.reshape(lead + (12, Y_RING, M_HEAD))
        grouped = lax.dynamic_slice_in_dim(grouped, HEADS_DEV * x, HEADS_DEV, len(lead))
        grouped = lax.dynamic_index_in_dim(grouped, y, len(lead) + 1, keepdims=False)
        return grouped.reshape(lead + (INNER,))

    def head_items(values):
        lead = values.shape[:-1]
        grouped = values.reshape(lead + (12, Y_RING))
        grouped = lax.dynamic_slice_in_dim(grouped, HEADS_DEV * x, HEADS_DEV, len(lead))
        return lax.dynamic_index_in_dim(grouped, y, len(lead) + 1, keepdims=False)

    kv_head = s // (H_Q // H_KV)

    def gather_rows(rows):
        return lax.all_gather(rows, "dp", axis=0, tiled=True)

    place = jnp.reshape(s, (1,)).astype(jnp.int32)
    in_all = gather_rows(
        pack(
            pack_input_kernel,
            (place, frozen_input_weight, input_adapter_lower, sixteen_rows(input_adapter_upper)),
            (128, IN_COLS + 2 * ADAPTERS),
        )
    )
    in_weight = in_all[:, : IN_COLS + ADAPTERS]
    in_raise = raising(in_all, (IN_COLS + ADAPTERS,), IN_COLS)

    out_rows = jnp.concatenate([frozen_output_weight, output_adapter_lower], axis=1)
    piece = lax.dynamic_slice_in_dim(out_rows, 64 * y, 64, 0)
    spread = jnp.zeros_like(piece)
    for k in range(1, Y_RING):
        block = lax.dynamic_slice_in_dim(out_rows, 64 * ((y + k) % Y_RING), 64, 0)
        pairs = [((i // 2) * SEQ + i, ((i // 2 + k) % Y_RING) * SEQ + i) for i in range(SEQ)]
        spread = spread + lax.ppermute(block, ("dp", "sp"), pairs)
    own_rows = (d >= Y_RING) | (d == y)
    model = frozen_output_weight.shape[1]
    out_all = gather_rows(
        pack(
            pack_output_kernel,
            (jnp.where(own_rows, piece, spread), sixteen_rows(output_adapter_upper)),
            (64, model + 3 * ADAPTERS),
        )
    )
    out_weight = out_all[:, : model + ADAPTERS]
    out_raise = raising(out_all, (model + ADAPTERS, model + 2 * ADAPTERS), model)

    ffn_all = gather_rows(
        pack(
            pack_ffn_kernel,
            (
                place,
                frozen_gate_up_weight,
                gate_up_adapter_lower,
                sixteen_rows(gate_up_adapter_upper),
                frozen_down_weight,
                down_adapter_lower,
                sixteen_rows(down_adapter_upper),
            ),
            (128, 2 * UNITS + model // 2 + 4 * ADAPTERS),
        )
    )
    edge = 2 * UNITS + ADAPTERS
    gu_weight = ffn_all[:, :edge]
    gu_raise = raising(ffn_all, (edge,), 2 * UNITS)
    edge += 128
    folded = ffn_all[:, edge : edge + model // 2].reshape(DP, 2, 64, model // 2)
    edge += model // 2
    down_raise = raising(ffn_all, (edge,), model)
    edge += 128
    lowers = ffn_all[:, edge:].reshape(DP, 2, 64, ADAPTERS)
    down_weight = jnp.concatenate(
        [
            folded[:, 0].reshape(UNITS, -1),
            folded[:, 1].reshape(UNITS, -1),
            lowers[:, 0].reshape(UNITS, -1),
        ],
        axis=1,
    )

    def masked(lowered, mask):
        return jnp.where(mask, lowered, 0.0).astype(bf16)

    def forward(left, weight, raising, mask):
        both = product(left, weight)
        width = raising.shape[1]
        lowered = masked(both[:, width:], mask)
        return both[:, :width] + product(lowered, raising), lowered

    def backward(left, lowered, upstream, weight, raising, mask):
        gradient_lowered = masked(contract_last(upstream, raising), mask)
        grad_raise = contract_first(lowered, upstream)
        grad_lower = contract_first(left, gradient_lowered)
        grad_left = contract_last(jnp.concatenate([upstream, gradient_lowered], axis=1), weight)
        return grad_left, grad_lower, grad_raise

    hidden = tokens.astype(f32)
    normed, norm_back = jax.vjp(partial(rms_scale, scale_gain=norm_gain), hidden)
    left_in = gather_seq(normed.astype(bf16))
    cot_ring = gather_ring(cotangent)
    projected, lower_in = forward(left_in, in_weight, in_raise, mask_all)

    projected = projected.astype(bf16)
    taps = jnp.concatenate(
        [
            jnp.concatenate([head_columns(conv_weight[:, :D_SSM]), conv_weight[:, D_SSM:]], axis=1),
            jnp.concatenate([head_columns(conv_bias[:D_SSM]), conv_bias[D_SSM:]])[None],
            jnp.zeros((3, INNER + 2 * STATE), f32),
        ],
        axis=0,
    )
    rate_rows = jnp.pad(
        jnp.stack([head_items(dt_bias), -jnp.exp(head_items(decay_log))]),
        ((0, 6), (0, 128 - HEADS_DEV)),
    )
    skip_rows = jnp.pad(
        jnp.stack([jnp.repeat(head_items(skip_gain), M_HEAD), head_columns(gate_gain)]),
        ((0, 6), (0, 0)),
    )
    gain_pair = lax.dynamic_index_in_dim(
        gate_gain.reshape(12, Y_RING, M_HEAD), y, 1, keepdims=False
    ).reshape(1, -1)
    cosine_table, sine_table = rotary_tables(position)
    gated, scanned, squares, convolved, states = scan_forward(
        seq_lengths, projected, taps, rate_rows, skip_rows
    )
    attended, log_totals = attention_forward(seq_lengths, projected, cosine_table, sine_table)
    inverse = lax.rsqrt(
        sum_seq_small(squares.reshape(SEQ, 8, tok_count)[:, 0]) / D_SSM + epsilon
    )
    mixed = jnp.concatenate([attended, gated], axis=1)

    def to_ring(values):
        doubled = jnp.concatenate([values, values], axis=0)
        rolled = lax.dynamic_slice_in_dim(doubled, X_PAIR * tok_count * y, group_len, 0)
        return rolled.reshape(Y_RING, X_PAIR, tok_count, -1)

    def from_ring(values):
        flat = values.reshape(group_len, -1)
        doubled = jnp.concatenate([flat, flat], axis=0)
        start = X_PAIR * tok_count * ((Y_RING - y) % Y_RING)
        return lax.dynamic_slice_in_dim(doubled, start, group_len, 0)

    ring_len = Y_RING * tok_count
    mixed_ring = to_ring(mixed)
    kept = lax.dynamic_index_in_dim(mixed_ring, x, 1, keepdims=False).reshape(ring_len, SLICE)
    other = lax.dynamic_index_in_dim(mixed_ring, 1 - x, 1, keepdims=False).reshape(ring_len, SLICE)
    received = hop(other, side)
    low = jnp.where(x == 0, kept, received)
    high = jnp.where(x == 0, received, kept)
    gated_pair = jnp.concatenate([low[:, HEAD:], high[:, HEAD:]], axis=1).astype(f32)
    inverse_ring = lax.dynamic_index_in_dim(
        to_ring(inverse.reshape(-1, 1)), x, 1, keepdims=False
    ).reshape(ring_len, 1)
    left_out = jnp.concatenate(
        [low[:, :HEAD], high[:, :HEAD], (gated_pair * inverse_ring * gain_pair).astype(bf16)],
        axis=1,
    )
    branch_part, lower_out = forward(left_out, out_weight, out_raise, mask_ring)
    residual = hidden + scatter_ring(branch_part)
    normed_ffn, ffn_norm_back = jax.vjp(partial(rms_scale, scale_gain=ffn_gain), residual)
    left_gu = gather_ring(normed_ffn.astype(bf16))
    gate_and_up, lower_gu = forward(left_gu, gu_weight, gu_raise, mask_ring)
    activated_hidden, act_back = jax.vjp(swiglu, gate_and_up)
    left_down = activated_hidden.astype(bf16)
    ffn_part, lower_down = forward(left_down, down_weight, down_raise, mask_ring)
    layer_out = (residual + scatter_ring(ffn_part)).astype(bf16)

    grad_act, grad_a_down, grad_b_down = backward(
        left_down, lower_down, cot_ring, down_weight, down_raise, mask_ring
    )
    (grad_gate_up,) = act_back(grad_act)
    grad_gu_part, grad_a_gu, grad_b_gu = backward(
        left_gu, lower_gu, grad_gate_up.astype(bf16), gu_weight, gu_raise, mask_ring
    )
    (grad_resid_norm,) = ffn_norm_back(scatter_ring(grad_gu_part))
    grad_residual = cotangent.astype(f32) + grad_resid_norm
    grad_ring = gather_ring(grad_residual.astype(bf16))
    grad_mixed, grad_a_out, grad_b_out = backward(
        left_out, lower_out, grad_ring, out_weight, out_raise, mask_ring
    )
    early = jnp.concatenate(
        [
            grad_a_out.astype(bf16).reshape(DP, -1, 128),
            blocks_of(grad_b_out.astype(bf16)),
            grad_a_gu.astype(bf16).reshape(DP, -1, 128),
            blocks_of(grad_b_gu.astype(bf16)),
            grad_a_down.astype(bf16).reshape(DP, -1, 128),
            blocks_of(grad_b_down.astype(bf16)),
        ],
        axis=1,
    ).reshape(-1, 128)
    grad_mixed, early = lax.optimization_barrier((grad_mixed.astype(bf16), early))
    early = lax.psum_scatter(early, "dp", scatter_dimension=0, tiled=True)
    a_out_block = early[:64]
    early = early.astype(f32)
    low = jnp.concatenate([grad_mixed[:, :HEAD], grad_mixed[:, 2 * HEAD : 2 * HEAD + INNER]], axis=1)
    high = jnp.concatenate([grad_mixed[:, HEAD : 2 * HEAD], grad_mixed[:, 2 * HEAD + INNER :]], axis=1)
    kept = jnp.where(x == 0, low, high)
    received = hop(jnp.where(x == 0, high, low), side)
    first = jnp.where(x == 0, kept, received).reshape(Y_RING, 1, tok_count, SLICE)
    second = jnp.where(x == 0, received, kept).reshape(Y_RING, 1, tok_count, SLICE)
    head_grads = from_ring(jnp.concatenate([first, second], axis=1))
    slope_ring = jnp.sum(
        grad_mixed[:, 2 * HEAD :].astype(f32) * gain_pair * gated_pair, axis=1
    ).reshape(Y_RING, 1, tok_count)
    own_half = jnp.arange(X_PAIR)[None, :, None] == x
    slope = sum_seq_small(
        from_ring(jnp.where(own_half, slope_ring, 0.0)).reshape(SEQ, tok_count)
    )
    scales = jnp.stack(
        [inverse.reshape(-1), (inverse * inverse * inverse * slope / D_SSM).reshape(-1)], axis=1
    )
    grad_qkv = attention_backward(
        seq_lengths, projected, cosine_table, sine_table, head_grads[:, :HEAD], log_totals
    )
    grad_projected = scan_backward(
        seq_lengths,
        projected,
        convolved,
        scanned,
        states,
        head_grads[:, HEAD:],
        scales,
        grad_qkv,
        taps,
        rate_rows,
        skip_rows,
    )
    grad_left_part, grad_a_in, grad_b_in = backward(
        left_in, lower_in, grad_projected, in_weight, in_raise, mask_all
    )
    (grad_hidden_norm,) = norm_back(scatter_seq(grad_left_part))
    grad_tokens = (grad_residual + grad_hidden_norm).astype(bf16)

    late = jnp.concatenate(
        [grad_a_in.astype(bf16).reshape(DP, -1, 128), blocks_of(grad_b_in.astype(bf16))], axis=1
    )
    late = jnp.sum(
        lax.all_to_all(late, "dp", split_axis=0, concat_axis=0).astype(f32), axis=0
    )
    a_in_own = late[:128]
    b_in_own = row_from_blocks(late[128:])
    b_out_own = early[64:192]
    a_gu_own = early[192:320]
    b_gu_own = early[320:448]
    a_down_own = early[448:512]
    b_down_own = early[512:640]
    zero_rows = jnp.zeros((256, 128), f32)
    a_out_own = lax.dynamic_update_slice_in_dim(
        zero_rows, jnp.where(own_rows, early[:64], 0.0), 64 * y, 0
    )
    for k in range(1, Y_RING):
        pairs = [(((i // 2 + k) % Y_RING) * SEQ + i, (i // 2) * SEQ + i) for i in range(SEQ)]
        moved = lax.ppermute(a_out_block, ("dp", "sp"), pairs)
        a_out_own = a_out_own + lax.dynamic_update_slice_in_dim(
            zero_rows, moved.astype(f32), 64 * ((y + k) % Y_RING), 0
        )
    a_down_own = lax.dynamic_update_slice_in_dim(zero_rows, a_down_own, 64 * y, 0)
    b_gu_full = lax.dynamic_update_slice_in_dim(
        jnp.zeros((8, 2 * DP, Y_RING, 64), f32),
        row_from_blocks(b_gu_own).reshape(8, 2 * DP, 1, 64),
        y,
        2,
    ).reshape(512, 128)

    def spread_heads(part, width):
        return lax.dynamic_update_slice(
            jnp.zeros((8, 12, Y_RING, width), f32),
            part.reshape(8, HEADS_DEV, 1, width),
            (0, HEADS_DEV * x, y, 0),
        ).reshape(8, -1)

    kv_width = H_KV * HEAD
    b_in_full = jnp.concatenate(
        [
            lax.dynamic_update_slice_in_dim(
                jnp.zeros((8, EDGE_INNER), f32), b_in_own[:, COL_Q:COL_INNER], s * HEAD, 1
            ),
            spread_heads(b_in_own[:, COL_INNER:COL_GATE], M_HEAD),
            lax.dynamic_update_slice_in_dim(
                jnp.zeros((8, kv_width), f32), b_in_own[:, COL_K:COL_V], kv_head * HEAD, 1
            ),
            lax.dynamic_update_slice_in_dim(
                jnp.zeros((8, kv_width), f32), b_in_own[:, COL_V:COL_BC], kv_head * HEAD, 1
            ),
            b_in_own[:, COL_BC:COL_STEP],
            spread_heads(b_in_own[:, COL_GATE:COL_K], M_HEAD),
            spread_heads(b_in_own[:, COL_STEP : COL_STEP + HEADS_DEV], 1),
            jnp.zeros((8, 80), f32),
        ],
        axis=1,
    )
    full = jnp.concatenate(
        [
            a_in_own,
            b_in_full.reshape(-1, 128),
            a_out_own,
            b_out_own,
            a_gu_own,
            b_gu_full,
            a_down_own,
            b_down_own,
        ],
        axis=0,
    )
    full = jnp.pad(full, ((0, (-full.shape[0]) % 128), (0, 0)))
    full = gather_seq(scatter_seq(full).astype(bf16)).astype(f32)
    out_a_in = full[:128]
    out_b_in = full[128:648].reshape(8, -1)[:, : EDGE_STEP + M_HEADS]
    full = full[648:]
    out_a_out = full[:256]
    out_b_out = row_from_blocks(full[256:384])
    out_a_gu = full[384:512]
    out_b_gu = full[512:1024].reshape(8, -1)
    out_a_down = full[1024:1280]
    out_b_down = row_from_blocks(full[1280:1408])
    return (
        layer_out,
        grad_tokens,
        out_a_in,
        out_b_in,
        out_a_out,
        out_b_out,
        out_a_gu,
        out_b_gu,
        out_a_down,
        out_b_down,
    )


def solution(mesh):
    rows = P("dp", None)
    both = P(("dp", "sp"), None)
    in_specs = (both, both) + (rows,) * 2 + (P(),) * 8 + (rows,) * 12
    out_specs = (both, both) + (rows,) * 8
    return jax.shard_map(
        per_device, mesh=mesh, in_specs=in_specs, out_specs=out_specs, check_vma=False
    )
```

```python
from functools import partial

import jax
import jax.numpy as jnp
from jax import lax
from jax.experimental import pallas as pl
from jax.experimental.pallas import tpu as pltpu
from jax.sharding import PartitionSpec as P

H_Q = 8
H_KV = 2
HEAD = 128
M_HEADS = 48
M_HEAD = 64
CONV = 4
ADAPTER_RANK = 16
ADAPTER_SETS = 8
SPAN = 128
STATE = 256
D_SSM = 3072
SHARED = 1024
ADAPTERS = ADAPTER_RANK * ADAPTER_SETS

Y_RING = 4
X_PAIR = 2
SEQ = 8
DP = 16
HEADS_DEV = 6
INNER = HEADS_DEV * M_HEAD
SLICE = HEAD + INNER
MIX = X_PAIR * SLICE
UNITS = 1024

COL_Q = 0
COL_INNER = COL_Q + HEAD
COL_GATE = COL_INNER + INNER
COL_K = COL_GATE + INNER
COL_V = COL_K + HEAD
COL_BC = COL_V + HEAD
COL_STEP = COL_BC + 2 * STATE
IN_COLS = COL_STEP + 128

EDGE_INNER = H_Q * HEAD
EDGE_SHARED = EDGE_INNER + D_SSM
EDGE_GATE = EDGE_SHARED + SHARED
EDGE_STEP = EDGE_GATE + D_SSM

CONVOLVED = INNER + 2 * STATE

epsilon = 1e-05
rope_base = 100000000000.0
masked_score = -1e30
highest = lax.Precision.HIGHEST
bf16 = jnp.bfloat16
f32 = jnp.float32


def rms_scale(vectors, scale_gain):
    return (
        vectors
        * lax.rsqrt(jnp.mean(vectors * vectors, axis=-1, keepdims=True) + epsilon)
        * scale_gain
    )


def silu_value(vectors):
    return vectors * jax.nn.sigmoid(vectors)


def swiglu(gate_and_up):
    half_width = gate_and_up.shape[1] // 2
    return silu_value(gate_and_up[:, :half_width]) * gate_and_up[:, half_width:]


def rotary_tables(position):
    lanes = jnp.arange(HEAD)
    half_width = HEAD // 2
    frequency = rope_base ** (-((lanes % half_width).astype(f32) * 2.0 / HEAD))
    angle = position.astype(f32)[:, None] * frequency[None, :]
    return jnp.cos(angle), jnp.where(lanes < half_width, -1.0, 1.0) * jnp.sin(angle)


def product(left, right):
    return jnp.dot(left, right, preferred_element_type=f32)


def contract_last(left, right):
    return lax.dot_general(left, right, (((1,), (1,)), ((), ())), preferred_element_type=f32)


def contract_first(left, right):
    return lax.dot_general(left, right, (((0,), (0,)), ((), ())), preferred_element_type=f32)


def hop(value, target):
    return lax.ppermute(value, "sp", [(i, target(i)) for i in range(SEQ)])


def up(i):
    return (i + X_PAIR) % SEQ


def down(i):
    return (i - X_PAIR) % SEQ


def side(i):
    return i ^ 1


def gather_ring(block):
    half = block.shape[0] // 2
    below = hop(block, up)
    above = hop(block, down)
    far_first = hop(below[:half], up)
    far_second = hop(above[half:], down)
    return jnp.concatenate([block, above, far_first, far_second, below], axis=0)


def scatter_ring(partial_rows, *after):
    n = partial_rows.shape[0] // Y_RING
    half = n // 2
    far = partial_rows[2 * n : 3 * n].astype(bf16)
    from_below = hop(far[:half], up)
    from_above = hop(far[half:], down)
    from_below, from_above, *after = lax.optimization_barrier((from_below, from_above, *after))
    partial_rows = partial_rows.astype(f32)
    to_up = partial_rows[n : 2 * n]
    to_up = jnp.concatenate([to_up[:half] + from_below.astype(f32), to_up[half:]], axis=0)
    to_down = partial_rows[3 * n :]
    to_down = jnp.concatenate([to_down[:half], to_down[half:] + from_above.astype(f32)], axis=0)
    low = hop(to_up.astype(bf16), up).astype(f32)
    high = hop(to_down.astype(bf16), down).astype(f32)
    return partial_rows[:n] + low + high, *after


def halve_shards(stack, core):
    rows = stack.shape[1]
    pairs = stack.reshape(DP // 2, 2, rows, 128)
    kept = lax.dynamic_index_in_dim(pairs, core, 1, keepdims=False)
    sent = lax.dynamic_index_in_dim(pairs, 1 - core, 1, keepdims=False)
    received = lax.ppermute(sent, "dp", [(i, i ^ 1) for i in range(DP)])
    return (kept.astype(f32) + received.astype(f32)).astype(bf16)


CHIPS = [[2 * i + c for i in range(DP // 2)] for c in range(2)]


def scatter_shards(stack, core):
    both = halve_shards(stack, core).reshape(-1, 128)
    return lax.psum_scatter(
        both, "dp", scatter_dimension=0, axis_index_groups=CHIPS, tiled=True
    ).astype(f32)


def exchange_shards(stack, core):
    both = lax.all_to_all(
        halve_shards(stack, core), "dp", split_axis=0, concat_axis=0, axis_index_groups=CHIPS
    )
    return jnp.sum(both.astype(f32), axis=0)


def gather_seq(block):
    copies = jnp.broadcast_to(block[None], (SEQ,) + block.shape)
    return lax.all_to_all(copies, "sp", split_axis=0, concat_axis=0).reshape(
        (SEQ * block.shape[0],) + block.shape[1:]
    )


def scatter_seq(partial_rows):
    n = partial_rows.shape[0] // SEQ
    pieces = partial_rows.astype(bf16).reshape((SEQ, n) + partial_rows.shape[1:])
    return jnp.sum(
        lax.all_to_all(pieces, "sp", split_axis=0, concat_axis=0).astype(f32), axis=0
    )


def gather_rings(block, y, x):
    n = block.shape[0]
    half = n // 2
    mate = hop(block, side)
    above = hop(block, down)
    below = hop(block, up)
    mate_above = hop(mate, down)
    mate_below = hop(mate, up)
    out = jnp.zeros((SEQ * n,) + block.shape[1:], block.dtype)
    for rows, distance, column, shift in (
        (block, 0, x, 0),
        (above, 1, x, 0),
        (below, 3, x, 0),
        (mate, 0, 1 - x, 0),
        (hop(below[:half], up), 2, x, 0),
        (hop(above[half:], down), 2, x, half),
        (mate_above, 1, 1 - x, 0),
        (mate_below, 3, 1 - x, 0),
        (hop(mate_below[:half], up), 2, 1 - x, 0),
        (hop(mate_above[half:], down), 2, 1 - x, half),
    ):
        start = n * (X_PAIR * ((y + distance) % Y_RING) + column) + shift
        out = lax.dynamic_update_slice_in_dim(out, rows, start, 0)
    return out


def sum_ring_small(value):
    total = value
    for offset in range(X_PAIR, SEQ, X_PAIR):
        total = total + hop(value, lambda i, offset=offset: (i + offset) % SEQ)
    return total


def blocks_of(matrix):
    n = matrix.shape[1] // 128
    return matrix.reshape(DP, 8, n, 128).transpose(0, 2, 1, 3).reshape(DP, 8 * n, 128)


def row_from_blocks(stacked):
    n = stacked.shape[0] // 8
    return stacked.reshape(n, 8, 128).transpose(1, 0, 2).reshape(8, 128 * n)


def sixteen_rows(rows):
    return jnp.pad(rows, ((0, 16 - rows.shape[0]), (0, 0)))


def pick_columns(block, y):
    rows = lax.broadcasted_iota(jnp.int32, (512, 128), 0)
    lanes = lax.broadcasted_iota(jnp.int32, (512, 128), 1)
    wanted = jnp.where(lanes < M_HEAD, lanes, lanes + 256 - M_HEAD) + M_HEAD * y
    return product(block, (rows == wanted).astype(bf16))


def pack_input_kernel(place_ref, weight_ref, lower_ref, upper_ref, out_ref):
    s = place_ref[0]
    y = s // X_PAIR
    x = s % X_PAIR
    kv_head = s // (H_Q // H_KV)

    def at(column):
        return pl.ds(pl.multiple_of(column, 128), 128)

    def share(ref):
        def heads(edge):
            return [
                pick_columns(
                    ref[:, pl.ds(pl.multiple_of(edge + 256 * (HEADS_DEV * x + 2 * pair), 128), 512)], y
                )
                for pair in range(HEADS_DEV // 2)
            ]

        step_rows = lax.broadcasted_iota(jnp.int32, (M_HEADS, 128), 0)
        step_lanes = lax.broadcasted_iota(jnp.int32, (M_HEADS, 128), 1)
        picked = (step_rows == Y_RING * (HEADS_DEV * x + step_lanes) + y) & (step_lanes < HEADS_DEV)
        return (
            [ref[:, at(HEAD * s)].astype(f32)]
            + heads(EDGE_INNER)
            + heads(EDGE_GATE)
            + [
                ref[:, at(EDGE_SHARED + HEAD * kv_head)].astype(f32),
                ref[:, at(EDGE_SHARED + HEAD * (H_KV + kv_head))].astype(f32),
            ]
            + [
                ref[:, EDGE_SHARED + 2 * H_KV * HEAD + 128 * i : EDGE_SHARED + 2 * H_KV * HEAD + 128 * i + 128].astype(f32)
                for i in range(2 * STATE // 128)
            ]
            + [product(ref[:, EDGE_STEP:], picked.astype(bf16))]
        )

    for i, piece in enumerate(share(weight_ref)):
        out_ref[:, 128 * i : 128 * i + 128] = piece.astype(bf16)
    out_ref[:, IN_COLS : IN_COLS + ADAPTERS] = lower_ref[...]
    upper = [piece[:8] for piece in share(upper_ref)]
    upper.append(jnp.zeros((128 - 8 * len(upper), 128), f32))
    out_ref[:, IN_COLS + ADAPTERS :] = jnp.concatenate(upper, axis=0).astype(bf16)


def pack_ffn_kernel(
    place_ref, gu_ref, gu_lower_ref, gu_upper_ref, down_ref, down_lower_ref, down_upper_ref, out_ref
):
    y = place_ref[0] // X_PAIR
    fold = down_ref.shape[1] // 2
    rows = pl.ds(pl.multiple_of(64 * y, 64), 64)
    out_ref[:64, :fold] = down_ref[rows, :fold]
    out_ref[64:, :fold] = down_ref[rows, fold:]
    pairs = 2 * UNITS // 128
    for i in range(pairs):
        out_ref[:, fold + 128 * i : fold + 128 * i + 128] = pick_columns(
            gu_ref[:, 512 * i : 512 * i + 512], y
        ).astype(bf16)
    edge = fold + 2 * UNITS
    out_ref[:, edge : edge + 128] = gu_lower_ref[...]
    edge += 128
    out_ref[:64, edge : edge + 128] = down_lower_ref[rows, :]
    out_ref[64:, edge : edge + 128] = jnp.zeros((64, 128), bf16)
    edge += 128
    out_ref[:, edge : edge + 128] = jnp.concatenate(
        [pick_columns(gu_upper_ref[:, 512 * i : 512 * i + 512], y)[:8] for i in range(pairs)], axis=0
    ).astype(bf16)
    edge += 128
    out_ref[:, edge:] = jnp.concatenate(
        [down_upper_ref[:, 128 * i : 128 * i + 128].astype(f32)[:8] for i in range(2 * fold // 128)],
        axis=0,
    ).astype(bf16)


def fold_upper(upper_ref, out_ref, column):
    for c in range(2):
        out_ref[:, column + 128 * c : column + 128 * c + 128] = jnp.concatenate(
            [
                upper_ref[:, 1024 * c + 128 * i : 1024 * c + 128 * i + 128].astype(f32)[:8]
                for i in range(8)
            ],
            axis=0,
        ).astype(bf16)


def pack_output_kernel(rows_ref, upper_ref, out_ref):
    width = rows_ref.shape[1]
    out_ref[:, :width] = rows_ref[...]
    fold_upper(upper_ref, out_ref, width)


def raising_kernel(*refs):
    out_ref = refs[-1]
    column = 0
    for ref in refs[:-1]:
        stacked = ref[...].astype(f32)
        depth = stacked.shape[0] // DP
        for block in range(min(depth // 8, out_ref.shape[1] // 128)):
            out_ref[:, column : column + 128] = jnp.concatenate(
                [
                    stacked[depth * shard + 8 * block : depth * shard + 8 * block + 8]
                    for shard in range(DP)
                ],
                axis=0,
            ).astype(bf16)
            column += 128


def raising(stacks, width):
    return pl.pallas_call(
        raising_kernel,
        in_specs=[pl.BlockSpec(memory_space=pltpu.VMEM)] * len(stacks),
        out_specs=pl.BlockSpec(memory_space=pltpu.VMEM),
        out_shape=jax.ShapeDtypeStruct((ADAPTERS, width), bf16),
        compiler_params=pltpu.CompilerParams(vmem_limit_bytes=32 * 1024 * 1024),
    )(*stacks)


def pack(kernel, arrays, shape):
    return pl.pallas_call(
        kernel,
        in_specs=[
            pl.BlockSpec(memory_space=pltpu.SMEM if a.ndim == 1 else pltpu.VMEM) for a in arrays
        ],
        out_specs=pl.BlockSpec(memory_space=pltpu.VMEM),
        out_shape=jax.ShapeDtypeStruct(shape, bf16),
        compiler_params=pltpu.CompilerParams(vmem_limit_bytes=32 * 1024 * 1024),
    )(*arrays)


def lane_index(shape):
    return lax.broadcasted_iota(jnp.int32, shape, 1)


def row_index(shape):
    return lax.broadcasted_iota(jnp.int32, shape, 0)


def over_heads(per_head):
    rows = per_head.shape[0]
    low = lane_index((rows, 128)) < M_HEAD
    return jnp.concatenate(
        [
            jnp.where(low, per_head[:, 2 * pair : 2 * pair + 1], per_head[:, 2 * pair + 1 : 2 * pair + 2])
            for pair in range(HEADS_DEV // 2)
        ],
        axis=1,
    )


def head_sums(values):
    member = (row_index((INNER, 128)) // M_HEAD == lane_index((INNER, 128))).astype(bf16)
    coarse = values.astype(bf16)
    fine = (values - coarse.astype(f32)).astype(bf16)
    return product(coarse, member) + product(fine, member)


def span_terms(convolved, step_block, rate_rows, first_len, start):
    shifted = step_block + rate_rows[0:1]
    rates = jnp.log1p(jnp.exp(-jnp.abs(shifted))) + jnp.maximum(shifted, 0.0)
    log_decay = rates * rate_rows[1:2]
    rows = row_index((SPAN, SPAN))
    lanes = lane_index((SPAN, SPAN))
    below = rows >= lanes
    cumulative = jnp.dot(
        below.astype(f32), log_decay, precision=highest, preferred_element_type=f32
    )
    seg_rows = (rows + start >= first_len).astype(jnp.int32)
    seg_lanes = (lanes + start >= first_len).astype(jnp.int32)
    allowed = below & (seg_rows == seg_lanes)
    last_seg = (start + SPAN - 1 >= first_len).astype(jnp.int32)
    previous = (start - 1 >= first_len).astype(jnp.int32)
    total = cumulative[SPAN - 1 : SPAN]
    entry = jnp.where(seg_rows == previous, jnp.exp(cumulative), 0.0)
    tail = jnp.where(seg_rows == last_seg, jnp.exp(total - cumulative), 0.0)
    keep = jnp.where(last_seg == previous, jnp.exp(total), 0.0)
    activated = convolved * jax.nn.sigmoid(convolved)
    x_in = activated[:, :INNER]
    in_state = activated[:, INNER : INNER + STATE]
    out_state = activated[:, INNER + STATE :]
    return shifted, rates, cumulative, allowed, entry, tail, keep, x_in, in_state, out_state


def decay_of(cumulative, across, allowed, head):
    gap = cumulative[:, head : head + 1] - across[head : head + 1]
    return jnp.exp(jnp.where(allowed, gap, masked_score))


def scan_forward_kernel(
    lengths_ref,
    proj_ref,
    taps_ref,
    rate_rows_ref,
    skip_ref,
    gated_ref,
    scanned_ref,
    squares_ref,
    convolved_ref,
    states_ref,
    state,
    last_rows,
):
    step = pl.program_id(0)
    start = step * SPAN
    first_len = lengths_ref[0, 0]

    @pl.when(step == 0)
    def _():
        state[...] = jnp.zeros_like(state)
        last_rows[...] = jnp.zeros_like(last_rows)

    signal = jnp.concatenate(
        [proj_ref[:, COL_INNER:COL_GATE], proj_ref[:, COL_BC:COL_STEP]], axis=1
    ).astype(f32)
    row = start + row_index((SPAN, 1))
    position = row - jnp.where(row >= first_len, first_len, 0)
    convolved = taps_ref[4:5] + taps_ref[3:4] * signal
    before = last_rows[...]
    top = row_index((8, 1))
    for offset in range(1, CONV):
        moved = pltpu.roll(signal, offset, 0)
        edge = jnp.where(top < offset, pltpu.roll(before, offset, 0), moved[:8])
        moved = jnp.concatenate([edge, moved[8:]], axis=0)
        convolved = convolved + taps_ref[3 - offset : 4 - offset] * jnp.where(
            position >= offset, moved, 0.0
        )
    last_rows[...] = signal[SPAN - 8 :]
    convolved_ref[...] = convolved
    step_block = proj_ref[:, COL_STEP:].astype(f32)
    _, rates, cumulative, allowed, entry, tail, keep, x_in, in_state, out_state = span_terms(
        convolved, step_block, rate_rows_ref[...], first_len, start
    )
    across = cumulative.T
    in_half = in_state.astype(bf16)
    out_half = out_state.astype(bf16)
    state_now = state[...]
    state_half = state_now.astype(bf16)
    states_ref[0] = state_half
    mixing = contract_last(out_half, in_half)
    rates_wide = over_heads(rates)
    weighted = (x_in * rates_wide).astype(bf16)
    low = lane_index((SPAN, 128)) < M_HEAD
    within = []
    for pair in range(HEADS_DEV // 2):
        block = weighted[:, 128 * pair : 128 * pair + 128]
        sides = [
            product(
                (mixing * decay_of(cumulative, across, allowed, 2 * pair + i)).astype(bf16), block
            )
            for i in range(2)
        ]
        within.append(jnp.where(low, sides[0], sides[1]))
    result = (
        jnp.concatenate(within, axis=1)
        + product(out_half, state_half) * over_heads(entry)
        + skip_ref[0:1] * x_in
    )
    scanned = result.astype(bf16)
    scanned_ref[...] = scanned
    gate = proj_ref[:, COL_GATE:COL_K].astype(f32)
    gated = scanned.astype(f32) * (gate * jax.nn.sigmoid(gate))
    gated_ref[...] = gated.astype(bf16)
    squares_ref[...] = lax.dot_general(
        jnp.ones((8, INNER), f32),
        gated * gated,
        (((1,), (1,)), ((), ())),
        precision=highest,
        preferred_element_type=f32,
    )
    state[...] = state_now * over_heads(keep) + contract_first(
        in_half, (x_in * over_heads(tail * rates)).astype(bf16)
    )


def scan_backward_kernel(
    lengths_ref,
    proj_ref,
    convolved_ref,
    scanned_ref,
    states_ref,
    upstream_ref,
    scales_ref,
    grad_query_ref,
    grad_key_ref,
    grad_value_ref,
    taps_ref,
    rate_rows_ref,
    skip_ref,
    out_ref,
    grad_state,
    next_rows,
):
    step = pl.num_programs(0) - 1 - pl.program_id(0)
    start = step * SPAN
    first_len = lengths_ref[0, 0]

    @pl.when(pl.program_id(0) == 0)
    def _():
        grad_state[...] = jnp.zeros_like(grad_state)
        next_rows[...] = jnp.zeros_like(next_rows)

    convolved = convolved_ref[...]
    step_block = proj_ref[:, COL_STEP:].astype(f32)
    rate_rows = rate_rows_ref[...]
    shifted, rates, cumulative, allowed, entry, tail, keep, x_in, in_state, out_state = span_terms(
        convolved, step_block, rate_rows, first_len, start
    )
    across = cumulative.T
    in_half = in_state.astype(bf16)
    out_half = out_state.astype(bf16)
    state_half = states_ref[0]

    gate = proj_ref[:, COL_GATE:COL_K].astype(f32)
    gate_sigmoid = jax.nn.sigmoid(gate)
    gate_silu = gate * gate_sigmoid
    scanned = scanned_ref[...].astype(f32)
    upstream = upstream_ref[...].astype(f32) * skip_ref[1:2]
    grad_gated = scales_ref[:, 0:1] * upstream - scales_ref[:, 1:2] * (scanned * gate_silu)
    out_ref[:, COL_GATE:COL_K] = (
        grad_gated * scanned * (gate_sigmoid * (1.0 + gate * (1.0 - gate_sigmoid)))
    ).astype(bf16)
    grad_half = (grad_gated * gate_silu).astype(bf16)
    grad_result = grad_half.astype(f32)

    mixing = contract_last(out_half, in_half)
    rates_wide = over_heads(rates)
    entry_wide = over_heads(entry)
    tail_wide = over_heads(tail)
    keep_wide = over_heads(keep)
    weighted = (x_in * rates_wide).astype(bf16)
    lane = lane_index((SPAN, 128))
    low = lane < M_HEAD
    grad_mixing = jnp.zeros((SPAN, SPAN), f32)
    grad_cumulative = jnp.zeros((SPAN, 128), f32)
    grad_across = jnp.zeros((SPAN, 128), f32)
    head_row = row_index((SPAN, 128))
    grad_weighted = []
    for pair in range(HEADS_DEV // 2):
        block = weighted[:, 128 * pair : 128 * pair + 128]
        grad_block = grad_half[:, 128 * pair : 128 * pair + 128]
        sides = []
        for i in range(2):
            head = 2 * pair + i
            decay = decay_of(cumulative, across, allowed, head)
            spread = mixing * decay
            sides.append(contract_first(spread.astype(bf16), grad_block))
            mine = low if i == 0 else jnp.logical_not(low)
            grad_spread = contract_last(jnp.where(mine, grad_block, jnp.zeros_like(grad_block)), block)
            grad_mixing = grad_mixing + grad_spread * decay
            grad_gap = grad_spread * spread
            grad_cumulative = jnp.where(
                lane == head, jnp.sum(grad_gap, axis=1, keepdims=True), grad_cumulative
            )
            grad_across = jnp.where(
                head_row == head, jnp.sum(grad_gap, axis=0, keepdims=True), grad_across
            )
        grad_weighted.append(jnp.where(low, sides[0], sides[1]))
    grad_weighted = jnp.concatenate(grad_weighted, axis=1)
    grad_cumulative = grad_cumulative - grad_across.T

    grad_next = grad_state[...]
    grad_next_half = grad_next.astype(bf16)
    grad_entered = (grad_result * entry_wide).astype(bf16)
    from_state = product(out_half, state_half)
    to_state = product(in_half, grad_next_half)
    tail_rates = tail_wide * rates_wide
    grad_mixing_half = grad_mixing.astype(bf16)
    grad_out_state = product(grad_mixing_half, in_half) + contract_last(grad_entered, state_half)
    grad_in_state = contract_first(grad_mixing_half, out_half) + contract_last(
        (x_in * tail_rates).astype(bf16), grad_next_half
    )
    sums = head_sums(
        jnp.concatenate(
            [
                grad_result * from_state,
                to_state * x_in,
                grad_weighted * x_in,
                jnp.broadcast_to(
                    jnp.sum(grad_next * state_half.astype(f32), axis=0, keepdims=True), (8, INNER)
                ),
            ],
            axis=0,
        )
    )
    grad_entry = sums[:SPAN]
    grad_tail = sums[SPAN : 2 * SPAN]
    grad_rates = sums[2 * SPAN : 3 * SPAN] + grad_tail * tail
    from_tail = grad_tail * tail * rates
    grad_total = (
        jnp.sum(from_tail, axis=0, keepdims=True) + sums[3 * SPAN : 3 * SPAN + 1] * keep
    )
    grad_cumulative = grad_cumulative + grad_entry * entry - from_tail
    grad_cumulative = grad_cumulative + jnp.where(head_row == SPAN - 1, grad_total, 0.0)
    above = (row_index((SPAN, SPAN)) <= lane_index((SPAN, SPAN))).astype(f32)
    grad_decay = jnp.dot(above, grad_cumulative, precision=highest, preferred_element_type=f32)
    grad_rates = grad_rates + grad_decay * rate_rows[1:2]
    out_ref[:, COL_STEP:] = jnp.where(
        lane < HEADS_DEV, grad_rates * jax.nn.sigmoid(shifted), 0.0
    ).astype(bf16)
    grad_x = grad_weighted * rates_wide + to_state * tail_rates + skip_ref[0:1] * grad_result
    grad_state[...] = grad_next * keep_wide + contract_first(out_half, grad_entered)

    conv_sigmoid = jax.nn.sigmoid(convolved)
    grad_conv = jnp.concatenate([grad_x, grad_in_state, grad_out_state], axis=1) * (
        conv_sigmoid * (1.0 + convolved * (1.0 - conv_sigmoid))
    )
    row = start + row_index((SPAN, 1))
    position = row - jnp.where(row >= first_len, first_len, 0)
    later_row = start + SPAN + row_index((8, 1))
    later_position = later_row - jnp.where(later_row >= first_len, first_len, 0)
    later = next_rows[...]
    bottom = row_index((8, 1))
    grad_signal = taps_ref[3:4] * grad_conv
    for offset in range(1, CONV):
        moved = pltpu.roll(jnp.where(position >= offset, grad_conv, 0.0), SPAN - offset, 0)
        edge = pltpu.roll(jnp.where(later_position >= offset, later, 0.0), 8 - offset, 0)
        edge = jnp.where(bottom >= 8 - offset, edge, moved[SPAN - 8 :])
        moved = jnp.concatenate([moved[: SPAN - 8], edge], axis=0)
        grad_signal = grad_signal + taps_ref[3 - offset : 4 - offset] * moved
    next_rows[...] = grad_conv[:8]
    out_ref[:, COL_INNER:COL_GATE] = grad_signal[:, :INNER].astype(bf16)
    out_ref[:, COL_BC:COL_STEP] = grad_signal[:, INNER:].astype(bf16)
    out_ref[:, :COL_INNER] = grad_query_ref[...]
    out_ref[:, COL_K:COL_V] = grad_key_ref[...]
    out_ref[:, COL_V:COL_BC] = grad_value_ref[...]


def whole(shape):
    return pl.BlockSpec(shape, lambda i: (0,) * len(shape))


smem = pl.BlockSpec(memory_space=pltpu.SMEM)


def scan_forward(lengths, proj, taps, rate_rows, skip_rows):
    length_all = proj.shape[0]
    spans = length_all // SPAN

    def rows(width):
        return pl.BlockSpec((SPAN, width), lambda i: (i, 0))

    return pl.pallas_call(
        scan_forward_kernel,
        grid=(spans,),
        in_specs=[smem, rows(IN_COLS), whole(taps.shape), whole(rate_rows.shape), whole(skip_rows.shape)],
        out_specs=[
            rows(INNER),
            rows(INNER),
            pl.BlockSpec((8, SPAN), lambda i: (i, 0)),
            rows(CONVOLVED),
            pl.BlockSpec((1, STATE, INNER), lambda i: (i, 0, 0)),
        ],
        out_shape=[
            jax.ShapeDtypeStruct((length_all, INNER), bf16),
            jax.ShapeDtypeStruct((length_all, INNER), bf16),
            jax.ShapeDtypeStruct((8 * spans, SPAN), f32),
            jax.ShapeDtypeStruct((length_all, CONVOLVED), f32),
            jax.ShapeDtypeStruct((spans, STATE, INNER), bf16),
        ],
        scratch_shapes=[pltpu.VMEM((STATE, INNER), f32), pltpu.VMEM((8, CONVOLVED), f32)],
        compiler_params=pltpu.CompilerParams(vmem_limit_bytes=16 * 1024 * 1024),
        cost_estimate=pl.CostEstimate(flops=10**10, bytes_accessed=10**7, transcendentals=10**6),
        name="scan_forward",
    )(lengths, proj, taps, rate_rows, skip_rows)


def scan_backward(
    lengths, proj, convolved, scanned, states, upstream, scales, grad_qkv, taps, rate_rows, skip_rows
):
    length_all = proj.shape[0]
    spans = length_all // SPAN

    def rows(width):
        return pl.BlockSpec((SPAN, width), lambda i: (spans - 1 - i, 0))

    return pl.pallas_call(
        scan_backward_kernel,
        grid=(spans,),
        in_specs=[
            smem,
            rows(IN_COLS),
            rows(CONVOLVED),
            rows(INNER),
            pl.BlockSpec((1, STATE, INNER), lambda i: (spans - 1 - i, 0, 0)),
            rows(INNER),
            rows(2),
            rows(HEAD),
            rows(HEAD),
            rows(HEAD),
            whole(taps.shape),
            whole(rate_rows.shape),
            whole(skip_rows.shape),
        ],
        out_specs=rows(IN_COLS),
        out_shape=jax.ShapeDtypeStruct((length_all, IN_COLS), bf16),
        scratch_shapes=[pltpu.VMEM((STATE, INNER), f32), pltpu.VMEM((8, CONVOLVED), f32)],
        compiler_params=pltpu.CompilerParams(vmem_limit_bytes=16 * 1024 * 1024),
        cost_estimate=pl.CostEstimate(flops=17 * 10**9, bytes_accessed=10**7, transcendentals=10**6),
        name="scan_backward",
    )(lengths, proj, convolved, scanned, states, upstream, scales, *grad_qkv, taps, rate_rows, skip_rows)


QUERY_ROWS = 256
score_scale = HEAD ** (-0.5)


def turn(values, cosine, sine):
    return values * cosine + pltpu.roll(values, HEAD // 2, 1) * sine


def allowed_scores(query_rot, key_rot, first_row, first_len):
    scores = contract_last(query_rot, key_rot) * score_scale
    rows = first_row + row_index(scores.shape)
    lanes = lane_index(scores.shape)
    allowed = (lanes <= rows) & ((lanes >= first_len) | (rows < first_len))
    return jnp.where(allowed, scores, masked_score)


def attention_forward_kernel(
    lengths_ref, query_ref, key_ref, value_ref, cosine_ref, sine_ref, out_ref, totals_ref
):
    first_len = lengths_ref[0, 0]
    length_all = query_ref.shape[0]
    key_rot = turn(key_ref[...].astype(f32), cosine_ref[...], sine_ref[...]).astype(bf16)
    for first in range(0, length_all, QUERY_ROWS):
        block = slice(first, first + QUERY_ROWS)
        seen = first + QUERY_ROWS
        query_rot = turn(
            query_ref[block].astype(f32), cosine_ref[block], sine_ref[block]
        ).astype(bf16)
        scores = allowed_scores(query_rot, key_rot[:seen], first, first_len)
        peak = jnp.max(scores, axis=1, keepdims=True)
        exponent = jnp.exp(scores - peak)
        total = jnp.sum(exponent, axis=1, keepdims=True)
        probs = (exponent * (1.0 / total)).astype(bf16)
        out_ref[block] = product(probs, value_ref[:seen]).astype(bf16)
        totals_ref[block] = peak + jnp.log(total)


def attention_backward_kernel(
    lengths_ref,
    query_ref,
    key_ref,
    value_ref,
    cosine_ref,
    sine_ref,
    upstream_ref,
    totals_ref,
    grad_query_ref,
    grad_key_ref,
    grad_value_ref,
    key_sum,
    value_sum,
):
    first_len = lengths_ref[0, 0]
    length_all = query_ref.shape[0]
    key_rot = turn(key_ref[...].astype(f32), cosine_ref[...], sine_ref[...]).astype(bf16)
    key_sum[...] = jnp.zeros_like(key_sum)
    value_sum[...] = jnp.zeros_like(value_sum)
    for first in range(0, length_all, QUERY_ROWS):
        block = slice(first, first + QUERY_ROWS)
        seen = first + QUERY_ROWS
        cosine = cosine_ref[block]
        sine = sine_ref[block]
        query_rot = turn(query_ref[block].astype(f32), cosine, sine).astype(bf16)
        probs = jnp.exp(
            allowed_scores(query_rot, key_rot[:seen], first, first_len) - totals_ref[block]
        )
        upstream = upstream_ref[block]
        grad_probs = contract_last(upstream, value_ref[:seen])
        delta = jnp.sum(probs * grad_probs, axis=1, keepdims=True)
        grad_scores = (probs * (grad_probs - delta)).astype(bf16)
        grad_query_ref[block] = turn(
            product(grad_scores, key_rot[:seen]) * score_scale, cosine, -sine
        ).astype(bf16)
        key_sum[:seen] += contract_first(grad_scores, query_rot)
        value_sum[:seen] += contract_first(probs.astype(bf16), upstream)
    grad_key_ref[...] = turn(
        key_sum[...] * score_scale, cosine_ref[...], -sine_ref[...]
    ).astype(bf16)
    grad_value_ref[...] = value_sum[...].astype(bf16)


def head_block(length_all, column):
    return pl.BlockSpec((length_all, HEAD), lambda i: (0, column // HEAD))


def attention_forward(lengths, proj, cosine, sine):
    length_all = proj.shape[0]
    block = head_block(length_all, 0)
    return pl.pallas_call(
        attention_forward_kernel,
        grid=(1,),
        in_specs=[
            smem,
            block,
            head_block(length_all, COL_K),
            head_block(length_all, COL_V),
            block,
            block,
        ],
        out_specs=[block, pl.BlockSpec((length_all, 1), lambda i: (0, 0))],
        out_shape=[
            jax.ShapeDtypeStruct((length_all, HEAD), bf16),
            jax.ShapeDtypeStruct((length_all, 1), f32),
        ],
        compiler_params=pltpu.CompilerParams(vmem_limit_bytes=20 * 1024 * 1024),
        name="attention_forward",
    )(lengths, proj, proj, proj, cosine, sine)


def attention_backward(lengths, proj, cosine, sine, upstream, totals):
    length_all = proj.shape[0]
    block = head_block(length_all, 0)
    return pl.pallas_call(
        attention_backward_kernel,
        grid=(1,),
        in_specs=[
            smem,
            block,
            head_block(length_all, COL_K),
            head_block(length_all, COL_V),
            block,
            block,
            block,
            pl.BlockSpec((length_all, 1), lambda i: (0, 0)),
        ],
        out_specs=[block, block, block],
        out_shape=[jax.ShapeDtypeStruct((length_all, HEAD), bf16)] * 3,
        scratch_shapes=[pltpu.VMEM((length_all, HEAD), f32)] * 2,
        compiler_params=pltpu.CompilerParams(vmem_limit_bytes=20 * 1024 * 1024),
        name="attention_backward",
    )(lengths, proj, proj, proj, cosine, sine, upstream, totals)


VMEM_LIMIT = 48 * 1024 * 1024


def input_forward_kernel(left_ref, mask_ref, weight_ref, lower_ref, raise_ref, out_ref, lowered_ref):
    @pl.when(pl.program_id(0) == 0)
    def _():
        lowered_ref[...] = (product(left_ref[...], lower_ref[...]) * mask_ref[...]).astype(bf16)

    out_ref[...] = (
        product(left_ref[...], weight_ref[...]) + product(lowered_ref[...], raise_ref[...])
    ).astype(bf16)


def fixed(shape, *place):
    return pl.BlockSpec(shape, lambda i: place)


def input_forward(left, mask, gathered, raising_all):
    rows, depth = left.shape
    tile = 256
    return pl.pallas_call(
        input_forward_kernel,
        grid=(IN_COLS // tile,),
        in_specs=[
            fixed((rows, depth), 0, 0),
            fixed((rows, ADAPTERS), 0, 0),
            pl.BlockSpec((depth, tile), lambda i: (0, i)),
            fixed((depth, ADAPTERS), 0, IN_COLS // ADAPTERS),
            pl.BlockSpec((ADAPTERS, tile), lambda i: (0, i)),
        ],
        out_specs=[
            pl.BlockSpec((rows, tile), lambda i: (0, i)),
            fixed((rows, ADAPTERS), 0, 0),
        ],
        out_shape=[
            jax.ShapeDtypeStruct((rows, IN_COLS), bf16),
            jax.ShapeDtypeStruct((rows, ADAPTERS), bf16),
        ],
        compiler_params=pltpu.CompilerParams(vmem_limit_bytes=VMEM_LIMIT),
        cost_estimate=pl.CostEstimate(flops=9 * 10**9, bytes_accessed=10**7, transcendentals=0),
        name="input_forward",
    )(left, mask, gathered, gathered, raising_all)


def input_backward_kernel(
    upstream_ref, left_ref, lowered_ref, mask_ref, weight_ref, raise_ref, out_ref, late_ref, scaled
):
    step = pl.program_id(0)

    @pl.when(step == 0)
    def _():
        scaled[...] = (contract_last(upstream_ref[...], raise_ref[...]) * mask_ref[...]).astype(bf16)
        grad_raise = contract_first(lowered_ref[...], upstream_ref[...])
        for shard in range(DP):
            late_ref[shard, 128:] = jnp.concatenate(
                [
                    grad_raise[8 * shard : 8 * shard + 8, 128 * i : 128 * i + 128]
                    for i in range(IN_COLS // 128)
                ]
                + [jnp.zeros((16, 128), f32)],
                axis=0,
            ).astype(bf16)

    out_ref[...] = (
        contract_last(upstream_ref[...], weight_ref[:, :IN_COLS])
        + contract_last(scaled[...], weight_ref[:, IN_COLS : IN_COLS + ADAPTERS])
    ).astype(bf16)
    grad_lower = contract_first(left_ref[...], scaled[...]).astype(bf16)
    late_ref[2 * step, :128] = grad_lower[:128]
    late_ref[2 * step + 1, :128] = grad_lower[128:]


def input_backward(upstream, left, lowered, mask, gathered, raising_all):
    rows, depth = left.shape
    tile = 256
    return pl.pallas_call(
        input_backward_kernel,
        grid=(depth // tile,),
        in_specs=[
            fixed((rows, IN_COLS), 0, 0),
            pl.BlockSpec((rows, tile), lambda i: (0, i)),
            fixed((rows, ADAPTERS), 0, 0),
            fixed((rows, ADAPTERS), 0, 0),
            pl.BlockSpec((tile, gathered.shape[1]), lambda i: (i, 0)),
            fixed((ADAPTERS, IN_COLS), 0, 0),
        ],
        out_specs=[
            pl.BlockSpec((rows, tile), lambda i: (0, i)),
            fixed((DP, 256, 128), 0, 0, 0),
        ],
        out_shape=[
            jax.ShapeDtypeStruct((rows, depth), bf16),
            jax.ShapeDtypeStruct((DP, 256, 128), bf16),
        ],
        scratch_shapes=[pltpu.VMEM((rows, ADAPTERS), bf16)],
        compiler_params=pltpu.CompilerParams(vmem_limit_bytes=VMEM_LIMIT),
        cost_estimate=pl.CostEstimate(flops=10**10, bytes_accessed=10**7, transcendentals=0),
        name="input_backward",
    )(upstream, left, lowered, mask, gathered, raising_all)


def ffn_kernel(
    left_ref,
    cotangent_ref,
    mask_ref,
    gate_ref,
    up_ref,
    lower_ref,
    raise_gate_ref,
    raise_up_ref,
    down_ref,
    lower_down_ref,
    raise_down_ref,
    left_down_ref,
    grad_gate_ref,
    grad_up_ref,
    grad_left_ref,
    lowered_ref,
    scaled_ref,
    scaled_down_ref,
    grad_left,
    grad_lowered,
):
    step = pl.program_id(0)
    model = left_ref.shape[1]

    @pl.when(step == 0)
    def _():
        lowered_ref[...] = (product(left_ref[...], lower_ref[...]) * mask_ref[...]).astype(bf16)
        scaled_down_ref[...] = (
            contract_last(cotangent_ref[...], raise_down_ref[...]) * mask_ref[...]
        ).astype(bf16)
        grad_left[...] = jnp.zeros_like(grad_left)
        grad_lowered[...] = jnp.zeros_like(grad_lowered)

    lowered = lowered_ref[...]
    gate = product(left_ref[...], gate_ref[...]) + product(lowered, raise_gate_ref[...])
    up = product(left_ref[...], up_ref[...]) + product(lowered, raise_up_ref[...])
    shards = range(0, down_ref.shape[0], 128)
    grad_act = contract_last(
        scaled_down_ref[...],
        jnp.concatenate([lower_down_ref[row : row + 64] for row in shards], axis=0),
    )
    for c in range(2):
        grad_act = grad_act + contract_last(
            cotangent_ref[:, c * model // 2 : (c + 1) * model // 2],
            jnp.concatenate([down_ref[row + 64 * c : row + 64 * c + 64] for row in shards], axis=0),
        )
    sigmoid = jax.nn.sigmoid(gate)
    silu = gate * sigmoid
    left_down_ref[...] = (silu * up).astype(bf16)
    grad_up = (grad_act * silu).astype(bf16)
    grad_gate = (grad_act * up * (sigmoid * (1.0 + gate * (1.0 - sigmoid)))).astype(bf16)
    grad_gate_ref[...] = grad_gate
    grad_up_ref[...] = grad_up
    grad_left[...] += contract_last(grad_gate, gate_ref[...]) + contract_last(grad_up, up_ref[...])
    grad_lowered[...] += contract_last(grad_gate, raise_gate_ref[...]) + contract_last(
        grad_up, raise_up_ref[...]
    )

    @pl.when(step == pl.num_programs(0) - 1)
    def _():
        scaled = (grad_lowered[...] * mask_ref[...]).astype(bf16)
        scaled_ref[...] = scaled
        grad_left_ref[...] = (grad_left[...] + contract_last(scaled, lower_ref[...])).astype(bf16)


def ffn_forward_backward(left, cotangent, mask, gathered, gu_raise, down_raise):
    rows, model = left.shape
    tile = 256
    tiles = UNITS // tile
    fold = model // 2
    first = fold // tile
    lower = (fold + 2 * UNITS) // ADAPTERS
    stacked = tile // 64 * 128
    whole_rows = fixed((rows, model), 0, 0)
    adapter_rows = fixed((rows, ADAPTERS), 0, 0)
    return pl.pallas_call(
        ffn_kernel,
        grid=(tiles,),
        in_specs=[
            whole_rows,
            whole_rows,
            adapter_rows,
            pl.BlockSpec((model, tile), lambda i: (0, first + i)),
            pl.BlockSpec((model, tile), lambda i: (0, first + tiles + i)),
            fixed((model, ADAPTERS), 0, lower),
            pl.BlockSpec((ADAPTERS, tile), lambda i: (0, i)),
            pl.BlockSpec((ADAPTERS, tile), lambda i: (0, tiles + i)),
            pl.BlockSpec((stacked, fold), lambda i: (i, 0)),
            pl.BlockSpec((stacked, ADAPTERS), lambda i: (i, lower + 1)),
            fixed((ADAPTERS, model), 0, 0),
        ],
        out_specs=[pl.BlockSpec((rows, tile), lambda i: (0, i))] * 3
        + [whole_rows, adapter_rows, adapter_rows, adapter_rows],
        out_shape=[jax.ShapeDtypeStruct((rows, UNITS), bf16)] * 3
        + [jax.ShapeDtypeStruct((rows, model), bf16)]
        + [jax.ShapeDtypeStruct((rows, ADAPTERS), bf16)] * 3,
        scratch_shapes=[pltpu.VMEM((rows, model), f32), pltpu.VMEM((rows, ADAPTERS), f32)],
        compiler_params=pltpu.CompilerParams(vmem_limit_bytes=VMEM_LIMIT),
        cost_estimate=pl.CostEstimate(flops=12 * 10**9, bytes_accessed=10**7, transcendentals=10**6),
        name="ffn",
    )(
        left,
        cotangent,
        mask,
        gathered,
        gathered,
        gathered,
        gu_raise,
        gu_raise,
        gathered,
        gathered,
        down_raise,
    )


def per_device(
    tokens,
    cotangent,
    seq_lengths,
    adapter_ids,
    norm_gain,
    ffn_gain,
    gate_gain,
    conv_weight,
    conv_bias,
    dt_bias,
    decay_log,
    skip_gain,
    frozen_input_weight,
    input_adapter_lower,
    input_adapter_upper,
    frozen_output_weight,
    output_adapter_lower,
    output_adapter_upper,
    frozen_gate_up_weight,
    gate_up_adapter_lower,
    gate_up_adapter_upper,
    frozen_down_weight,
    down_adapter_lower,
    down_adapter_upper,
):
    s = lax.axis_index("sp")
    d = lax.axis_index("dp")
    y = s // X_PAIR
    x = s % X_PAIR
    tok_count = tokens.shape[0]
    group_len = tok_count * SEQ
    first_len = seq_lengths[0, 0]
    set_ids = adapter_ids[0]

    def adapter_mask(token_index):
        resident = jnp.where(token_index >= first_len, set_ids[1], set_ids[0])
        return jnp.arange(ADAPTERS)[None, :] // ADAPTER_RANK == resident[:, None]

    group_index = jnp.arange(group_len)
    segment = (group_index >= first_len).astype(jnp.int32)
    position = group_index - first_len * segment
    mask_all = adapter_mask(group_index)
    ring_blocks = X_PAIR * ((y + jnp.arange(Y_RING)) % Y_RING) + x
    ring_index = (ring_blocks[:, None] * tok_count + jnp.arange(tok_count)[None, :]).reshape(-1)
    mask_ring = adapter_mask(ring_index)

    def head_columns(values):
        lead = values.shape[:-1]
        grouped = values.reshape(lead + (12, Y_RING, M_HEAD))
        grouped = lax.dynamic_slice_in_dim(grouped, HEADS_DEV * x, HEADS_DEV, len(lead))
        grouped = lax.dynamic_index_in_dim(grouped, y, len(lead) + 1, keepdims=False)
        return grouped.reshape(lead + (INNER,))

    def head_items(values):
        lead = values.shape[:-1]
        grouped = values.reshape(lead + (12, Y_RING))
        grouped = lax.dynamic_slice_in_dim(grouped, HEADS_DEV * x, HEADS_DEV, len(lead))
        return lax.dynamic_index_in_dim(grouped, y, len(lead) + 1, keepdims=False)

    kv_head = s // (H_Q // H_KV)

    def gather_rows(rows):
        return lax.all_gather(rows, "dp", axis=0, tiled=True)

    place = jnp.reshape(s, (1,)).astype(jnp.int32)
    in_all = gather_rows(
        pack(
            pack_input_kernel,
            (place, frozen_input_weight, input_adapter_lower, sixteen_rows(input_adapter_upper)),
            (128, IN_COLS + 2 * ADAPTERS),
        )
    )
    in_raise = raising([in_all[:, IN_COLS + ADAPTERS :]], IN_COLS)

    hidden = tokens.astype(f32)
    normed, norm_back = jax.vjp(partial(rms_scale, scale_gain=norm_gain), hidden)
    normed, frozen_output_weight, frozen_down_weight = lax.optimization_barrier(
        (normed.astype(bf16), frozen_output_weight, frozen_down_weight)
    )
    left_in = gather_rings(normed, y, x)

    out_rows = jnp.concatenate([frozen_output_weight, output_adapter_lower], axis=1)
    piece = lax.dynamic_slice_in_dim(out_rows, 64 * y, 64, 0)
    spread = jnp.zeros_like(piece)
    for k in range(1, Y_RING):
        block = lax.dynamic_slice_in_dim(out_rows, 64 * ((y + k) % Y_RING), 64, 0)
        pairs = [((i // 2) * SEQ + i, ((i // 2 + k) % Y_RING) * SEQ + i) for i in range(SEQ)]
        spread = spread + lax.ppermute(block, ("dp", "sp"), pairs)
    own_rows = (d >= Y_RING) | (d == y)
    model = frozen_output_weight.shape[1]
    out_all = gather_rows(
        pack(
            pack_output_kernel,
            (jnp.where(own_rows, piece, spread), sixteen_rows(output_adapter_upper)),
            (64, model + 3 * ADAPTERS),
        )
    )
    out_weight = out_all[:, : model + ADAPTERS]
    out_raise = raising(
        [out_all[:, model + 128 * c : model + 128 * c + 128] for c in (1, 2)], model
    )

    fold = model // 2
    ffn_all = gather_rows(
        pack(
            pack_ffn_kernel,
            (
                place,
                frozen_gate_up_weight,
                gate_up_adapter_lower,
                sixteen_rows(gate_up_adapter_upper),
                frozen_down_weight,
                down_adapter_lower,
                sixteen_rows(down_adapter_upper),
            ),
            (128, fold + 2 * UNITS + 4 * ADAPTERS),
        )
    )
    edge = fold + 2 * UNITS + 2 * ADAPTERS
    gu_raise = raising([ffn_all[:, edge : edge + ADAPTERS]], 2 * UNITS)
    down_raise = raising([ffn_all[:, edge + ADAPTERS :]], model)

    def masked(lowered, mask):
        return jnp.where(mask, lowered, 0.0).astype(bf16)

    def forward(left, weight, raising, mask):
        both = product(left, weight)
        width = raising.shape[1]
        lowered = masked(both[:, width:], mask)
        return both[:, :width] + product(lowered, raising), lowered

    def backward(left, lowered, upstream, weight, raising, mask):
        gradient_lowered = masked(contract_last(upstream, raising), mask)
        grad_raise = contract_first(lowered, upstream)
        grad_lower = contract_first(left, gradient_lowered)
        grad_left = contract_last(jnp.concatenate([upstream, gradient_lowered], axis=1), weight)
        return grad_left, grad_lower, grad_raise

    projected, lower_in = input_forward(left_in, mask_all.astype(f32), in_all, in_raise)

    projected, cot_own = lax.optimization_barrier((projected, cotangent))
    cot_ring = gather_ring(cot_own)
    taps = jnp.concatenate(
        [
            jnp.concatenate([head_columns(conv_weight[:, :D_SSM]), conv_weight[:, D_SSM:]], axis=1),
            jnp.concatenate([head_columns(conv_bias[:D_SSM]), conv_bias[D_SSM:]])[None],
            jnp.zeros((3, INNER + 2 * STATE), f32),
        ],
        axis=0,
    )
    rate_rows = jnp.pad(
        jnp.stack([head_items(dt_bias), -jnp.exp(head_items(decay_log))]),
        ((0, 6), (0, 128 - HEADS_DEV)),
    )
    skip_rows = jnp.pad(
        jnp.stack([jnp.repeat(head_items(skip_gain), M_HEAD), head_columns(gate_gain)]),
        ((0, 6), (0, 0)),
    )
    gain_pair = lax.dynamic_index_in_dim(
        gate_gain.reshape(12, Y_RING, M_HEAD), y, 1, keepdims=False
    ).reshape(1, -1)
    cosine_table, sine_table = rotary_tables(position)
    gated, scanned, squares, convolved, states = scan_forward(
        seq_lengths, projected, taps, rate_rows, skip_rows
    )
    attended, log_totals = attention_forward(seq_lengths, projected, cosine_table, sine_table)
    squares = sum_ring_small(squares.reshape(SEQ, 8, tok_count)[:, 0])
    inverse = lax.rsqrt((squares + hop(squares, side)) / D_SSM + epsilon)
    mixed, cot_ring = lax.optimization_barrier(
        (jnp.concatenate([attended, gated], axis=1), cot_ring)
    )

    def to_ring(values):
        doubled = jnp.concatenate([values, values], axis=0)
        rolled = lax.dynamic_slice_in_dim(doubled, X_PAIR * tok_count * y, group_len, 0)
        return rolled.reshape(Y_RING, X_PAIR, tok_count, -1)

    def from_ring(values):
        flat = values.reshape(group_len, -1)
        doubled = jnp.concatenate([flat, flat], axis=0)
        start = X_PAIR * tok_count * ((Y_RING - y) % Y_RING)
        return lax.dynamic_slice_in_dim(doubled, start, group_len, 0)

    ring_len = Y_RING * tok_count
    mixed_ring = to_ring(mixed)
    kept = lax.dynamic_index_in_dim(mixed_ring, x, 1, keepdims=False).reshape(ring_len, SLICE)
    other = lax.dynamic_index_in_dim(mixed_ring, 1 - x, 1, keepdims=False).reshape(ring_len, SLICE)
    received = hop(other, side)
    low = jnp.where(x == 0, kept, received)
    high = jnp.where(x == 0, received, kept)
    gated_pair = jnp.concatenate([low[:, HEAD:], high[:, HEAD:]], axis=1).astype(f32)
    inverse_ring = lax.dynamic_index_in_dim(
        to_ring(inverse.reshape(-1, 1)), x, 1, keepdims=False
    ).reshape(ring_len, 1)
    left_out = jnp.concatenate(
        [low[:, :HEAD], high[:, :HEAD], (gated_pair * inverse_ring * gain_pair).astype(bf16)],
        axis=1,
    )
    branch_part, lower_out = forward(left_out, out_weight, out_raise, mask_ring)
    (branch,) = scatter_ring(branch_part)
    residual = hidden + branch
    normed_ffn, ffn_norm_back = jax.vjp(partial(rms_scale, scale_gain=ffn_gain), residual)
    left_gu = gather_ring(normed_ffn.astype(bf16))
    left_down, grad_gate_half, grad_up_half, grad_gu_part, lower_gu, scaled_gu, scaled_down = (
        ffn_forward_backward(
            left_gu, cot_ring, mask_ring.astype(f32), ffn_all, gu_raise, down_raise
        )
    )
    folded = ffn_all[:, :fold].reshape(DP, 2, 64, fold)
    lowers = ffn_all[:, fold + 2 * UNITS + ADAPTERS : edge].reshape(DP, 2, 64, ADAPTERS)
    down_weight = jnp.concatenate(
        [
            folded[:, 0].reshape(UNITS, -1),
            folded[:, 1].reshape(UNITS, -1),
            lowers[:, 0].reshape(UNITS, -1),
        ],
        axis=1,
    )
    ffn_part, lower_down = forward(left_down, down_weight, down_raise, mask_ring)
    grad_a_down = contract_first(left_down, scaled_down)
    grad_b_down = contract_first(lower_down, cot_ring)
    grad_a_gu = contract_first(left_gu, scaled_gu)
    grad_b_gu = contract_first(
        lower_gu, jnp.concatenate([grad_gate_half, grad_up_half], axis=1)
    )
    (grad_left_gu,) = scatter_ring(grad_gu_part)
    (grad_resid_norm,) = ffn_norm_back(grad_left_gu)
    grad_residual = cotangent.astype(f32) + grad_resid_norm
    grad_ring = gather_ring(grad_residual.astype(bf16))
    grad_mixed, grad_a_out, grad_b_out = backward(
        left_out, lower_out, grad_ring, out_weight, out_raise, mask_ring
    )
    early = jnp.concatenate(
        [
            grad_a_out.astype(bf16).reshape(DP, -1, 128),
            blocks_of(grad_b_out.astype(bf16)),
            grad_a_gu.astype(bf16).reshape(DP, -1, 128),
            blocks_of(grad_b_gu.astype(bf16)),
            grad_a_down.astype(bf16).reshape(DP, -1, 128),
            blocks_of(grad_b_down.astype(bf16)),
        ],
        axis=1,
    )
    grad_mixed = grad_mixed.astype(bf16)
    low = jnp.concatenate([grad_mixed[:, :HEAD], grad_mixed[:, 2 * HEAD : 2 * HEAD + INNER]], axis=1)
    high = jnp.concatenate([grad_mixed[:, HEAD : 2 * HEAD], grad_mixed[:, 2 * HEAD + INNER :]], axis=1)
    kept = jnp.where(x == 0, low, high)
    received = hop(jnp.where(x == 0, high, low), side)
    first = jnp.where(x == 0, kept, received).reshape(Y_RING, 1, tok_count, SLICE)
    second = jnp.where(x == 0, received, kept).reshape(Y_RING, 1, tok_count, SLICE)
    head_grads, early, ffn_part = lax.optimization_barrier(
        (from_ring(jnp.concatenate([first, second], axis=1)), early, ffn_part)
    )
    early = exchange_shards(early, d % 2)
    (ffn,) = scatter_ring(ffn_part)
    layer_out = (residual + ffn).astype(bf16)
    slope_ring = jnp.sum(
        grad_mixed[:, 2 * HEAD :].astype(f32) * gain_pair * gated_pair, axis=1
    ).reshape(Y_RING, tok_count)
    slope_own = sum_ring_small(
        lax.dynamic_slice_in_dim(
            jnp.concatenate([slope_ring, slope_ring], axis=0), (Y_RING - y) % Y_RING, Y_RING, 0
        )
    )
    slope_mate = hop(slope_own, side)
    slope = jnp.stack(
        [jnp.where(x == 0, slope_own, slope_mate), jnp.where(x == 0, slope_mate, slope_own)],
        axis=1,
    ).reshape(SEQ, tok_count)
    scales = jnp.stack(
        [inverse.reshape(-1), (inverse * inverse * inverse * slope / D_SSM).reshape(-1)], axis=1
    )
    grad_qkv = attention_backward(
        seq_lengths, projected, cosine_table, sine_table, head_grads[:, :HEAD], log_totals
    )
    grad_projected = scan_backward(
        seq_lengths,
        projected,
        convolved,
        scanned,
        states,
        head_grads[:, HEAD:],
        scales,
        grad_qkv,
        taps,
        rate_rows,
        skip_rows,
    )
    grad_projected, layer_out, early = lax.optimization_barrier((grad_projected, layer_out, early))
    grad_left_part, late = input_backward(
        grad_projected, left_in, lower_in, mask_all.astype(f32), in_all, in_raise
    )
    late = scatter_shards(late, d % 2)
    grad_left = scatter_seq(grad_left_part)
    grad_left, late = lax.optimization_barrier((grad_left, late))
    (grad_hidden_norm,) = norm_back(grad_left)
    grad_tokens = (grad_residual + grad_hidden_norm).astype(bf16)

    a_in_own = late[:128]
    b_in_own = row_from_blocks(late[128:240])
    a_out_block = early[:64].astype(bf16)
    b_out_own = early[64:192]
    a_gu_own = early[192:320]
    b_gu_own = early[320:448]
    a_down_own = early[448:512]
    b_down_own = early[512:640]
    zero_rows = jnp.zeros((256, 128), f32)
    a_out_own = lax.dynamic_update_slice_in_dim(
        zero_rows, jnp.where(own_rows, early[:64], 0.0), 64 * y, 0
    )
    for k in range(1, Y_RING):
        pairs = [(((i // 2 + k) % Y_RING) * SEQ + i, (i // 2) * SEQ + i) for i in range(SEQ)]
        moved = lax.ppermute(a_out_block, ("dp", "sp"), pairs)
        a_out_own = a_out_own + lax.dynamic_update_slice_in_dim(
            zero_rows, moved.astype(f32), 64 * ((y + k) % Y_RING), 0
        )
    a_down_own = lax.dynamic_update_slice_in_dim(zero_rows, a_down_own, 64 * y, 0)
    b_gu_full = lax.dynamic_update_slice_in_dim(
        jnp.zeros((8, 2 * DP, Y_RING, 64), f32),
        row_from_blocks(b_gu_own).reshape(8, 2 * DP, 1, 64),
        y,
        2,
    ).reshape(512, 128)

    def spread_heads(part, width):
        return lax.dynamic_update_slice(
            jnp.zeros((8, 12, Y_RING, width), f32),
            part.reshape(8, HEADS_DEV, 1, width),
            (0, HEADS_DEV * x, y, 0),
        ).reshape(8, -1)

    kv_width = H_KV * HEAD
    b_in_full = jnp.concatenate(
        [
            lax.dynamic_update_slice_in_dim(
                jnp.zeros((8, EDGE_INNER), f32), b_in_own[:, COL_Q:COL_INNER], s * HEAD, 1
            ),
            spread_heads(b_in_own[:, COL_INNER:COL_GATE], M_HEAD),
            lax.dynamic_update_slice_in_dim(
                jnp.zeros((8, kv_width), f32), b_in_own[:, COL_K:COL_V], kv_head * HEAD, 1
            ),
            lax.dynamic_update_slice_in_dim(
                jnp.zeros((8, kv_width), f32), b_in_own[:, COL_V:COL_BC], kv_head * HEAD, 1
            ),
            b_in_own[:, COL_BC:COL_STEP],
            spread_heads(b_in_own[:, COL_GATE:COL_K], M_HEAD),
            spread_heads(b_in_own[:, COL_STEP : COL_STEP + HEADS_DEV], 1),
            jnp.zeros((8, 80), f32),
        ],
        axis=1,
    )
    full = jnp.concatenate(
        [
            a_in_own,
            b_in_full.reshape(-1, 128),
            a_out_own,
            b_out_own,
            a_gu_own,
            b_gu_full,
            a_down_own,
            b_down_own,
        ],
        axis=0,
    )
    full = jnp.pad(full, ((0, (-full.shape[0]) % 128), (0, 0)))
    full = gather_seq(scatter_seq(full).astype(bf16)).astype(f32)
    out_a_in = full[:128]
    out_b_in = full[128:648].reshape(8, -1)[:, : EDGE_STEP + M_HEADS]
    full = full[648:]
    out_a_out = full[:256]
    out_b_out = row_from_blocks(full[256:384])
    out_a_gu = full[384:512]
    out_b_gu = full[512:1024].reshape(8, -1)
    out_a_down = full[1024:1280]
    out_b_down = row_from_blocks(full[1280:1408])
    return (
        layer_out,
        grad_tokens,
        out_a_in,
        out_b_in,
        out_a_out,
        out_b_out,
        out_a_gu,
        out_b_gu,
        out_a_down,
        out_b_down,
    )


def solution(mesh):
    rows = P("dp", None)
    both = P(("dp", "sp"), None)
    in_specs = (both, both) + (rows,) * 2 + (P(),) * 8 + (rows,) * 12
    out_specs = (both, both) + (rows,) * 8
    return jax.shard_map(
        per_device, mesh=mesh, in_specs=in_specs, out_specs=out_specs, check_vma=False
    )
```

```python
from functools import partial

import jax
import jax.numpy as jnp
from jax import lax
from jax.experimental import pallas as pl
from jax.experimental.pallas import tpu as pltpu
from jax.sharding import PartitionSpec as P

H_Q = 8
H_KV = 2
HEAD = 128
M_HEADS = 48
M_HEAD = 64
CONV = 4
ADAPTER_RANK = 16
ADAPTER_SETS = 8
SPAN = 128
STATE = 256
D_SSM = 3072
SHARED = 1024
ADAPTERS = ADAPTER_RANK * ADAPTER_SETS

Y_RING = 4
X_PAIR = 2
SEQ = 8
DP = 16
HEADS_DEV = 6
INNER = HEADS_DEV * M_HEAD
SLICE = HEAD + INNER
MIX = X_PAIR * SLICE
UNITS = 1024

COL_Q = 0
COL_INNER = COL_Q + HEAD
COL_GATE = COL_INNER + INNER
COL_K = COL_GATE + INNER
COL_V = COL_K + HEAD
COL_BC = COL_V + HEAD
COL_STEP = COL_BC + 2 * STATE
IN_COLS = COL_STEP + 128

EDGE_INNER = H_Q * HEAD
EDGE_SHARED = EDGE_INNER + D_SSM
EDGE_GATE = EDGE_SHARED + SHARED
EDGE_STEP = EDGE_GATE + D_SSM

CONVOLVED = INNER + 2 * STATE
VMEM_ALL = 56 * 1024 * 1024

epsilon = 1e-05
rope_base = 100000000000.0
masked_score = -1e30
highest = lax.Precision.HIGHEST
bf16 = jnp.bfloat16
f32 = jnp.float32


def rms_scale(vectors, scale_gain):
    return (
        vectors
        * lax.rsqrt(jnp.mean(vectors * vectors, axis=-1, keepdims=True) + epsilon)
        * scale_gain
    )


def silu_value(vectors):
    return vectors * jax.nn.sigmoid(vectors)


def swiglu(gate_and_up):
    half_width = gate_and_up.shape[1] // 2
    return silu_value(gate_and_up[:, :half_width]) * gate_and_up[:, half_width:]


def rotary_tables(position):
    lanes = jnp.arange(HEAD)
    half_width = HEAD // 2
    frequency = rope_base ** (-((lanes % half_width).astype(f32) * 2.0 / HEAD))
    angle = position.astype(f32)[:, None] * frequency[None, :]
    return jnp.cos(angle), jnp.where(lanes < half_width, -1.0, 1.0) * jnp.sin(angle)


def product(left, right):
    return jnp.dot(left, right, preferred_element_type=f32)


def contract_last(left, right):
    return lax.dot_general(left, right, (((1,), (1,)), ((), ())), preferred_element_type=f32)


def contract_first(left, right):
    return lax.dot_general(left, right, (((0,), (0,)), ((), ())), preferred_element_type=f32)


def hop(value, target):
    return lax.ppermute(value, "sp", [(i, target(i)) for i in range(SEQ)])


def up(i):
    return (i + X_PAIR) % SEQ


def down(i):
    return (i - X_PAIR) % SEQ


def side(i):
    return i ^ 1


def gather_ring(block):
    half = block.shape[0] // 2
    below = hop(block, up)
    above = hop(block, down)
    far_first = hop(below[:half], up)
    far_second = hop(above[half:], down)
    return jnp.concatenate([block, above, far_first, far_second, below], axis=0)


def scatter_ring(partial_rows, *after):
    n = partial_rows.shape[0] // Y_RING
    half = n // 2
    far = partial_rows[2 * n : 3 * n].astype(bf16)
    from_below = hop(far[:half], up)
    from_above = hop(far[half:], down)
    from_below, from_above, *after = lax.optimization_barrier((from_below, from_above, *after))
    partial_rows = partial_rows.astype(f32)
    to_up = partial_rows[n : 2 * n]
    to_up = jnp.concatenate([to_up[:half] + from_below.astype(f32), to_up[half:]], axis=0)
    to_down = partial_rows[3 * n :]
    to_down = jnp.concatenate([to_down[:half], to_down[half:] + from_above.astype(f32)], axis=0)
    low = hop(to_up.astype(bf16), up).astype(f32)
    high = hop(to_down.astype(bf16), down).astype(f32)
    return partial_rows[:n] + low + high, *after


def halved(stack, own, axis, target):
    kept = lax.dynamic_index_in_dim(stack, own, axis, keepdims=False)
    sent = lax.dynamic_index_in_dim(stack, 1 - own, axis, keepdims=False)
    received = lax.ppermute(sent, "dp", [(i, target(i)) for i in range(DP)])
    return (kept.astype(f32) + received.astype(f32)).astype(bf16)


def halve_cores(stack, d):
    return halved(stack.reshape(8, 2, -1, 128), d % 2, 1, lambda i: i ^ 1)


def halve_neighbours(stack, d):
    return halved(stack.reshape(2, 4, -1, 128), d // 8, 0, lambda i: (i + 8) % DP)


CHIPS = [[2 * i + c for i in range(DP // 2)] for c in range(2)]
Z_RINGS = [[8 * n + 2 * z + c for z in range(4)] for n in range(2) for c in range(2)]


def scatter_shards(stack, groups):
    return lax.psum_scatter(
        stack.reshape(-1, 128), "dp", scatter_dimension=0, axis_index_groups=groups, tiled=True
    ).astype(f32)


def gather_seq(block):
    copies = jnp.broadcast_to(block[None], (SEQ,) + block.shape)
    return lax.all_to_all(copies, "sp", split_axis=0, concat_axis=0).reshape(
        (SEQ * block.shape[0],) + block.shape[1:]
    )


def exchange_seq(partial_rows):
    pieces = partial_rows.astype(bf16).reshape((SEQ, -1) + partial_rows.shape[1:])
    return lax.all_to_all(pieces, "sp", split_axis=0, concat_axis=0)


def scatter_seq(partial_rows):
    return jnp.sum(exchange_seq(partial_rows).astype(f32), axis=0)


def gather_rings(block, y, x):
    n = block.shape[0]
    half = n // 2
    mate = hop(block, side)
    above = hop(block, down)
    below = hop(block, up)
    mate_above = hop(mate, down)
    mate_below = hop(mate, up)
    out = jnp.zeros((SEQ * n,) + block.shape[1:], block.dtype)
    for rows, distance, column, shift in (
        (block, 0, x, 0),
        (above, 1, x, 0),
        (below, 3, x, 0),
        (mate, 0, 1 - x, 0),
        (hop(below[:half], up), 2, x, 0),
        (hop(above[half:], down), 2, x, half),
        (mate_above, 1, 1 - x, 0),
        (mate_below, 3, 1 - x, 0),
        (hop(mate_below[:half], up), 2, 1 - x, 0),
        (hop(mate_above[half:], down), 2, 1 - x, half),
    ):
        start = n * (X_PAIR * ((y + distance) % Y_RING) + column) + shift
        out = lax.dynamic_update_slice_in_dim(out, rows, start, 0)
    return out


def sum_ring_small(value):
    total = value
    for offset in range(X_PAIR, SEQ, X_PAIR):
        total = total + hop(value, lambda i, offset=offset: (i + offset) % SEQ)
    return total


def blocks_of(matrix):
    n = matrix.shape[1] // 128
    return matrix.reshape(DP, 8, n, 128).transpose(0, 2, 1, 3).reshape(DP, 8 * n, 128)


def row_from_blocks(stacked):
    n = stacked.shape[0] // 8
    return stacked.reshape(n, 8, 128).transpose(1, 0, 2).reshape(8, 128 * n)


def sixteen_rows(rows):
    return jnp.pad(rows, ((0, 16 - rows.shape[0]), (0, 0)))


def pick_columns(block, y):
    rows = lax.broadcasted_iota(jnp.int32, (512, 128), 0)
    lanes = lax.broadcasted_iota(jnp.int32, (512, 128), 1)
    wanted = jnp.where(lanes < M_HEAD, lanes, lanes + 256 - M_HEAD) + M_HEAD * y
    return product(block, (rows == wanted).astype(bf16))


def pack_input_kernel(place_ref, weight_ref, lower_ref, upper_ref, out_ref):
    s = place_ref[0]
    y = s // X_PAIR
    x = s % X_PAIR
    kv_head = s // (H_Q // H_KV)

    def at(column):
        return pl.ds(pl.multiple_of(column, 128), 128)

    def share(ref):
        def heads(edge):
            return [
                pick_columns(
                    ref[:, pl.ds(pl.multiple_of(edge + 256 * (HEADS_DEV * x + 2 * pair), 128), 512)], y
                )
                for pair in range(HEADS_DEV // 2)
            ]

        step_rows = lax.broadcasted_iota(jnp.int32, (M_HEADS, 128), 0)
        step_lanes = lax.broadcasted_iota(jnp.int32, (M_HEADS, 128), 1)
        picked = (step_rows == Y_RING * (HEADS_DEV * x + step_lanes) + y) & (step_lanes < HEADS_DEV)
        return (
            [ref[:, at(HEAD * s)].astype(f32)]
            + heads(EDGE_INNER)
            + heads(EDGE_GATE)
            + [
                ref[:, at(EDGE_SHARED + HEAD * kv_head)].astype(f32),
                ref[:, at(EDGE_SHARED + HEAD * (H_KV + kv_head))].astype(f32),
            ]
            + [
                ref[:, EDGE_SHARED + 2 * H_KV * HEAD + 128 * i : EDGE_SHARED + 2 * H_KV * HEAD + 128 * i + 128].astype(f32)
                for i in range(2 * STATE // 128)
            ]
            + [product(ref[:, EDGE_STEP:], picked.astype(bf16))]
        )

    for i, piece in enumerate(share(weight_ref)):
        out_ref[:, 128 * i : 128 * i + 128] = piece.astype(bf16)
    out_ref[:, IN_COLS : IN_COLS + ADAPTERS] = lower_ref[...]
    upper = [piece[:8] for piece in share(upper_ref)]
    upper.append(jnp.zeros((128 - 8 * len(upper), 128), f32))
    out_ref[:, IN_COLS + ADAPTERS :] = jnp.concatenate(upper, axis=0).astype(bf16)


def pack_ffn_kernel(
    place_ref, gu_ref, gu_lower_ref, gu_upper_ref, down_ref, down_lower_ref, down_upper_ref, out_ref
):
    y = place_ref[0] // X_PAIR
    fold = down_ref.shape[1] // 2
    rows = pl.ds(pl.multiple_of(64 * y, 64), 64)
    out_ref[:64, :fold] = down_ref[rows, :fold]
    out_ref[64:, :fold] = down_ref[rows, fold:]
    pairs = 2 * UNITS // 128
    for i in range(pairs):
        out_ref[:, fold + 128 * i : fold + 128 * i + 128] = pick_columns(
            gu_ref[:, 512 * i : 512 * i + 512], y
        ).astype(bf16)
    edge = fold + 2 * UNITS
    out_ref[:, edge : edge + 128] = gu_lower_ref[...]
    edge += 128
    out_ref[:64, edge : edge + 128] = down_lower_ref[rows, :]
    out_ref[64:, edge : edge + 128] = jnp.zeros((64, 128), bf16)
    edge += 128
    out_ref[:, edge : edge + 128] = jnp.concatenate(
        [pick_columns(gu_upper_ref[:, 512 * i : 512 * i + 512], y)[:8] for i in range(pairs)], axis=0
    ).astype(bf16)
    edge += 128
    out_ref[:, edge:] = jnp.concatenate(
        [down_upper_ref[:, 128 * i : 128 * i + 128].astype(f32)[:8] for i in range(2 * fold // 128)],
        axis=0,
    ).astype(bf16)


def fold_upper(upper_ref, out_ref, column):
    for c in range(2):
        out_ref[:, column + 128 * c : column + 128 * c + 128] = jnp.concatenate(
            [
                upper_ref[:, 1024 * c + 128 * i : 1024 * c + 128 * i + 128].astype(f32)[:8]
                for i in range(8)
            ],
            axis=0,
        ).astype(bf16)


def pack_output_kernel(rows_ref, upper_ref, out_ref):
    width = rows_ref.shape[1]
    out_ref[:, :width] = rows_ref[...]
    fold_upper(upper_ref, out_ref, width)


def raising_kernel(*refs):
    out_ref = refs[-1]
    column = 0
    for ref in refs[:-1]:
        stacked = ref[...].astype(f32)
        depth = stacked.shape[0] // DP
        for block in range(min(depth // 8, out_ref.shape[1] // 128)):
            out_ref[:, column : column + 128] = jnp.concatenate(
                [
                    stacked[depth * shard + 8 * block : depth * shard + 8 * block + 8]
                    for shard in range(DP)
                ],
                axis=0,
            ).astype(bf16)
            column += 128


def raising(stacks, width):
    return pl.pallas_call(
        raising_kernel,
        in_specs=[pl.BlockSpec(memory_space=pltpu.VMEM)] * len(stacks),
        out_specs=pl.BlockSpec(memory_space=pltpu.VMEM),
        out_shape=jax.ShapeDtypeStruct((ADAPTERS, width), bf16),
        compiler_params=pltpu.CompilerParams(vmem_limit_bytes=32 * 1024 * 1024),
    )(*stacks)


def pack(kernel, arrays, shape):
    return pl.pallas_call(
        kernel,
        in_specs=[
            pl.BlockSpec(memory_space=pltpu.SMEM if a.ndim == 1 else pltpu.VMEM) for a in arrays
        ],
        out_specs=pl.BlockSpec(memory_space=pltpu.VMEM),
        out_shape=jax.ShapeDtypeStruct(shape, bf16),
        compiler_params=pltpu.CompilerParams(vmem_limit_bytes=32 * 1024 * 1024),
    )(*arrays)


def lane_index(shape):
    return lax.broadcasted_iota(jnp.int32, shape, 1)


def row_index(shape):
    return lax.broadcasted_iota(jnp.int32, shape, 0)


def over_heads(per_head):
    rows = per_head.shape[0]
    low = lane_index((rows, 128)) < M_HEAD
    return jnp.concatenate(
        [
            jnp.where(low, per_head[:, 2 * pair : 2 * pair + 1], per_head[:, 2 * pair + 1 : 2 * pair + 2])
            for pair in range(HEADS_DEV // 2)
        ],
        axis=1,
    )


def head_sums(values):
    member = (row_index((INNER, 128)) // M_HEAD == lane_index((INNER, 128))).astype(bf16)
    coarse = values.astype(bf16)
    fine = (values - coarse.astype(f32)).astype(bf16)
    return product(coarse, member) + product(fine, member)


def span_terms(convolved, step_block, rate_rows, first_len, start):
    shifted = step_block + rate_rows[0:1]
    rates = jnp.log1p(jnp.exp(-jnp.abs(shifted))) + jnp.maximum(shifted, 0.0)
    log_decay = rates * rate_rows[1:2]
    rows = row_index((SPAN, SPAN))
    lanes = lane_index((SPAN, SPAN))
    below = rows >= lanes
    cumulative = jnp.dot(
        below.astype(f32), log_decay, precision=highest, preferred_element_type=f32
    )
    seg_rows = (rows + start >= first_len).astype(jnp.int32)
    seg_lanes = (lanes + start >= first_len).astype(jnp.int32)
    allowed = below & (seg_rows == seg_lanes)
    last_seg = (start + SPAN - 1 >= first_len).astype(jnp.int32)
    previous = (start - 1 >= first_len).astype(jnp.int32)
    total = cumulative[SPAN - 1 : SPAN]
    entry = jnp.where(seg_rows == previous, jnp.exp(cumulative), 0.0)
    tail = jnp.where(seg_rows == last_seg, jnp.exp(total - cumulative), 0.0)
    keep = jnp.where(last_seg == previous, jnp.exp(total), 0.0)
    activated = convolved * jax.nn.sigmoid(convolved)
    x_in = activated[:, :INNER]
    in_state = activated[:, INNER : INNER + STATE]
    out_state = activated[:, INNER + STATE :]
    return shifted, rates, cumulative, allowed, entry, tail, keep, x_in, in_state, out_state


def decay_of(cumulative, across, allowed, head):
    gap = cumulative[:, head : head + 1] - across[head : head + 1]
    return jnp.exp(jnp.where(allowed, gap, masked_score))


def scan_forward_kernel(
    lengths_ref,
    proj_ref,
    taps_ref,
    rate_rows_ref,
    skip_ref,
    gated_ref,
    scanned_ref,
    squares_ref,
    convolved_ref,
    states_ref,
    state,
    last_rows,
):
    step = pl.program_id(0)
    start = step * SPAN
    first_len = lengths_ref[0, 0]

    @pl.when(step == 0)
    def _():
        state[...] = jnp.zeros_like(state)
        last_rows[...] = jnp.zeros_like(last_rows)

    signal = jnp.concatenate(
        [proj_ref[:, COL_INNER:COL_GATE], proj_ref[:, COL_BC:COL_STEP]], axis=1
    ).astype(f32)
    row = start + row_index((SPAN, 1))
    position = row - jnp.where(row >= first_len, first_len, 0)
    convolved = taps_ref[4:5] + taps_ref[3:4] * signal
    before = last_rows[...]
    top = row_index((8, 1))
    for offset in range(1, CONV):
        moved = pltpu.roll(signal, offset, 0)
        edge = jnp.where(top < offset, pltpu.roll(before, offset, 0), moved[:8])
        moved = jnp.concatenate([edge, moved[8:]], axis=0)
        convolved = convolved + taps_ref[3 - offset : 4 - offset] * jnp.where(
            position >= offset, moved, 0.0
        )
    last_rows[...] = signal[SPAN - 8 :]
    convolved_ref[...] = convolved
    step_block = proj_ref[:, COL_STEP:].astype(f32)
    _, rates, cumulative, allowed, entry, tail, keep, x_in, in_state, out_state = span_terms(
        convolved, step_block, rate_rows_ref[...], first_len, start
    )
    across = cumulative.T
    in_half = in_state.astype(bf16)
    out_half = out_state.astype(bf16)
    state_now = state[...]
    state_half = state_now.astype(bf16)
    states_ref[0] = state_half
    mixing = contract_last(out_half, in_half)
    rates_wide = over_heads(rates)
    weighted = (x_in * rates_wide).astype(bf16)
    low = lane_index((SPAN, 128)) < M_HEAD
    within = []
    for pair in range(HEADS_DEV // 2):
        block = weighted[:, 128 * pair : 128 * pair + 128]
        sides = [
            product(
                (mixing * decay_of(cumulative, across, allowed, 2 * pair + i)).astype(bf16), block
            )
            for i in range(2)
        ]
        within.append(jnp.where(low, sides[0], sides[1]))
    result = (
        jnp.concatenate(within, axis=1)
        + product(out_half, state_half) * over_heads(entry)
        + skip_ref[0:1] * x_in
    )
    scanned = result.astype(bf16)
    scanned_ref[...] = scanned
    gate = proj_ref[:, COL_GATE:COL_K].astype(f32)
    gated = scanned.astype(f32) * (gate * jax.nn.sigmoid(gate))
    gated_ref[...] = gated.astype(bf16)
    squares_ref[...] = lax.dot_general(
        jnp.ones((8, INNER), f32),
        gated * gated,
        (((1,), (1,)), ((), ())),
        precision=highest,
        preferred_element_type=f32,
    )
    state[...] = state_now * over_heads(keep) + contract_first(
        in_half, (x_in * over_heads(tail * rates)).astype(bf16)
    )


def scan_backward_kernel(
    lengths_ref,
    proj_ref,
    convolved_ref,
    scanned_ref,
    states_ref,
    upstream_ref,
    scales_ref,
    grad_query_ref,
    grad_key_ref,
    grad_value_ref,
    taps_ref,
    rate_rows_ref,
    skip_ref,
    out_ref,
    grad_state,
    next_rows,
):
    step = pl.num_programs(0) - 1 - pl.program_id(0)
    start = step * SPAN
    first_len = lengths_ref[0, 0]

    @pl.when(pl.program_id(0) == 0)
    def _():
        grad_state[...] = jnp.zeros_like(grad_state)
        next_rows[...] = jnp.zeros_like(next_rows)

    convolved = convolved_ref[...]
    step_block = proj_ref[:, COL_STEP:].astype(f32)
    rate_rows = rate_rows_ref[...]
    shifted, rates, cumulative, allowed, entry, tail, keep, x_in, in_state, out_state = span_terms(
        convolved, step_block, rate_rows, first_len, start
    )
    across = cumulative.T
    in_half = in_state.astype(bf16)
    out_half = out_state.astype(bf16)
    state_half = states_ref[0]

    gate = proj_ref[:, COL_GATE:COL_K].astype(f32)
    gate_sigmoid = jax.nn.sigmoid(gate)
    gate_silu = gate * gate_sigmoid
    scanned = scanned_ref[...].astype(f32)
    upstream = upstream_ref[:, HEAD:].astype(f32) * skip_ref[1:2]
    grad_gated = scales_ref[:, 0:1] * upstream - scales_ref[:, 1:2] * (scanned * gate_silu)
    out_ref[:, COL_GATE:COL_K] = (
        grad_gated * scanned * (gate_sigmoid * (1.0 + gate * (1.0 - gate_sigmoid)))
    ).astype(bf16)
    grad_half = (grad_gated * gate_silu).astype(bf16)
    grad_result = grad_half.astype(f32)

    mixing = contract_last(out_half, in_half)
    rates_wide = over_heads(rates)
    entry_wide = over_heads(entry)
    tail_wide = over_heads(tail)
    keep_wide = over_heads(keep)
    weighted = (x_in * rates_wide).astype(bf16)
    lane = lane_index((SPAN, 128))
    low = lane < M_HEAD
    grad_mixing = jnp.zeros((SPAN, SPAN), f32)
    grad_cumulative = jnp.zeros((SPAN, 128), f32)
    grad_across = jnp.zeros((SPAN, 128), f32)
    head_row = row_index((SPAN, 128))
    grad_weighted = []
    for pair in range(HEADS_DEV // 2):
        block = weighted[:, 128 * pair : 128 * pair + 128]
        grad_block = grad_half[:, 128 * pair : 128 * pair + 128]
        sides = []
        for i in range(2):
            head = 2 * pair + i
            decay = decay_of(cumulative, across, allowed, head)
            spread = mixing * decay
            sides.append(contract_first(spread.astype(bf16), grad_block))
            mine = low if i == 0 else jnp.logical_not(low)
            grad_spread = contract_last(jnp.where(mine, grad_block, jnp.zeros_like(grad_block)), block)
            grad_mixing = grad_mixing + grad_spread * decay
            grad_gap = grad_spread * spread
            grad_cumulative = jnp.where(
                lane == head, jnp.sum(grad_gap, axis=1, keepdims=True), grad_cumulative
            )
            grad_across = jnp.where(
                head_row == head, jnp.sum(grad_gap, axis=0, keepdims=True), grad_across
            )
        grad_weighted.append(jnp.where(low, sides[0], sides[1]))
    grad_weighted = jnp.concatenate(grad_weighted, axis=1)
    grad_cumulative = grad_cumulative - grad_across.T

    grad_next = grad_state[...]
    grad_next_half = grad_next.astype(bf16)
    grad_entered = (grad_result * entry_wide).astype(bf16)
    from_state = product(out_half, state_half)
    to_state = product(in_half, grad_next_half)
    tail_rates = tail_wide * rates_wide
    grad_mixing_half = grad_mixing.astype(bf16)
    grad_out_state = product(grad_mixing_half, in_half) + contract_last(grad_entered, state_half)
    grad_in_state = contract_first(grad_mixing_half, out_half) + contract_last(
        (x_in * tail_rates).astype(bf16), grad_next_half
    )
    sums = head_sums(
        jnp.concatenate(
            [
                grad_result * from_state,
                to_state * x_in,
                grad_weighted * x_in,
                jnp.broadcast_to(
                    jnp.sum(grad_next * state_half.astype(f32), axis=0, keepdims=True), (8, INNER)
                ),
            ],
            axis=0,
        )
    )
    grad_entry = sums[:SPAN]
    grad_tail = sums[SPAN : 2 * SPAN]
    grad_rates = sums[2 * SPAN : 3 * SPAN] + grad_tail * tail
    from_tail = grad_tail * tail * rates
    grad_total = (
        jnp.sum(from_tail, axis=0, keepdims=True) + sums[3 * SPAN : 3 * SPAN + 1] * keep
    )
    grad_cumulative = grad_cumulative + grad_entry * entry - from_tail
    grad_cumulative = grad_cumulative + jnp.where(head_row == SPAN - 1, grad_total, 0.0)
    above = (row_index((SPAN, SPAN)) <= lane_index((SPAN, SPAN))).astype(f32)
    grad_decay = jnp.dot(above, grad_cumulative, precision=highest, preferred_element_type=f32)
    grad_rates = grad_rates + grad_decay * rate_rows[1:2]
    out_ref[:, COL_STEP:] = jnp.where(
        lane < HEADS_DEV, grad_rates * jax.nn.sigmoid(shifted), 0.0
    ).astype(bf16)
    grad_x = grad_weighted * rates_wide + to_state * tail_rates + skip_ref[0:1] * grad_result
    grad_state[...] = grad_next * keep_wide + contract_first(out_half, grad_entered)

    conv_sigmoid = jax.nn.sigmoid(convolved)
    grad_conv = jnp.concatenate([grad_x, grad_in_state, grad_out_state], axis=1) * (
        conv_sigmoid * (1.0 + convolved * (1.0 - conv_sigmoid))
    )
    row = start + row_index((SPAN, 1))
    position = row - jnp.where(row >= first_len, first_len, 0)
    later_row = start + SPAN + row_index((8, 1))
    later_position = later_row - jnp.where(later_row >= first_len, first_len, 0)
    later = next_rows[...]
    bottom = row_index((8, 1))
    grad_signal = taps_ref[3:4] * grad_conv
    for offset in range(1, CONV):
        moved = pltpu.roll(jnp.where(position >= offset, grad_conv, 0.0), SPAN - offset, 0)
        edge = pltpu.roll(jnp.where(later_position >= offset, later, 0.0), 8 - offset, 0)
        edge = jnp.where(bottom >= 8 - offset, edge, moved[SPAN - 8 :])
        moved = jnp.concatenate([moved[: SPAN - 8], edge], axis=0)
        grad_signal = grad_signal + taps_ref[3 - offset : 4 - offset] * moved
    next_rows[...] = grad_conv[:8]
    out_ref[:, COL_INNER:COL_GATE] = grad_signal[:, :INNER].astype(bf16)
    out_ref[:, COL_BC:COL_STEP] = grad_signal[:, INNER:].astype(bf16)
    out_ref[:, :COL_INNER] = grad_query_ref[...]
    out_ref[:, COL_K:COL_V] = grad_key_ref[...]
    out_ref[:, COL_V:COL_BC] = grad_value_ref[...]


def whole(shape):
    return pl.BlockSpec(shape, lambda i: (0,) * len(shape))


smem = pl.BlockSpec(memory_space=pltpu.SMEM)


def scan_forward(lengths, proj, taps, rate_rows, skip_rows):
    length_all = proj.shape[0]
    spans = length_all // SPAN

    def rows(width):
        return pl.BlockSpec((SPAN, width), lambda i: (i, 0))

    return pl.pallas_call(
        scan_forward_kernel,
        grid=(spans,),
        in_specs=[smem, rows(IN_COLS), whole(taps.shape), whole(rate_rows.shape), whole(skip_rows.shape)],
        out_specs=[
            rows(INNER),
            rows(INNER),
            pl.BlockSpec((8, SPAN), lambda i: (i, 0)),
            rows(CONVOLVED),
            pl.BlockSpec((1, STATE, INNER), lambda i: (i, 0, 0)),
        ],
        out_shape=[
            jax.ShapeDtypeStruct((length_all, INNER), bf16),
            jax.ShapeDtypeStruct((length_all, INNER), bf16),
            jax.ShapeDtypeStruct((8 * spans, SPAN), f32),
            jax.ShapeDtypeStruct((length_all, CONVOLVED), f32),
            jax.ShapeDtypeStruct((spans, STATE, INNER), bf16),
        ],
        scratch_shapes=[pltpu.VMEM((STATE, INNER), f32), pltpu.VMEM((8, CONVOLVED), f32)],
        compiler_params=pltpu.CompilerParams(vmem_limit_bytes=VMEM_ALL),
        cost_estimate=pl.CostEstimate(flops=10**10, bytes_accessed=10**7, transcendentals=10**6),
        name="scan_forward",
    )(lengths, proj, taps, rate_rows, skip_rows)


def scan_backward(
    lengths, proj, convolved, scanned, states, upstream, scales, grad_qkv, taps, rate_rows, skip_rows
):
    length_all = proj.shape[0]
    spans = length_all // SPAN

    def rows(width):
        return pl.BlockSpec((SPAN, width), lambda i: (spans - 1 - i, 0))

    return pl.pallas_call(
        scan_backward_kernel,
        grid=(spans,),
        in_specs=[
            smem,
            rows(IN_COLS),
            rows(CONVOLVED),
            rows(INNER),
            pl.BlockSpec((1, STATE, INNER), lambda i: (spans - 1 - i, 0, 0)),
            rows(HEAD + INNER),
            rows(2),
            rows(HEAD),
            rows(HEAD),
            rows(HEAD),
            whole(taps.shape),
            whole(rate_rows.shape),
            whole(skip_rows.shape),
        ],
        out_specs=rows(IN_COLS),
        out_shape=jax.ShapeDtypeStruct((length_all, IN_COLS), bf16),
        scratch_shapes=[pltpu.VMEM((STATE, INNER), f32), pltpu.VMEM((8, CONVOLVED), f32)],
        compiler_params=pltpu.CompilerParams(vmem_limit_bytes=VMEM_ALL),
        cost_estimate=pl.CostEstimate(flops=17 * 10**9, bytes_accessed=10**7, transcendentals=10**6),
        name="scan_backward",
    )(lengths, proj, convolved, scanned, states, upstream, scales, *grad_qkv, taps, rate_rows, skip_rows)


QUERY_ROWS = 256
score_scale = HEAD ** (-0.5)


def turn(values, cosine, sine):
    return values * cosine + pltpu.roll(values, HEAD // 2, 1) * sine


def allowed_scores(query_rot, key_rot, first_row, first_len):
    scores = contract_last(query_rot, key_rot) * score_scale
    rows = first_row + row_index(scores.shape)
    lanes = lane_index(scores.shape)
    allowed = (lanes <= rows) & ((lanes >= first_len) | (rows < first_len))
    return jnp.where(allowed, scores, masked_score)


def attention_forward_kernel(
    lengths_ref, query_ref, key_ref, value_ref, cosine_ref, sine_ref, out_ref, totals_ref
):
    first_len = lengths_ref[0, 0]
    length_all = query_ref.shape[0]
    key_rot = turn(key_ref[...].astype(f32), cosine_ref[...], sine_ref[...]).astype(bf16)
    for first in range(0, length_all, QUERY_ROWS):
        block = slice(first, first + QUERY_ROWS)
        seen = first + QUERY_ROWS
        query_rot = turn(
            query_ref[block].astype(f32), cosine_ref[block], sine_ref[block]
        ).astype(bf16)
        scores = allowed_scores(query_rot, key_rot[:seen], first, first_len)
        peak = jnp.max(scores, axis=1, keepdims=True)
        exponent = jnp.exp(scores - peak)
        total = jnp.sum(exponent, axis=1, keepdims=True)
        probs = (exponent * (1.0 / total)).astype(bf16)
        out_ref[block] = product(probs, value_ref[:seen]).astype(bf16)
        totals_ref[block] = peak + jnp.log(total)


def attention_backward_kernel(
    lengths_ref,
    query_ref,
    key_ref,
    value_ref,
    cosine_ref,
    sine_ref,
    upstream_ref,
    totals_ref,
    grad_query_ref,
    grad_key_ref,
    grad_value_ref,
    key_sum,
    value_sum,
):
    first_len = lengths_ref[0, 0]
    length_all = query_ref.shape[0]
    key_rot = turn(key_ref[...].astype(f32), cosine_ref[...], sine_ref[...]).astype(bf16)
    key_sum[...] = jnp.zeros_like(key_sum)
    value_sum[...] = jnp.zeros_like(value_sum)
    for first in range(0, length_all, QUERY_ROWS):
        block = slice(first, first + QUERY_ROWS)
        seen = first + QUERY_ROWS
        cosine = cosine_ref[block]
        sine = sine_ref[block]
        query_rot = turn(query_ref[block].astype(f32), cosine, sine).astype(bf16)
        probs = jnp.exp(
            allowed_scores(query_rot, key_rot[:seen], first, first_len) - totals_ref[block]
        )
        upstream = upstream_ref[block]
        grad_probs = contract_last(upstream, value_ref[:seen])
        delta = jnp.sum(probs * grad_probs, axis=1, keepdims=True)
        grad_scores = (probs * (grad_probs - delta)).astype(bf16)
        grad_query_ref[block] = turn(
            product(grad_scores, key_rot[:seen]) * score_scale, cosine, -sine
        ).astype(bf16)
        key_sum[:seen] += contract_first(grad_scores, query_rot)
        value_sum[:seen] += contract_first(probs.astype(bf16), upstream)
    grad_key_ref[...] = turn(
        key_sum[...] * score_scale, cosine_ref[...], -sine_ref[...]
    ).astype(bf16)
    grad_value_ref[...] = value_sum[...].astype(bf16)


def head_block(length_all, column):
    return pl.BlockSpec((length_all, HEAD), lambda i: (0, column // HEAD))


def attention_forward(lengths, proj, cosine, sine):
    length_all = proj.shape[0]
    block = head_block(length_all, 0)
    return pl.pallas_call(
        attention_forward_kernel,
        grid=(1,),
        in_specs=[
            smem,
            block,
            head_block(length_all, COL_K),
            head_block(length_all, COL_V),
            block,
            block,
        ],
        out_specs=[block, pl.BlockSpec((length_all, 1), lambda i: (0, 0))],
        out_shape=[
            jax.ShapeDtypeStruct((length_all, HEAD), bf16),
            jax.ShapeDtypeStruct((length_all, 1), f32),
        ],
        compiler_params=pltpu.CompilerParams(vmem_limit_bytes=VMEM_ALL),
        name="attention_forward",
    )(lengths, proj, proj, proj, cosine, sine)


def attention_backward(lengths, proj, cosine, sine, upstream, totals):
    length_all = proj.shape[0]
    block = head_block(length_all, 0)
    return pl.pallas_call(
        attention_backward_kernel,
        grid=(1,),
        in_specs=[
            smem,
            block,
            head_block(length_all, COL_K),
            head_block(length_all, COL_V),
            block,
            block,
            block,
            pl.BlockSpec((length_all, 1), lambda i: (0, 0)),
        ],
        out_specs=[block, block, block],
        out_shape=[jax.ShapeDtypeStruct((length_all, HEAD), bf16)] * 3,
        scratch_shapes=[pltpu.VMEM((length_all, HEAD), f32)] * 2,
        compiler_params=pltpu.CompilerParams(vmem_limit_bytes=VMEM_ALL),
        name="attention_backward",
    )(lengths, proj, proj, proj, cosine, sine, upstream, totals)


VMEM_LIMIT = 48 * 1024 * 1024


def input_forward_kernel(left_ref, mask_ref, weight_ref, lower_ref, raise_ref, out_ref, lowered_ref):
    @pl.when(pl.program_id(0) == 0)
    def _():
        lowered_ref[...] = (product(left_ref[...], lower_ref[...]) * mask_ref[...]).astype(bf16)

    out_ref[...] = (
        product(left_ref[...], weight_ref[...]) + product(lowered_ref[...], raise_ref[...])
    ).astype(bf16)


def fixed(shape, *place):
    return pl.BlockSpec(shape, lambda i: place)


def input_forward(left, mask, gathered, raising_all):
    rows, depth = left.shape
    tile = 256
    return pl.pallas_call(
        input_forward_kernel,
        grid=(IN_COLS // tile,),
        in_specs=[
            fixed((rows, depth), 0, 0),
            fixed((rows, ADAPTERS), 0, 0),
            pl.BlockSpec((depth, tile), lambda i: (0, i)),
            fixed((depth, ADAPTERS), 0, IN_COLS // ADAPTERS),
            pl.BlockSpec((ADAPTERS, tile), lambda i: (0, i)),
        ],
        out_specs=[
            pl.BlockSpec((rows, tile), lambda i: (0, i)),
            fixed((rows, ADAPTERS), 0, 0),
        ],
        out_shape=[
            jax.ShapeDtypeStruct((rows, IN_COLS), bf16),
            jax.ShapeDtypeStruct((rows, ADAPTERS), bf16),
        ],
        compiler_params=pltpu.CompilerParams(vmem_limit_bytes=VMEM_ALL),
        cost_estimate=pl.CostEstimate(flops=9 * 10**9, bytes_accessed=10**7, transcendentals=0),
        name="input_forward",
    )(left, mask, gathered, gathered, raising_all)


def input_backward_kernel(
    upstream_ref, left_ref, lowered_ref, mask_ref, weight_ref, raise_ref, out_ref, late_ref, scaled
):
    step = pl.program_id(0)

    @pl.when(step == 0)
    def _():
        scaled[...] = (contract_last(upstream_ref[...], raise_ref[...]) * mask_ref[...]).astype(bf16)
        grad_raise = contract_first(lowered_ref[...], upstream_ref[...])
        for shard in range(DP):
            late_ref[shard, 128:] = jnp.concatenate(
                [
                    grad_raise[8 * shard : 8 * shard + 8, 128 * i : 128 * i + 128]
                    for i in range(IN_COLS // 128)
                ]
                + [jnp.zeros((16, 128), f32)],
                axis=0,
            ).astype(bf16)

    out_ref[...] = (
        contract_last(upstream_ref[...], weight_ref[:, :IN_COLS])
        + contract_last(scaled[...], weight_ref[:, IN_COLS : IN_COLS + ADAPTERS])
    ).astype(bf16)
    grad_lower = contract_first(left_ref[...], scaled[...]).astype(bf16)
    shards = grad_lower.shape[0] // 128
    for shard in range(shards):
        late_ref[shards * step + shard, :128] = grad_lower[128 * shard : 128 * shard + 128]


def input_backward(upstream, left, lowered, mask, gathered, raising_all):
    rows, depth = left.shape
    tile = 512
    return pl.pallas_call(
        input_backward_kernel,
        grid=(depth // tile,),
        in_specs=[
            fixed((rows, IN_COLS), 0, 0),
            pl.BlockSpec((rows, tile), lambda i: (0, i)),
            fixed((rows, ADAPTERS), 0, 0),
            fixed((rows, ADAPTERS), 0, 0),
            pl.BlockSpec((tile, gathered.shape[1]), lambda i: (i, 0)),
            fixed((ADAPTERS, IN_COLS), 0, 0),
        ],
        out_specs=[
            pl.BlockSpec((rows, tile), lambda i: (0, i)),
            fixed((DP, 256, 128), 0, 0, 0),
        ],
        out_shape=[
            jax.ShapeDtypeStruct((rows, depth), bf16),
            jax.ShapeDtypeStruct((DP, 256, 128), bf16),
        ],
        scratch_shapes=[pltpu.VMEM((rows, ADAPTERS), bf16)],
        compiler_params=pltpu.CompilerParams(vmem_limit_bytes=VMEM_ALL),
        cost_estimate=pl.CostEstimate(flops=10**10, bytes_accessed=10**7, transcendentals=0),
        name="input_backward",
    )(upstream, left, lowered, mask, gathered, raising_all)


def ffn_kernel(
    left_ref,
    cotangent_ref,
    mask_ref,
    gate_ref,
    up_ref,
    lower_ref,
    raise_gate_ref,
    raise_up_ref,
    down_ref,
    lower_down_ref,
    raise_down_ref,
    left_down_ref,
    grad_gate_ref,
    grad_up_ref,
    grad_left_ref,
    lowered_ref,
    scaled_ref,
    scaled_down_ref,
    grad_left,
    grad_lowered,
):
    step = pl.program_id(0)
    model = left_ref.shape[1]

    @pl.when(step == 0)
    def _():
        lowered_ref[...] = (product(left_ref[...], lower_ref[...]) * mask_ref[...]).astype(bf16)
        scaled_down_ref[...] = (
            contract_last(cotangent_ref[...], raise_down_ref[...]) * mask_ref[...]
        ).astype(bf16)
        grad_left[...] = jnp.zeros_like(grad_left)
        grad_lowered[...] = jnp.zeros_like(grad_lowered)

    lowered = lowered_ref[...]
    gate = product(left_ref[...], gate_ref[...]) + product(lowered, raise_gate_ref[...])
    up = product(left_ref[...], up_ref[...]) + product(lowered, raise_up_ref[...])
    shards = range(0, down_ref.shape[0], 128)
    grad_act = contract_last(
        scaled_down_ref[...],
        jnp.concatenate([lower_down_ref[row : row + 64] for row in shards], axis=0),
    )
    for c in range(2):
        grad_act = grad_act + contract_last(
            cotangent_ref[:, c * model // 2 : (c + 1) * model // 2],
            jnp.concatenate([down_ref[row + 64 * c : row + 64 * c + 64] for row in shards], axis=0),
        )
    sigmoid = jax.nn.sigmoid(gate)
    silu = gate * sigmoid
    left_down_ref[...] = (silu * up).astype(bf16)
    grad_up = (grad_act * silu).astype(bf16)
    grad_gate = (grad_act * up * (sigmoid * (1.0 + gate * (1.0 - sigmoid)))).astype(bf16)
    grad_gate_ref[...] = grad_gate
    grad_up_ref[...] = grad_up
    grad_left[...] += contract_last(grad_gate, gate_ref[...]) + contract_last(grad_up, up_ref[...])
    grad_lowered[...] += contract_last(grad_gate, raise_gate_ref[...]) + contract_last(
        grad_up, raise_up_ref[...]
    )

    @pl.when(step == pl.num_programs(0) - 1)
    def _():
        scaled = (grad_lowered[...] * mask_ref[...]).astype(bf16)
        scaled_ref[...] = scaled
        grad_left_ref[...] = (grad_left[...] + contract_last(scaled, lower_ref[...])).astype(bf16)


def ffn_forward_backward(left, cotangent, mask, gathered, gu_raise, down_raise):
    rows, model = left.shape
    tile = 512
    tiles = UNITS // tile
    fold = model // 2
    first = fold // tile
    lower = (fold + 2 * UNITS) // ADAPTERS
    stacked = tile // 64 * 128
    whole_rows = fixed((rows, model), 0, 0)
    adapter_rows = fixed((rows, ADAPTERS), 0, 0)
    return pl.pallas_call(
        ffn_kernel,
        grid=(tiles,),
        in_specs=[
            whole_rows,
            whole_rows,
            adapter_rows,
            pl.BlockSpec((model, tile), lambda i: (0, first + i)),
            pl.BlockSpec((model, tile), lambda i: (0, first + tiles + i)),
            fixed((model, ADAPTERS), 0, lower),
            pl.BlockSpec((ADAPTERS, tile), lambda i: (0, i)),
            pl.BlockSpec((ADAPTERS, tile), lambda i: (0, tiles + i)),
            pl.BlockSpec((stacked, fold), lambda i: (i, 0)),
            pl.BlockSpec((stacked, ADAPTERS), lambda i: (i, lower + 1)),
            fixed((ADAPTERS, model), 0, 0),
        ],
        out_specs=[pl.BlockSpec((rows, tile), lambda i: (0, i))] * 3
        + [whole_rows, adapter_rows, adapter_rows, adapter_rows],
        out_shape=[jax.ShapeDtypeStruct((rows, UNITS), bf16)] * 3
        + [jax.ShapeDtypeStruct((rows, model), bf16)]
        + [jax.ShapeDtypeStruct((rows, ADAPTERS), bf16)] * 3,
        scratch_shapes=[pltpu.VMEM((rows, model), f32), pltpu.VMEM((rows, ADAPTERS), f32)],
        compiler_params=pltpu.CompilerParams(vmem_limit_bytes=VMEM_LIMIT),
        cost_estimate=pl.CostEstimate(flops=12 * 10**9, bytes_accessed=10**7, transcendentals=10**6),
        name="ffn",
    )(
        left,
        cotangent,
        mask,
        gathered,
        gathered,
        gathered,
        gu_raise,
        gu_raise,
        gathered,
        gathered,
        down_raise,
    )


def per_device(
    tokens,
    cotangent,
    seq_lengths,
    adapter_ids,
    norm_gain,
    ffn_gain,
    gate_gain,
    conv_weight,
    conv_bias,
    dt_bias,
    decay_log,
    skip_gain,
    frozen_input_weight,
    input_adapter_lower,
    input_adapter_upper,
    frozen_output_weight,
    output_adapter_lower,
    output_adapter_upper,
    frozen_gate_up_weight,
    gate_up_adapter_lower,
    gate_up_adapter_upper,
    frozen_down_weight,
    down_adapter_lower,
    down_adapter_upper,
):
    s = lax.axis_index("sp")
    d = lax.axis_index("dp")
    y = s // X_PAIR
    x = s % X_PAIR
    tok_count = tokens.shape[0]
    group_len = tok_count * SEQ
    first_len = seq_lengths[0, 0]
    set_ids = adapter_ids[0]

    def adapter_mask(token_index):
        resident = jnp.where(token_index >= first_len, set_ids[1], set_ids[0])
        return jnp.arange(ADAPTERS)[None, :] // ADAPTER_RANK == resident[:, None]

    group_index = jnp.arange(group_len)
    segment = (group_index >= first_len).astype(jnp.int32)
    position = group_index - first_len * segment
    mask_all = adapter_mask(group_index)
    ring_blocks = X_PAIR * ((y + jnp.arange(Y_RING)) % Y_RING) + x
    ring_index = (ring_blocks[:, None] * tok_count + jnp.arange(tok_count)[None, :]).reshape(-1)
    mask_ring = adapter_mask(ring_index)

    def head_columns(values):
        lead = values.shape[:-1]
        grouped = values.reshape(lead + (12, Y_RING, M_HEAD))
        grouped = lax.dynamic_slice_in_dim(grouped, HEADS_DEV * x, HEADS_DEV, len(lead))
        grouped = lax.dynamic_index_in_dim(grouped, y, len(lead) + 1, keepdims=False)
        return grouped.reshape(lead + (INNER,))

    def head_items(values):
        lead = values.shape[:-1]
        grouped = values.reshape(lead + (12, Y_RING))
        grouped = lax.dynamic_slice_in_dim(grouped, HEADS_DEV * x, HEADS_DEV, len(lead))
        return lax.dynamic_index_in_dim(grouped, y, len(lead) + 1, keepdims=False)

    kv_head = s // (H_Q // H_KV)

    def gather_rows(rows):
        return lax.all_gather(rows, "dp", axis=0, tiled=True)

    place = jnp.reshape(s, (1,)).astype(jnp.int32)
    in_all = gather_rows(
        pack(
            pack_input_kernel,
            (place, frozen_input_weight, input_adapter_lower, sixteen_rows(input_adapter_upper)),
            (128, IN_COLS + 2 * ADAPTERS),
        )
    )
    in_raise = raising([in_all[:, IN_COLS + ADAPTERS :]], IN_COLS)

    hidden = tokens.astype(f32)
    normed, norm_back = jax.vjp(partial(rms_scale, scale_gain=norm_gain), hidden)
    normed, frozen_output_weight, frozen_down_weight = lax.optimization_barrier(
        (normed.astype(bf16), frozen_output_weight, frozen_down_weight)
    )
    left_in = gather_rings(normed, y, x)

    out_rows = jnp.concatenate([frozen_output_weight, output_adapter_lower], axis=1)
    piece = lax.dynamic_slice_in_dim(out_rows, 64 * y, 64, 0)
    spread = jnp.zeros_like(piece)
    for k in range(1, Y_RING):
        block = lax.dynamic_slice_in_dim(out_rows, 64 * ((y + k) % Y_RING), 64, 0)
        pairs = [((i // 2) * SEQ + i, ((i // 2 + k) % Y_RING) * SEQ + i) for i in range(SEQ)]
        spread = spread + lax.ppermute(block, ("dp", "sp"), pairs)
    own_rows = (d >= Y_RING) | (d == y)
    model = frozen_output_weight.shape[1]
    out_all = gather_rows(
        pack(
            pack_output_kernel,
            (jnp.where(own_rows, piece, spread), sixteen_rows(output_adapter_upper)),
            (64, model + 3 * ADAPTERS),
        )
    )
    out_weight = out_all[:, : model + ADAPTERS]
    out_raise = raising(
        [out_all[:, model + 128 * c : model + 128 * c + 128] for c in (1, 2)], model
    )

    fold = model // 2
    ffn_all = gather_rows(
        pack(
            pack_ffn_kernel,
            (
                place,
                frozen_gate_up_weight,
                gate_up_adapter_lower,
                sixteen_rows(gate_up_adapter_upper),
                frozen_down_weight,
                down_adapter_lower,
                sixteen_rows(down_adapter_upper),
            ),
            (128, fold + 2 * UNITS + 4 * ADAPTERS),
        )
    )
    edge = fold + 2 * UNITS + 2 * ADAPTERS
    gu_raise = raising([ffn_all[:, edge : edge + ADAPTERS]], 2 * UNITS)
    down_raise = raising([ffn_all[:, edge + ADAPTERS :]], model)

    def masked(lowered, mask):
        return jnp.where(mask, lowered, 0.0).astype(bf16)

    def forward(left, weight, raising, mask):
        both = product(left, weight)
        width = raising.shape[1]
        lowered = masked(both[:, width:], mask)
        return both[:, :width] + product(lowered, raising), lowered

    def backward(left, lowered, upstream, weight, raising, mask):
        gradient_lowered = masked(contract_last(upstream, raising), mask)
        grad_raise = contract_first(lowered, upstream)
        grad_lower = contract_first(left, gradient_lowered)
        grad_left = contract_last(jnp.concatenate([upstream, gradient_lowered], axis=1), weight)
        return grad_left, grad_lower, grad_raise

    left_in, cot_own = lax.optimization_barrier((left_in, cotangent))
    cot_below = hop(cot_own, up)
    cot_above = hop(cot_own, down)
    projected, lower_in = input_forward(left_in, mask_all.astype(f32), in_all, in_raise)

    projected, cot_below, cot_above = lax.optimization_barrier((projected, cot_below, cot_above))
    half = tok_count // 2
    cot_far = hop(cot_below[:half], up), hop(cot_above[half:], down)
    taps = jnp.concatenate(
        [
            jnp.concatenate([head_columns(conv_weight[:, :D_SSM]), conv_weight[:, D_SSM:]], axis=1),
            jnp.concatenate([head_columns(conv_bias[:D_SSM]), conv_bias[D_SSM:]])[None],
            jnp.zeros((3, INNER + 2 * STATE), f32),
        ],
        axis=0,
    )
    rate_rows = jnp.pad(
        jnp.stack([head_items(dt_bias), -jnp.exp(head_items(decay_log))]),
        ((0, 6), (0, 128 - HEADS_DEV)),
    )
    skip_rows = jnp.pad(
        jnp.stack([jnp.repeat(head_items(skip_gain), M_HEAD), head_columns(gate_gain)]),
        ((0, 6), (0, 0)),
    )
    gain_pair = lax.dynamic_index_in_dim(
        gate_gain.reshape(12, Y_RING, M_HEAD), y, 1, keepdims=False
    ).reshape(1, -1)
    cosine_table, sine_table = rotary_tables(position)
    gated, scanned, squares, convolved, states = scan_forward(
        seq_lengths, projected, taps, rate_rows, skip_rows
    )
    squares, cot_far = lax.optimization_barrier((squares, cot_far))
    attended, log_totals = attention_forward(seq_lengths, projected, cosine_table, sine_table)
    squares = sum_ring_small(squares.reshape(SEQ, 8, tok_count)[:, 0])
    inverse = lax.rsqrt((squares + hop(squares, side)) / D_SSM + epsilon)
    mixed = jnp.concatenate([attended, gated], axis=1)
    cot_ring = jnp.concatenate([cot_own, cot_above, *cot_far, cot_below], axis=0)

    def to_ring(values):
        doubled = jnp.concatenate([values, values], axis=0)
        rolled = lax.dynamic_slice_in_dim(doubled, X_PAIR * tok_count * y, group_len, 0)
        return rolled.reshape(Y_RING, X_PAIR, tok_count, -1)

    def from_ring(values):
        flat = values.reshape(group_len, -1)
        doubled = jnp.concatenate([flat, flat], axis=0)
        start = X_PAIR * tok_count * ((Y_RING - y) % Y_RING)
        return lax.dynamic_slice_in_dim(doubled, start, group_len, 0)

    ring_len = Y_RING * tok_count
    mixed_ring = to_ring(mixed)
    kept = lax.dynamic_index_in_dim(mixed_ring, x, 1, keepdims=False).reshape(ring_len, SLICE)
    other = lax.dynamic_index_in_dim(mixed_ring, 1 - x, 1, keepdims=False).reshape(ring_len, SLICE)
    received = hop(other, side)
    low = jnp.where(x == 0, kept, received)
    high = jnp.where(x == 0, received, kept)
    gated_pair = jnp.concatenate([low[:, HEAD:], high[:, HEAD:]], axis=1).astype(f32)
    inverse_ring = lax.dynamic_index_in_dim(
        to_ring(inverse.reshape(-1, 1)), x, 1, keepdims=False
    ).reshape(ring_len, 1)
    left_out = jnp.concatenate(
        [low[:, :HEAD], high[:, :HEAD], (gated_pair * inverse_ring * gain_pair).astype(bf16)],
        axis=1,
    )
    branch_part, lower_out = forward(left_out, out_weight, out_raise, mask_ring)
    (branch,) = scatter_ring(branch_part)
    residual = hidden + branch
    normed_ffn, ffn_norm_back = jax.vjp(partial(rms_scale, scale_gain=ffn_gain), residual)
    left_gu = gather_ring(normed_ffn.astype(bf16))
    left_down, grad_gate_half, grad_up_half, grad_gu_part, lower_gu, scaled_gu, scaled_down = (
        ffn_forward_backward(
            left_gu, cot_ring, mask_ring.astype(f32), ffn_all, gu_raise, down_raise
        )
    )
    folded = ffn_all[:, :fold].reshape(DP, 2, 64, fold)
    lowers = ffn_all[:, fold + 2 * UNITS + ADAPTERS : edge].reshape(DP, 2, 64, ADAPTERS)
    down_weight = jnp.concatenate(
        [
            folded[:, 0].reshape(UNITS, -1),
            folded[:, 1].reshape(UNITS, -1),
            lowers[:, 0].reshape(UNITS, -1),
        ],
        axis=1,
    )
    ffn_part, lower_down = forward(left_down, down_weight, down_raise, mask_ring)
    grad_a_down = contract_first(left_down, scaled_down)
    grad_b_down = contract_first(lower_down, cot_ring)
    grad_a_gu = contract_first(left_gu, scaled_gu)
    grad_b_gu = contract_first(
        lower_gu, jnp.concatenate([grad_gate_half, grad_up_half], axis=1)
    )
    (grad_left_gu,) = scatter_ring(grad_gu_part)
    (grad_resid_norm,) = ffn_norm_back(grad_left_gu)
    grad_residual = cotangent.astype(f32) + grad_resid_norm
    grad_ring = gather_ring(grad_residual.astype(bf16))
    grad_mixed, grad_a_out, grad_b_out = backward(
        left_out, lower_out, grad_ring, out_weight, out_raise, mask_ring
    )
    early = jnp.concatenate(
        [
            grad_a_out.astype(bf16).reshape(DP, -1, 128),
            blocks_of(grad_b_out.astype(bf16)),
            grad_a_gu.astype(bf16).reshape(DP, -1, 128),
            blocks_of(grad_b_gu.astype(bf16)),
            grad_a_down.astype(bf16).reshape(DP, -1, 128),
            blocks_of(grad_b_down.astype(bf16)),
        ],
        axis=1,
    )
    grad_mixed = grad_mixed.astype(bf16)
    low = jnp.concatenate([grad_mixed[:, :HEAD], grad_mixed[:, 2 * HEAD : 2 * HEAD + INNER]], axis=1)
    high = jnp.concatenate([grad_mixed[:, HEAD : 2 * HEAD], grad_mixed[:, 2 * HEAD + INNER :]], axis=1)
    kept = jnp.where(x == 0, low, high)
    received, grad_mixed = lax.optimization_barrier(
        (hop(jnp.where(x == 0, high, low), side), grad_mixed)
    )
    first = jnp.where(x == 0, kept, received).reshape(Y_RING, 1, tok_count, SLICE)
    second = jnp.where(x == 0, received, kept).reshape(Y_RING, 1, tok_count, SLICE)
    head_grads, early, ffn_part = lax.optimization_barrier(
        (from_ring(jnp.concatenate([first, second], axis=1)), halve_cores(early, d), ffn_part)
    )
    early = halve_neighbours(early, d)
    (ffn,) = scatter_ring(ffn_part)
    layer_out = (residual + ffn).astype(bf16)
    slope_ring = jnp.sum(
        grad_mixed[:, 2 * HEAD :].astype(f32) * gain_pair * gated_pair, axis=1
    ).reshape(Y_RING, tok_count)
    slope_own = sum_ring_small(
        lax.dynamic_slice_in_dim(
            jnp.concatenate([slope_ring, slope_ring], axis=0), (Y_RING - y) % Y_RING, Y_RING, 0
        )
    )
    slope_mate = hop(slope_own, side)
    slope = jnp.stack(
        [jnp.where(x == 0, slope_own, slope_mate), jnp.where(x == 0, slope_mate, slope_own)],
        axis=1,
    ).reshape(SEQ, tok_count)
    scales = jnp.stack(
        [inverse.reshape(-1), (inverse * inverse * inverse * slope / D_SSM).reshape(-1)], axis=1
    )
    grad_qkv = attention_backward(
        seq_lengths, projected, cosine_table, sine_table, head_grads, log_totals
    )
    grad_qkv, early = lax.optimization_barrier((grad_qkv, early))
    early = scatter_shards(early, Z_RINGS)
    grad_projected = scan_backward(
        seq_lengths,
        projected,
        convolved,
        scanned,
        states,
        head_grads,
        scales,
        grad_qkv,
        taps,
        rate_rows,
        skip_rows,
    )
    grad_projected, layer_out, early = lax.optimization_barrier((grad_projected, layer_out, early))
    grad_left_part, late = input_backward(
        grad_projected, left_in, lower_in, mask_all.astype(f32), in_all, in_raise
    )
    late, early = lax.optimization_barrier((halve_cores(late, d), early))
    grad_left_parts, late = lax.optimization_barrier(
        (exchange_seq(grad_left_part), scatter_shards(late, CHIPS))
    )
    grad_left = jnp.sum(grad_left_parts.astype(f32), axis=0)
    (grad_hidden_norm,) = norm_back(grad_left)
    grad_tokens = (grad_residual + grad_hidden_norm).astype(bf16)

    a_in_own = late[:128]
    b_in_own = row_from_blocks(late[128:240])
    a_out_block = early[:64].astype(bf16)
    b_out_own = early[64:192]
    a_gu_own = early[192:320]
    b_gu_own = early[320:448]
    a_down_own = early[448:512]
    b_down_own = early[512:640]
    zero_rows = jnp.zeros((256, 128), f32)
    a_out_own = lax.dynamic_update_slice_in_dim(
        zero_rows, jnp.where(own_rows, early[:64], 0.0), 64 * y, 0
    )
    for k in range(1, Y_RING):
        pairs = [(((i // 2 + k) % Y_RING) * SEQ + i, (i // 2) * SEQ + i) for i in range(SEQ)]
        moved = lax.ppermute(a_out_block, ("dp", "sp"), pairs)
        a_out_own = a_out_own + lax.dynamic_update_slice_in_dim(
            zero_rows, moved.astype(f32), 64 * ((y + k) % Y_RING), 0
        )
    a_down_own = lax.dynamic_update_slice_in_dim(zero_rows, a_down_own, 64 * y, 0)
    b_gu_full = lax.dynamic_update_slice_in_dim(
        jnp.zeros((8, 2 * DP, Y_RING, 64), f32),
        row_from_blocks(b_gu_own).reshape(8, 2 * DP, 1, 64),
        y,
        2,
    ).reshape(512, 128)

    def spread_heads(part, width):
        return lax.dynamic_update_slice(
            jnp.zeros((8, 12, Y_RING, width), f32),
            part.reshape(8, HEADS_DEV, 1, width),
            (0, HEADS_DEV * x, y, 0),
        ).reshape(8, -1)

    kv_width = H_KV * HEAD
    b_in_full = jnp.concatenate(
        [
            lax.dynamic_update_slice_in_dim(
                jnp.zeros((8, EDGE_INNER), f32), b_in_own[:, COL_Q:COL_INNER], s * HEAD, 1
            ),
            spread_heads(b_in_own[:, COL_INNER:COL_GATE], M_HEAD),
            lax.dynamic_update_slice_in_dim(
                jnp.zeros((8, kv_width), f32), b_in_own[:, COL_K:COL_V], kv_head * HEAD, 1
            ),
            lax.dynamic_update_slice_in_dim(
                jnp.zeros((8, kv_width), f32), b_in_own[:, COL_V:COL_BC], kv_head * HEAD, 1
            ),
            b_in_own[:, COL_BC:COL_STEP],
            spread_heads(b_in_own[:, COL_GATE:COL_K], M_HEAD),
            spread_heads(b_in_own[:, COL_STEP : COL_STEP + HEADS_DEV], 1),
            jnp.zeros((8, 80), f32),
        ],
        axis=1,
    )
    full = jnp.concatenate(
        [
            a_in_own,
            b_in_full.reshape(-1, 128),
            a_out_own,
            b_out_own,
            a_gu_own,
            b_gu_full,
            a_down_own,
            b_down_own,
        ],
        axis=0,
    )
    full = jnp.pad(full, ((0, (-full.shape[0]) % 128), (0, 0)))
    full = gather_seq(scatter_seq(full).astype(bf16)).astype(f32)
    out_a_in = full[:128]
    out_b_in = full[128:648].reshape(8, -1)[:, : EDGE_STEP + M_HEADS]
    full = full[648:]
    out_a_out = full[:256]
    out_b_out = row_from_blocks(full[256:384])
    out_a_gu = full[384:512]
    out_b_gu = full[512:1024].reshape(8, -1)
    out_a_down = full[1024:1280]
    out_b_down = row_from_blocks(full[1280:1408])
    return (
        layer_out,
        grad_tokens,
        out_a_in,
        out_b_in,
        out_a_out,
        out_b_out,
        out_a_gu,
        out_b_gu,
        out_a_down,
        out_b_down,
    )


def solution(mesh):
    rows = P("dp", None)
    both = P(("dp", "sp"), None)
    in_specs = (both, both) + (rows,) * 2 + (P(),) * 8 + (rows,) * 12
    out_specs = (both, both) + (rows,) * 8
    return jax.shard_map(
        per_device, mesh=mesh, in_specs=in_specs, out_specs=out_specs, check_vma=False
    )
```

```python
from functools import partial

import jax
import jax.numpy as jnp
from jax import lax
from jax.experimental import pallas as pl
from jax.experimental.pallas import tpu as pltpu
from jax.sharding import PartitionSpec as P

H_Q = 8
H_KV = 2
HEAD = 128
M_HEADS = 48
M_HEAD = 64
CONV = 4
ADAPTER_RANK = 16
ADAPTER_SETS = 8
SPAN = 128
STATE = 256
D_SSM = 3072
SHARED = 1024
ADAPTERS = ADAPTER_RANK * ADAPTER_SETS

Y_RING = 4
X_PAIR = 2
SEQ = 8
DP = 16
HEADS_DEV = 6
INNER = HEADS_DEV * M_HEAD
SLICE = HEAD + INNER
MIX = X_PAIR * SLICE
UNITS = 1024

COL_Q = 0
COL_INNER = COL_Q + HEAD
COL_GATE = COL_INNER + INNER
COL_K = COL_GATE + INNER
COL_V = COL_K + HEAD
COL_BC = COL_V + HEAD
COL_STEP = COL_BC + 2 * STATE
IN_COLS = COL_STEP + 128

EDGE_INNER = H_Q * HEAD
EDGE_SHARED = EDGE_INNER + D_SSM
EDGE_GATE = EDGE_SHARED + SHARED
EDGE_STEP = EDGE_GATE + D_SSM

CONVOLVED = INNER + 2 * STATE
VMEM_ALL = 56 * 1024 * 1024

epsilon = 1e-05
rope_base = 100000000000.0
masked_score = -1e30
highest = lax.Precision.HIGHEST
bf16 = jnp.bfloat16
f32 = jnp.float32


def rms_scale(vectors, scale_gain):
    return (
        vectors
        * lax.rsqrt(jnp.mean(vectors * vectors, axis=-1, keepdims=True) + epsilon)
        * scale_gain
    )


def silu_value(vectors):
    return vectors * jax.nn.sigmoid(vectors)


def swiglu(gate_and_up):
    half_width = gate_and_up.shape[1] // 2
    return silu_value(gate_and_up[:, :half_width]) * gate_and_up[:, half_width:]


def rotary_tables(position):
    lanes = jnp.arange(HEAD)
    half_width = HEAD // 2
    frequency = rope_base ** (-((lanes % half_width).astype(f32) * 2.0 / HEAD))
    angle = position.astype(f32)[:, None] * frequency[None, :]
    return jnp.cos(angle), jnp.where(lanes < half_width, -1.0, 1.0) * jnp.sin(angle)


def product(left, right):
    return jnp.dot(left, right, preferred_element_type=f32)


def contract_last(left, right):
    return lax.dot_general(left, right, (((1,), (1,)), ((), ())), preferred_element_type=f32)


def contract_first(left, right):
    return lax.dot_general(left, right, (((0,), (0,)), ((), ())), preferred_element_type=f32)


def hop(value, target):
    return lax.ppermute(value, "sp", [(i, target(i)) for i in range(SEQ)])


def up(i):
    return (i + X_PAIR) % SEQ


def down(i):
    return (i - X_PAIR) % SEQ


def side(i):
    return i ^ 1


def gather_ring(block):
    half = block.shape[0] // 2
    below = hop(block, up)
    above = hop(block, down)
    far_first = hop(below[:half], up)
    far_second = hop(above[half:], down)
    return jnp.concatenate([block, above, far_first, far_second, below], axis=0)


def scatter_ring(partial_rows, *after):
    n = partial_rows.shape[0] // Y_RING
    half = n // 2
    far = partial_rows[2 * n : 3 * n].astype(bf16)
    from_below = hop(far[:half], up)
    from_above = hop(far[half:], down)
    from_below, from_above, *after = lax.optimization_barrier((from_below, from_above, *after))
    partial_rows = partial_rows.astype(f32)
    to_up = partial_rows[n : 2 * n]
    to_up = jnp.concatenate([to_up[:half] + from_below.astype(f32), to_up[half:]], axis=0)
    to_down = partial_rows[3 * n :]
    to_down = jnp.concatenate([to_down[:half], to_down[half:] + from_above.astype(f32)], axis=0)
    low = hop(to_up.astype(bf16), up).astype(f32)
    high = hop(to_down.astype(bf16), down).astype(f32)
    return partial_rows[:n] + low + high, *after


def halved(stack, own, axis, target):
    kept = lax.dynamic_index_in_dim(stack, own, axis, keepdims=False)
    sent = lax.dynamic_index_in_dim(stack, 1 - own, axis, keepdims=False)
    received = lax.ppermute(sent, "dp", [(i, target(i)) for i in range(DP)])
    return (kept.astype(f32) + received.astype(f32)).astype(bf16)


def halve_cores(stack, d):
    return halved(stack.reshape(8, 2, -1, 128), d % 2, 1, lambda i: i ^ 1)


def halve_neighbours(stack, d):
    return halved(stack.reshape(2, 4, -1, 128), d // 8, 0, lambda i: (i + 8) % DP)


CHIPS = [[2 * i + c for i in range(DP // 2)] for c in range(2)]
Z_RINGS = [[8 * n + 2 * z + c for z in range(4)] for n in range(2) for c in range(2)]


def scatter_shards(stack, groups):
    return lax.psum_scatter(
        stack.reshape(-1, 128), "dp", scatter_dimension=0, axis_index_groups=groups, tiled=True
    ).astype(f32)


def gather_seq(block):
    copies = jnp.broadcast_to(block[None], (SEQ,) + block.shape)
    return lax.all_to_all(copies, "sp", split_axis=0, concat_axis=0).reshape(
        (SEQ * block.shape[0],) + block.shape[1:]
    )


def exchange_seq(partial_rows):
    pieces = partial_rows.astype(bf16).reshape((SEQ, -1) + partial_rows.shape[1:])
    return lax.all_to_all(pieces, "sp", split_axis=0, concat_axis=0)


def scatter_seq(partial_rows):
    return jnp.sum(exchange_seq(partial_rows).astype(f32), axis=0)


def gather_rings(block, y, x):
    n = block.shape[0]
    half = n // 2
    mate = hop(block, side)
    above = hop(block, down)
    below = hop(block, up)
    mate_above = hop(mate, down)
    mate_below = hop(mate, up)
    out = jnp.zeros((SEQ * n,) + block.shape[1:], block.dtype)
    for rows, distance, column, shift in (
        (block, 0, x, 0),
        (above, 1, x, 0),
        (below, 3, x, 0),
        (mate, 0, 1 - x, 0),
        (hop(below[:half], up), 2, x, 0),
        (hop(above[half:], down), 2, x, half),
        (mate_above, 1, 1 - x, 0),
        (mate_below, 3, 1 - x, 0),
        (hop(mate_below[:half], up), 2, 1 - x, 0),
        (hop(mate_above[half:], down), 2, 1 - x, half),
    ):
        start = n * (X_PAIR * ((y + distance) % Y_RING) + column) + shift
        out = lax.dynamic_update_slice_in_dim(out, rows, start, 0)
    return out


def sum_ring_small(value):
    total = value
    for offset in range(X_PAIR, SEQ, X_PAIR):
        total = total + hop(value, lambda i, offset=offset: (i + offset) % SEQ)
    return total


def blocks_of(matrix):
    n = matrix.shape[1] // 128
    return matrix.reshape(DP, 8, n, 128).transpose(0, 2, 1, 3).reshape(DP, 8 * n, 128)


def row_from_blocks(stacked):
    n = stacked.shape[0] // 8
    return stacked.reshape(n, 8, 128).transpose(1, 0, 2).reshape(8, 128 * n)


def sixteen_rows(rows):
    return jnp.pad(rows, ((0, 16 - rows.shape[0]), (0, 0)))


def pick_columns(block, y):
    rows = lax.broadcasted_iota(jnp.int32, (512, 128), 0)
    lanes = lax.broadcasted_iota(jnp.int32, (512, 128), 1)
    wanted = jnp.where(lanes < M_HEAD, lanes, lanes + 256 - M_HEAD) + M_HEAD * y
    return product(block, (rows == wanted).astype(bf16))


def pack_input_kernel(place_ref, weight_ref, lower_ref, upper_ref, out_ref):
    s = place_ref[0]
    y = s // X_PAIR
    x = s % X_PAIR
    kv_head = s // (H_Q // H_KV)

    def at(column):
        return pl.ds(pl.multiple_of(column, 128), 128)

    def share(ref):
        def heads(edge):
            return [
                pick_columns(
                    ref[:, pl.ds(pl.multiple_of(edge + 256 * (HEADS_DEV * x + 2 * pair), 128), 512)], y
                )
                for pair in range(HEADS_DEV // 2)
            ]

        step_rows = lax.broadcasted_iota(jnp.int32, (M_HEADS, 128), 0)
        step_lanes = lax.broadcasted_iota(jnp.int32, (M_HEADS, 128), 1)
        picked = (step_rows == Y_RING * (HEADS_DEV * x + step_lanes) + y) & (step_lanes < HEADS_DEV)
        return (
            [ref[:, at(HEAD * s)].astype(f32)]
            + heads(EDGE_INNER)
            + heads(EDGE_GATE)
            + [
                ref[:, at(EDGE_SHARED + HEAD * kv_head)].astype(f32),
                ref[:, at(EDGE_SHARED + HEAD * (H_KV + kv_head))].astype(f32),
            ]
            + [
                ref[:, EDGE_SHARED + 2 * H_KV * HEAD + 128 * i : EDGE_SHARED + 2 * H_KV * HEAD + 128 * i + 128].astype(f32)
                for i in range(2 * STATE // 128)
            ]
            + [product(ref[:, EDGE_STEP:], picked.astype(bf16))]
        )

    for i, piece in enumerate(share(weight_ref)):
        out_ref[:, 128 * i : 128 * i + 128] = piece.astype(bf16)
    out_ref[:, IN_COLS : IN_COLS + ADAPTERS] = lower_ref[...]
    upper = [piece[:8] for piece in share(upper_ref)]
    upper.append(jnp.zeros((128 - 8 * len(upper), 128), f32))
    out_ref[:, IN_COLS + ADAPTERS :] = jnp.concatenate(upper, axis=0).astype(bf16)


def pack_ffn_kernel(
    place_ref, gu_ref, gu_lower_ref, gu_upper_ref, down_ref, down_lower_ref, down_upper_ref, out_ref
):
    y = place_ref[0] // X_PAIR
    fold = down_ref.shape[1] // 2
    rows = pl.ds(pl.multiple_of(64 * y, 64), 64)
    out_ref[:64, :fold] = down_ref[rows, :fold]
    out_ref[64:, :fold] = down_ref[rows, fold:]
    pairs = 2 * UNITS // 128
    for i in range(pairs):
        out_ref[:, fold + 128 * i : fold + 128 * i + 128] = pick_columns(
            gu_ref[:, 512 * i : 512 * i + 512], y
        ).astype(bf16)
    edge = fold + 2 * UNITS
    out_ref[:, edge : edge + 128] = gu_lower_ref[...]
    edge += 128
    out_ref[:64, edge : edge + 128] = down_lower_ref[rows, :]
    out_ref[64:, edge : edge + 128] = jnp.zeros((64, 128), bf16)
    edge += 128
    out_ref[:, edge : edge + 128] = jnp.concatenate(
        [pick_columns(gu_upper_ref[:, 512 * i : 512 * i + 512], y)[:8] for i in range(pairs)], axis=0
    ).astype(bf16)
    edge += 128
    out_ref[:, edge:] = jnp.concatenate(
        [down_upper_ref[:, 128 * i : 128 * i + 128].astype(f32)[:8] for i in range(2 * fold // 128)],
        axis=0,
    ).astype(bf16)


def fold_upper(upper_ref, out_ref, column):
    for c in range(2):
        out_ref[:, column + 128 * c : column + 128 * c + 128] = jnp.concatenate(
            [
                upper_ref[:, 1024 * c + 128 * i : 1024 * c + 128 * i + 128].astype(f32)[:8]
                for i in range(8)
            ],
            axis=0,
        ).astype(bf16)


def pack_output_kernel(rows_ref, upper_ref, out_ref):
    width = rows_ref.shape[1]
    out_ref[:, :width] = rows_ref[...]
    fold_upper(upper_ref, out_ref, width)


def raising_kernel(*refs):
    out_ref = refs[-1]
    column = 0
    for ref in refs[:-1]:
        stacked = ref[...].astype(f32)
        depth = stacked.shape[0] // DP
        for block in range(min(depth // 8, out_ref.shape[1] // 128)):
            out_ref[:, column : column + 128] = jnp.concatenate(
                [
                    stacked[depth * shard + 8 * block : depth * shard + 8 * block + 8]
                    for shard in range(DP)
                ],
                axis=0,
            ).astype(bf16)
            column += 128


def raising(stacks, width):
    return pl.pallas_call(
        raising_kernel,
        in_specs=[pl.BlockSpec(memory_space=pltpu.VMEM)] * len(stacks),
        out_specs=pl.BlockSpec(memory_space=pltpu.VMEM),
        out_shape=jax.ShapeDtypeStruct((ADAPTERS, width), bf16),
        compiler_params=pltpu.CompilerParams(vmem_limit_bytes=32 * 1024 * 1024),
    )(*stacks)


def pack(kernel, arrays, shape):
    return pl.pallas_call(
        kernel,
        in_specs=[
            pl.BlockSpec(memory_space=pltpu.SMEM if a.ndim == 1 else pltpu.VMEM) for a in arrays
        ],
        out_specs=pl.BlockSpec(memory_space=pltpu.VMEM),
        out_shape=jax.ShapeDtypeStruct(shape, bf16),
        compiler_params=pltpu.CompilerParams(vmem_limit_bytes=32 * 1024 * 1024),
    )(*arrays)


def lane_index(shape):
    return lax.broadcasted_iota(jnp.int32, shape, 1)


def row_index(shape):
    return lax.broadcasted_iota(jnp.int32, shape, 0)


def over_heads(per_head):
    rows = per_head.shape[0]
    low = lane_index((rows, 128)) < M_HEAD
    return jnp.concatenate(
        [
            jnp.where(low, per_head[:, 2 * pair : 2 * pair + 1], per_head[:, 2 * pair + 1 : 2 * pair + 2])
            for pair in range(HEADS_DEV // 2)
        ],
        axis=1,
    )


def head_sums(values):
    member = (row_index((INNER, 128)) // M_HEAD == lane_index((INNER, 128))).astype(bf16)
    coarse = values.astype(bf16)
    fine = (values - coarse.astype(f32)).astype(bf16)
    return product(coarse, member) + product(fine, member)


def span_terms(convolved, step_block, rate_rows, first_len, start):
    shifted = step_block + rate_rows[0:1]
    rates = jnp.log1p(jnp.exp(-jnp.abs(shifted))) + jnp.maximum(shifted, 0.0)
    log_decay = rates * rate_rows[1:2]
    rows = row_index((SPAN, SPAN))
    lanes = lane_index((SPAN, SPAN))
    below = rows >= lanes
    cumulative = jnp.dot(
        below.astype(f32), log_decay, precision=highest, preferred_element_type=f32
    )
    seg_rows = (rows + start >= first_len).astype(jnp.int32)
    seg_lanes = (lanes + start >= first_len).astype(jnp.int32)
    allowed = below & (seg_rows == seg_lanes)
    last_seg = (start + SPAN - 1 >= first_len).astype(jnp.int32)
    previous = (start - 1 >= first_len).astype(jnp.int32)
    total = cumulative[SPAN - 1 : SPAN]
    entry = jnp.where(seg_rows == previous, jnp.exp(cumulative), 0.0)
    tail = jnp.where(seg_rows == last_seg, jnp.exp(total - cumulative), 0.0)
    keep = jnp.where(last_seg == previous, jnp.exp(total), 0.0)
    activated = convolved * jax.nn.sigmoid(convolved)
    x_in = activated[:, :INNER]
    in_state = activated[:, INNER : INNER + STATE]
    out_state = activated[:, INNER + STATE :]
    return shifted, rates, cumulative, allowed, entry, tail, keep, x_in, in_state, out_state


def decay_of(cumulative, across, allowed, head):
    gap = cumulative[:, head : head + 1] - across[head : head + 1]
    return jnp.exp(jnp.where(allowed, gap, masked_score))


def scan_forward_kernel(
    lengths_ref,
    proj_ref,
    taps_ref,
    rate_rows_ref,
    skip_ref,
    gated_ref,
    scanned_ref,
    squares_ref,
    convolved_ref,
    states_ref,
    state,
    last_rows,
):
    step = pl.program_id(0)
    start = step * SPAN
    first_len = lengths_ref[0, 0]

    @pl.when(step == 0)
    def _():
        state[...] = jnp.zeros_like(state)
        last_rows[...] = jnp.zeros_like(last_rows)

    signal = jnp.concatenate(
        [proj_ref[:, COL_INNER:COL_GATE], proj_ref[:, COL_BC:COL_STEP]], axis=1
    ).astype(f32)
    row = start + row_index((SPAN, 1))
    position = row - jnp.where(row >= first_len, first_len, 0)
    convolved = taps_ref[4:5] + taps_ref[3:4] * signal
    before = last_rows[...]
    top = row_index((8, 1))
    for offset in range(1, CONV):
        moved = pltpu.roll(signal, offset, 0)
        edge = jnp.where(top < offset, pltpu.roll(before, offset, 0), moved[:8])
        moved = jnp.concatenate([edge, moved[8:]], axis=0)
        convolved = convolved + taps_ref[3 - offset : 4 - offset] * jnp.where(
            position >= offset, moved, 0.0
        )
    last_rows[...] = signal[SPAN - 8 :]
    convolved_ref[...] = convolved
    step_block = proj_ref[:, COL_STEP:].astype(f32)
    _, rates, cumulative, allowed, entry, tail, keep, x_in, in_state, out_state = span_terms(
        convolved, step_block, rate_rows_ref[...], first_len, start
    )
    across = cumulative.T
    in_half = in_state.astype(bf16)
    out_half = out_state.astype(bf16)
    state_now = state[...]
    state_half = state_now.astype(bf16)
    states_ref[0] = state_half
    mixing = contract_last(out_half, in_half)
    rates_wide = over_heads(rates)
    weighted = (x_in * rates_wide).astype(bf16)
    low = lane_index((SPAN, 128)) < M_HEAD
    within = []
    for pair in range(HEADS_DEV // 2):
        block = weighted[:, 128 * pair : 128 * pair + 128]
        sides = [
            product(
                (mixing * decay_of(cumulative, across, allowed, 2 * pair + i)).astype(bf16), block
            )
            for i in range(2)
        ]
        within.append(jnp.where(low, sides[0], sides[1]))
    result = (
        jnp.concatenate(within, axis=1)
        + product(out_half, state_half) * over_heads(entry)
        + skip_ref[0:1] * x_in
    )
    scanned = result.astype(bf16)
    scanned_ref[...] = scanned
    gate = proj_ref[:, COL_GATE:COL_K].astype(f32)
    gated = scanned.astype(f32) * (gate * jax.nn.sigmoid(gate))
    gated_ref[...] = gated.astype(bf16)
    squares_ref[...] = lax.dot_general(
        jnp.ones((8, INNER), f32),
        gated * gated,
        (((1,), (1,)), ((), ())),
        precision=highest,
        preferred_element_type=f32,
    )
    state[...] = state_now * over_heads(keep) + contract_first(
        in_half, (x_in * over_heads(tail * rates)).astype(bf16)
    )


def scan_backward_kernel(
    lengths_ref,
    proj_ref,
    convolved_ref,
    scanned_ref,
    states_ref,
    upstream_ref,
    scales_ref,
    grad_query_ref,
    grad_key_ref,
    grad_value_ref,
    taps_ref,
    rate_rows_ref,
    skip_ref,
    out_ref,
    grad_state,
    next_rows,
):
    step = pl.num_programs(0) - 1 - pl.program_id(0)
    start = step * SPAN
    first_len = lengths_ref[0, 0]

    @pl.when(pl.program_id(0) == 0)
    def _():
        grad_state[...] = jnp.zeros_like(grad_state)
        next_rows[...] = jnp.zeros_like(next_rows)

    convolved = convolved_ref[...]
    step_block = proj_ref[:, COL_STEP:].astype(f32)
    rate_rows = rate_rows_ref[...]
    shifted, rates, cumulative, allowed, entry, tail, keep, x_in, in_state, out_state = span_terms(
        convolved, step_block, rate_rows, first_len, start
    )
    across = cumulative.T
    in_half = in_state.astype(bf16)
    out_half = out_state.astype(bf16)
    state_half = states_ref[0]

    gate = proj_ref[:, COL_GATE:COL_K].astype(f32)
    gate_sigmoid = jax.nn.sigmoid(gate)
    gate_silu = gate * gate_sigmoid
    scanned = scanned_ref[...].astype(f32)
    upstream = upstream_ref[:, HEAD:].astype(f32) * skip_ref[1:2]
    grad_gated = scales_ref[:, 0:1] * upstream - scales_ref[:, 1:2] * (scanned * gate_silu)
    out_ref[:, COL_GATE:COL_K] = (
        grad_gated * scanned * (gate_sigmoid * (1.0 + gate * (1.0 - gate_sigmoid)))
    ).astype(bf16)
    grad_half = (grad_gated * gate_silu).astype(bf16)
    grad_result = grad_half.astype(f32)

    mixing = contract_last(out_half, in_half)
    rates_wide = over_heads(rates)
    entry_wide = over_heads(entry)
    tail_wide = over_heads(tail)
    keep_wide = over_heads(keep)
    weighted = (x_in * rates_wide).astype(bf16)
    lane = lane_index((SPAN, 128))
    low = lane < M_HEAD
    grad_mixing = jnp.zeros((SPAN, SPAN), f32)
    grad_cumulative = jnp.zeros((SPAN, 128), f32)
    grad_across = jnp.zeros((SPAN, 128), f32)
    head_row = row_index((SPAN, 128))
    grad_weighted = []
    for pair in range(HEADS_DEV // 2):
        block = weighted[:, 128 * pair : 128 * pair + 128]
        grad_block = grad_half[:, 128 * pair : 128 * pair + 128]
        sides = []
        for i in range(2):
            head = 2 * pair + i
            decay = decay_of(cumulative, across, allowed, head)
            spread = mixing * decay
            sides.append(contract_first(spread.astype(bf16), grad_block))
            mine = low if i == 0 else jnp.logical_not(low)
            grad_spread = contract_last(jnp.where(mine, grad_block, jnp.zeros_like(grad_block)), block)
            grad_mixing = grad_mixing + grad_spread * decay
            grad_gap = grad_spread * spread
            grad_cumulative = jnp.where(
                lane == head, jnp.sum(grad_gap, axis=1, keepdims=True), grad_cumulative
            )
            grad_across = jnp.where(
                head_row == head, jnp.sum(grad_gap, axis=0, keepdims=True), grad_across
            )
        grad_weighted.append(jnp.where(low, sides[0], sides[1]))
    grad_weighted = jnp.concatenate(grad_weighted, axis=1)
    grad_cumulative = grad_cumulative - grad_across.T

    grad_next = grad_state[...]
    grad_next_half = grad_next.astype(bf16)
    grad_entered = (grad_result * entry_wide).astype(bf16)
    from_state = product(out_half, state_half)
    to_state = product(in_half, grad_next_half)
    tail_rates = tail_wide * rates_wide
    grad_mixing_half = grad_mixing.astype(bf16)
    grad_out_state = product(grad_mixing_half, in_half) + contract_last(grad_entered, state_half)
    grad_in_state = contract_first(grad_mixing_half, out_half) + contract_last(
        (x_in * tail_rates).astype(bf16), grad_next_half
    )
    sums = head_sums(
        jnp.concatenate(
            [
                grad_result * from_state,
                to_state * x_in,
                grad_weighted * x_in,
                jnp.broadcast_to(
                    jnp.sum(grad_next * state_half.astype(f32), axis=0, keepdims=True), (8, INNER)
                ),
            ],
            axis=0,
        )
    )
    grad_entry = sums[:SPAN]
    grad_tail = sums[SPAN : 2 * SPAN]
    grad_rates = sums[2 * SPAN : 3 * SPAN] + grad_tail * tail
    from_tail = grad_tail * tail * rates
    grad_total = (
        jnp.sum(from_tail, axis=0, keepdims=True) + sums[3 * SPAN : 3 * SPAN + 1] * keep
    )
    grad_cumulative = grad_cumulative + grad_entry * entry - from_tail
    grad_cumulative = grad_cumulative + jnp.where(head_row == SPAN - 1, grad_total, 0.0)
    above = (row_index((SPAN, SPAN)) <= lane_index((SPAN, SPAN))).astype(f32)
    grad_decay = jnp.dot(above, grad_cumulative, precision=highest, preferred_element_type=f32)
    grad_rates = grad_rates + grad_decay * rate_rows[1:2]
    out_ref[:, COL_STEP:] = jnp.where(
        lane < HEADS_DEV, grad_rates * jax.nn.sigmoid(shifted), 0.0
    ).astype(bf16)
    grad_x = grad_weighted * rates_wide + to_state * tail_rates + skip_ref[0:1] * grad_result
    grad_state[...] = grad_next * keep_wide + contract_first(out_half, grad_entered)

    conv_sigmoid = jax.nn.sigmoid(convolved)
    grad_conv = jnp.concatenate([grad_x, grad_in_state, grad_out_state], axis=1) * (
        conv_sigmoid * (1.0 + convolved * (1.0 - conv_sigmoid))
    )
    row = start + row_index((SPAN, 1))
    position = row - jnp.where(row >= first_len, first_len, 0)
    later_row = start + SPAN + row_index((8, 1))
    later_position = later_row - jnp.where(later_row >= first_len, first_len, 0)
    later = next_rows[...]
    bottom = row_index((8, 1))
    grad_signal = taps_ref[3:4] * grad_conv
    for offset in range(1, CONV):
        moved = pltpu.roll(jnp.where(position >= offset, grad_conv, 0.0), SPAN - offset, 0)
        edge = pltpu.roll(jnp.where(later_position >= offset, later, 0.0), 8 - offset, 0)
        edge = jnp.where(bottom >= 8 - offset, edge, moved[SPAN - 8 :])
        moved = jnp.concatenate([moved[: SPAN - 8], edge], axis=0)
        grad_signal = grad_signal + taps_ref[3 - offset : 4 - offset] * moved
    next_rows[...] = grad_conv[:8]
    out_ref[:, COL_INNER:COL_GATE] = grad_signal[:, :INNER].astype(bf16)
    out_ref[:, COL_BC:COL_STEP] = grad_signal[:, INNER:].astype(bf16)
    out_ref[:, :COL_INNER] = grad_query_ref[...]
    out_ref[:, COL_K:COL_V] = grad_key_ref[...]
    out_ref[:, COL_V:COL_BC] = grad_value_ref[...]


def whole(shape):
    return pl.BlockSpec(shape, lambda i: (0,) * len(shape))


smem = pl.BlockSpec(memory_space=pltpu.SMEM)


def scan_forward(lengths, proj, taps, rate_rows, skip_rows):
    length_all = proj.shape[0]
    spans = length_all // SPAN

    def rows(width):
        return pl.BlockSpec((SPAN, width), lambda i: (i, 0))

    return pl.pallas_call(
        scan_forward_kernel,
        grid=(spans,),
        in_specs=[smem, rows(IN_COLS), whole(taps.shape), whole(rate_rows.shape), whole(skip_rows.shape)],
        out_specs=[
            rows(INNER),
            rows(INNER),
            pl.BlockSpec((8, SPAN), lambda i: (i, 0)),
            rows(CONVOLVED),
            pl.BlockSpec((1, STATE, INNER), lambda i: (i, 0, 0)),
        ],
        out_shape=[
            jax.ShapeDtypeStruct((length_all, INNER), bf16),
            jax.ShapeDtypeStruct((length_all, INNER), bf16),
            jax.ShapeDtypeStruct((8 * spans, SPAN), f32),
            jax.ShapeDtypeStruct((length_all, CONVOLVED), f32),
            jax.ShapeDtypeStruct((spans, STATE, INNER), bf16),
        ],
        scratch_shapes=[pltpu.VMEM((STATE, INNER), f32), pltpu.VMEM((8, CONVOLVED), f32)],
        compiler_params=pltpu.CompilerParams(vmem_limit_bytes=VMEM_ALL),
        cost_estimate=pl.CostEstimate(flops=10**10, bytes_accessed=10**7, transcendentals=10**6),
        name="scan_forward",
    )(lengths, proj, taps, rate_rows, skip_rows)


def scan_backward(
    lengths, proj, convolved, scanned, states, upstream, scales, grad_qkv, taps, rate_rows, skip_rows
):
    length_all = proj.shape[0]
    spans = length_all // SPAN

    def rows(width):
        return pl.BlockSpec((SPAN, width), lambda i: (spans - 1 - i, 0))

    return pl.pallas_call(
        scan_backward_kernel,
        grid=(spans,),
        in_specs=[
            smem,
            rows(IN_COLS),
            rows(CONVOLVED),
            rows(INNER),
            pl.BlockSpec((1, STATE, INNER), lambda i: (spans - 1 - i, 0, 0)),
            rows(HEAD + INNER),
            rows(2),
            rows(HEAD),
            rows(HEAD),
            rows(HEAD),
            whole(taps.shape),
            whole(rate_rows.shape),
            whole(skip_rows.shape),
        ],
        out_specs=rows(IN_COLS),
        out_shape=jax.ShapeDtypeStruct((length_all, IN_COLS), bf16),
        scratch_shapes=[pltpu.VMEM((STATE, INNER), f32), pltpu.VMEM((8, CONVOLVED), f32)],
        compiler_params=pltpu.CompilerParams(vmem_limit_bytes=VMEM_ALL),
        cost_estimate=pl.CostEstimate(flops=17 * 10**9, bytes_accessed=10**7, transcendentals=10**6),
        name="scan_backward",
    )(lengths, proj, convolved, scanned, states, upstream, scales, *grad_qkv, taps, rate_rows, skip_rows)


QUERY_ROWS = 256
score_scale = HEAD ** (-0.5)


def turn(values, cosine, sine):
    return values * cosine + pltpu.roll(values, HEAD // 2, 1) * sine


def allowed_scores(query_rot, key_rot, first_row, first_len):
    scores = contract_last(query_rot, key_rot) * score_scale
    rows = first_row + row_index(scores.shape)
    lanes = lane_index(scores.shape)
    allowed = (lanes <= rows) & ((lanes >= first_len) | (rows < first_len))
    return jnp.where(allowed, scores, masked_score)


def attention_forward_kernel(
    lengths_ref, query_ref, key_ref, value_ref, cosine_ref, sine_ref, out_ref, totals_ref
):
    first_len = lengths_ref[0, 0]
    length_all = query_ref.shape[0]
    key_rot = turn(key_ref[...].astype(f32), cosine_ref[...], sine_ref[...]).astype(bf16)
    for first in range(0, length_all, QUERY_ROWS):
        block = slice(first, first + QUERY_ROWS)
        seen = first + QUERY_ROWS
        query_rot = turn(
            query_ref[block].astype(f32), cosine_ref[block], sine_ref[block]
        ).astype(bf16)
        scores = allowed_scores(query_rot, key_rot[:seen], first, first_len)
        peak = jnp.max(scores, axis=1, keepdims=True)
        exponent = jnp.exp(scores - peak)
        total = jnp.sum(exponent, axis=1, keepdims=True)
        probs = (exponent * (1.0 / total)).astype(bf16)
        out_ref[block] = product(probs, value_ref[:seen]).astype(bf16)
        totals_ref[block] = peak + jnp.log(total)


def attention_backward_kernel(
    lengths_ref,
    query_ref,
    key_ref,
    value_ref,
    cosine_ref,
    sine_ref,
    upstream_ref,
    totals_ref,
    grad_query_ref,
    grad_key_ref,
    grad_value_ref,
    key_sum,
    value_sum,
):
    first_len = lengths_ref[0, 0]
    length_all = query_ref.shape[0]
    key_rot = turn(key_ref[...].astype(f32), cosine_ref[...], sine_ref[...]).astype(bf16)
    key_sum[...] = jnp.zeros_like(key_sum)
    value_sum[...] = jnp.zeros_like(value_sum)
    for first in range(0, length_all, QUERY_ROWS):
        block = slice(first, first + QUERY_ROWS)
        seen = first + QUERY_ROWS
        cosine = cosine_ref[block]
        sine = sine_ref[block]
        query_rot = turn(query_ref[block].astype(f32), cosine, sine).astype(bf16)
        probs = jnp.exp(
            allowed_scores(query_rot, key_rot[:seen], first, first_len) - totals_ref[block]
        )
        upstream = upstream_ref[block]
        grad_probs = contract_last(upstream, value_ref[:seen])
        delta = jnp.sum(probs * grad_probs, axis=1, keepdims=True)
        grad_scores = (probs * (grad_probs - delta)).astype(bf16)
        grad_query_ref[block] = turn(
            product(grad_scores, key_rot[:seen]) * score_scale, cosine, -sine
        ).astype(bf16)
        key_sum[:seen] += contract_first(grad_scores, query_rot)
        value_sum[:seen] += contract_first(probs.astype(bf16), upstream)
    grad_key_ref[...] = turn(
        key_sum[...] * score_scale, cosine_ref[...], -sine_ref[...]
    ).astype(bf16)
    grad_value_ref[...] = value_sum[...].astype(bf16)


def head_block(length_all, column):
    return pl.BlockSpec((length_all, HEAD), lambda i: (0, column // HEAD))


def attention_forward(lengths, proj, cosine, sine):
    length_all = proj.shape[0]
    block = head_block(length_all, 0)
    return pl.pallas_call(
        attention_forward_kernel,
        grid=(1,),
        in_specs=[
            smem,
            block,
            head_block(length_all, COL_K),
            head_block(length_all, COL_V),
            block,
            block,
        ],
        out_specs=[block, pl.BlockSpec((length_all, 1), lambda i: (0, 0))],
        out_shape=[
            jax.ShapeDtypeStruct((length_all, HEAD), bf16),
            jax.ShapeDtypeStruct((length_all, 1), f32),
        ],
        compiler_params=pltpu.CompilerParams(vmem_limit_bytes=VMEM_ALL),
        name="attention_forward",
    )(lengths, proj, proj, proj, cosine, sine)


def attention_backward(lengths, proj, cosine, sine, upstream, totals):
    length_all = proj.shape[0]
    block = head_block(length_all, 0)
    return pl.pallas_call(
        attention_backward_kernel,
        grid=(1,),
        in_specs=[
            smem,
            block,
            head_block(length_all, COL_K),
            head_block(length_all, COL_V),
            block,
            block,
            block,
            pl.BlockSpec((length_all, 1), lambda i: (0, 0)),
        ],
        out_specs=[block, block, block],
        out_shape=[jax.ShapeDtypeStruct((length_all, HEAD), bf16)] * 3,
        scratch_shapes=[pltpu.VMEM((length_all, HEAD), f32)] * 2,
        compiler_params=pltpu.CompilerParams(vmem_limit_bytes=VMEM_ALL),
        name="attention_backward",
    )(lengths, proj, proj, proj, cosine, sine, upstream, totals)


VMEM_LIMIT = 48 * 1024 * 1024


def input_forward_kernel(left_ref, mask_ref, weight_ref, lower_ref, raise_ref, out_ref, lowered_ref):
    @pl.when(pl.program_id(0) == 0)
    def _():
        lowered_ref[...] = (product(left_ref[...], lower_ref[...]) * mask_ref[...]).astype(bf16)

    out_ref[...] = (
        product(left_ref[...], weight_ref[...]) + product(lowered_ref[...], raise_ref[...])
    ).astype(bf16)


def fixed(shape, *place):
    return pl.BlockSpec(shape, lambda i: place)


def input_forward(left, mask, gathered, raising_all):
    rows, depth = left.shape
    tile = 256
    return pl.pallas_call(
        input_forward_kernel,
        grid=(IN_COLS // tile,),
        in_specs=[
            fixed((rows, depth), 0, 0),
            fixed((rows, ADAPTERS), 0, 0),
            pl.BlockSpec((depth, tile), lambda i: (0, i)),
            fixed((depth, ADAPTERS), 0, IN_COLS // ADAPTERS),
            pl.BlockSpec((ADAPTERS, tile), lambda i: (0, i)),
        ],
        out_specs=[
            pl.BlockSpec((rows, tile), lambda i: (0, i)),
            fixed((rows, ADAPTERS), 0, 0),
        ],
        out_shape=[
            jax.ShapeDtypeStruct((rows, IN_COLS), bf16),
            jax.ShapeDtypeStruct((rows, ADAPTERS), bf16),
        ],
        compiler_params=pltpu.CompilerParams(vmem_limit_bytes=VMEM_ALL),
        cost_estimate=pl.CostEstimate(flops=9 * 10**9, bytes_accessed=10**7, transcendentals=0),
        name="input_forward",
    )(left, mask, gathered, gathered, raising_all)


def input_backward_kernel(
    upstream_ref, left_ref, lowered_ref, mask_ref, weight_ref, raise_ref, out_ref, late_ref, scaled
):
    step = pl.program_id(0)

    @pl.when(step == 0)
    def _():
        scaled[...] = (contract_last(upstream_ref[...], raise_ref[...]) * mask_ref[...]).astype(bf16)
        grad_raise = contract_first(lowered_ref[...], upstream_ref[...])
        for shard in range(DP):
            late_ref[shard, 128:] = jnp.concatenate(
                [
                    grad_raise[8 * shard : 8 * shard + 8, 128 * i : 128 * i + 128]
                    for i in range(IN_COLS // 128)
                ]
                + [jnp.zeros((16, 128), f32)],
                axis=0,
            ).astype(bf16)

    out_ref[...] = (
        contract_last(upstream_ref[...], weight_ref[:, :IN_COLS])
        + contract_last(scaled[...], weight_ref[:, IN_COLS : IN_COLS + ADAPTERS])
    ).astype(bf16)
    grad_lower = contract_first(left_ref[...], scaled[...]).astype(bf16)
    shards = grad_lower.shape[0] // 128
    for shard in range(shards):
        late_ref[shards * step + shard, :128] = grad_lower[128 * shard : 128 * shard + 128]


def input_backward(upstream, left, lowered, mask, gathered, raising_all):
    rows, depth = left.shape
    tile = 512
    return pl.pallas_call(
        input_backward_kernel,
        grid=(depth // tile,),
        in_specs=[
            fixed((rows, IN_COLS), 0, 0),
            pl.BlockSpec((rows, tile), lambda i: (0, i)),
            fixed((rows, ADAPTERS), 0, 0),
            fixed((rows, ADAPTERS), 0, 0),
            pl.BlockSpec((tile, gathered.shape[1]), lambda i: (i, 0)),
            fixed((ADAPTERS, IN_COLS), 0, 0),
        ],
        out_specs=[
            pl.BlockSpec((rows, tile), lambda i: (0, i)),
            fixed((DP, 256, 128), 0, 0, 0),
        ],
        out_shape=[
            jax.ShapeDtypeStruct((rows, depth), bf16),
            jax.ShapeDtypeStruct((DP, 256, 128), bf16),
        ],
        scratch_shapes=[pltpu.VMEM((rows, ADAPTERS), bf16)],
        compiler_params=pltpu.CompilerParams(vmem_limit_bytes=VMEM_ALL),
        cost_estimate=pl.CostEstimate(flops=10**10, bytes_accessed=10**7, transcendentals=0),
        name="input_backward",
    )(upstream, left, lowered, mask, gathered, raising_all)


def ffn_kernel(
    left_ref,
    cotangent_ref,
    mask_ref,
    gate_ref,
    up_ref,
    lower_ref,
    raise_gate_ref,
    raise_up_ref,
    down_ref,
    lower_down_ref,
    raise_down_ref,
    left_down_ref,
    grad_gate_ref,
    grad_up_ref,
    grad_left_ref,
    lowered_ref,
    scaled_ref,
    scaled_down_ref,
    grad_left,
    grad_lowered,
):
    step = pl.program_id(0)
    model = left_ref.shape[1]

    @pl.when(step == 0)
    def _():
        lowered_ref[...] = (product(left_ref[...], lower_ref[...]) * mask_ref[...]).astype(bf16)
        scaled_down_ref[...] = (
            contract_last(cotangent_ref[...], raise_down_ref[...]) * mask_ref[...]
        ).astype(bf16)
        grad_left[...] = jnp.zeros_like(grad_left)
        grad_lowered[...] = jnp.zeros_like(grad_lowered)

    lowered = lowered_ref[...]
    gate = product(left_ref[...], gate_ref[...]) + product(lowered, raise_gate_ref[...])
    up = product(left_ref[...], up_ref[...]) + product(lowered, raise_up_ref[...])
    shards = range(0, down_ref.shape[0], 128)
    grad_act = contract_last(
        scaled_down_ref[...],
        jnp.concatenate([lower_down_ref[row : row + 64] for row in shards], axis=0),
    )
    for c in range(2):
        grad_act = grad_act + contract_last(
            cotangent_ref[:, c * model // 2 : (c + 1) * model // 2],
            jnp.concatenate([down_ref[row + 64 * c : row + 64 * c + 64] for row in shards], axis=0),
        )
    sigmoid = jax.nn.sigmoid(gate)
    silu = gate * sigmoid
    left_down_ref[...] = (silu * up).astype(bf16)
    grad_up = (grad_act * silu).astype(bf16)
    grad_gate = (grad_act * up * (sigmoid * (1.0 + gate * (1.0 - sigmoid)))).astype(bf16)
    grad_gate_ref[...] = grad_gate
    grad_up_ref[...] = grad_up
    grad_left[...] += contract_last(grad_gate, gate_ref[...]) + contract_last(grad_up, up_ref[...])
    grad_lowered[...] += contract_last(grad_gate, raise_gate_ref[...]) + contract_last(
        grad_up, raise_up_ref[...]
    )

    @pl.when(step == pl.num_programs(0) - 1)
    def _():
        scaled = (grad_lowered[...] * mask_ref[...]).astype(bf16)
        scaled_ref[...] = scaled
        grad_left_ref[...] = (grad_left[...] + contract_last(scaled, lower_ref[...])).astype(bf16)


def ffn_forward_backward(left, cotangent, mask, gathered, gu_raise, down_raise):
    rows, model = left.shape
    tile = 512
    tiles = UNITS // tile
    fold = model // 2
    first = fold // tile
    lower = (fold + 2 * UNITS) // ADAPTERS
    stacked = tile // 64 * 128
    whole_rows = fixed((rows, model), 0, 0)
    adapter_rows = fixed((rows, ADAPTERS), 0, 0)
    return pl.pallas_call(
        ffn_kernel,
        grid=(tiles,),
        in_specs=[
            whole_rows,
            whole_rows,
            adapter_rows,
            pl.BlockSpec((model, tile), lambda i: (0, first + i)),
            pl.BlockSpec((model, tile), lambda i: (0, first + tiles + i)),
            fixed((model, ADAPTERS), 0, lower),
            pl.BlockSpec((ADAPTERS, tile), lambda i: (0, i)),
            pl.BlockSpec((ADAPTERS, tile), lambda i: (0, tiles + i)),
            pl.BlockSpec((stacked, fold), lambda i: (i, 0)),
            pl.BlockSpec((stacked, ADAPTERS), lambda i: (i, lower + 1)),
            fixed((ADAPTERS, model), 0, 0),
        ],
        out_specs=[pl.BlockSpec((rows, tile), lambda i: (0, i))] * 3
        + [whole_rows, adapter_rows, adapter_rows, adapter_rows],
        out_shape=[jax.ShapeDtypeStruct((rows, UNITS), bf16)] * 3
        + [jax.ShapeDtypeStruct((rows, model), bf16)]
        + [jax.ShapeDtypeStruct((rows, ADAPTERS), bf16)] * 3,
        scratch_shapes=[pltpu.VMEM((rows, model), f32), pltpu.VMEM((rows, ADAPTERS), f32)],
        compiler_params=pltpu.CompilerParams(vmem_limit_bytes=VMEM_LIMIT),
        cost_estimate=pl.CostEstimate(flops=12 * 10**9, bytes_accessed=10**7, transcendentals=10**6),
        name="ffn",
    )(
        left,
        cotangent,
        mask,
        gathered,
        gathered,
        gathered,
        gu_raise,
        gu_raise,
        gathered,
        gathered,
        down_raise,
    )


def per_device(
    tokens,
    cotangent,
    seq_lengths,
    adapter_ids,
    norm_gain,
    ffn_gain,
    gate_gain,
    conv_weight,
    conv_bias,
    dt_bias,
    decay_log,
    skip_gain,
    frozen_input_weight,
    input_adapter_lower,
    input_adapter_upper,
    frozen_output_weight,
    output_adapter_lower,
    output_adapter_upper,
    frozen_gate_up_weight,
    gate_up_adapter_lower,
    gate_up_adapter_upper,
    frozen_down_weight,
    down_adapter_lower,
    down_adapter_upper,
):
    s = lax.axis_index("sp")
    d = lax.axis_index("dp")
    y = s // X_PAIR
    x = s % X_PAIR
    tok_count = tokens.shape[0]
    group_len = tok_count * SEQ
    first_len = seq_lengths[0, 0]
    set_ids = adapter_ids[0]

    def adapter_mask(token_index):
        resident = jnp.where(token_index >= first_len, set_ids[1], set_ids[0])
        return jnp.arange(ADAPTERS)[None, :] // ADAPTER_RANK == resident[:, None]

    group_index = jnp.arange(group_len)
    segment = (group_index >= first_len).astype(jnp.int32)
    position = group_index - first_len * segment
    mask_all = adapter_mask(group_index)
    ring_blocks = X_PAIR * ((y + jnp.arange(Y_RING)) % Y_RING) + x
    ring_index = (ring_blocks[:, None] * tok_count + jnp.arange(tok_count)[None, :]).reshape(-1)
    mask_ring = adapter_mask(ring_index)

    def head_columns(values):
        lead = values.shape[:-1]
        grouped = values.reshape(lead + (12, Y_RING, M_HEAD))
        grouped = lax.dynamic_slice_in_dim(grouped, HEADS_DEV * x, HEADS_DEV, len(lead))
        grouped = lax.dynamic_index_in_dim(grouped, y, len(lead) + 1, keepdims=False)
        return grouped.reshape(lead + (INNER,))

    def head_items(values):
        lead = values.shape[:-1]
        grouped = values.reshape(lead + (12, Y_RING))
        grouped = lax.dynamic_slice_in_dim(grouped, HEADS_DEV * x, HEADS_DEV, len(lead))
        return lax.dynamic_index_in_dim(grouped, y, len(lead) + 1, keepdims=False)

    kv_head = s // (H_Q // H_KV)

    def gather_rows(rows):
        return lax.all_gather(rows, "dp", axis=0, tiled=True)

    place = jnp.reshape(s, (1,)).astype(jnp.int32)
    in_all = gather_rows(
        pack(
            pack_input_kernel,
            (place, frozen_input_weight, input_adapter_lower, sixteen_rows(input_adapter_upper)),
            (128, IN_COLS + 2 * ADAPTERS),
        )
    )
    in_raise = raising([in_all[:, IN_COLS + ADAPTERS :]], IN_COLS)

    hidden = tokens.astype(f32)
    normed, norm_back = jax.vjp(partial(rms_scale, scale_gain=norm_gain), hidden)
    normed, frozen_output_weight, frozen_down_weight = lax.optimization_barrier(
        (normed.astype(bf16), frozen_output_weight, frozen_down_weight)
    )
    left_in = gather_rings(normed, y, x)

    out_rows = jnp.concatenate([frozen_output_weight, output_adapter_lower], axis=1)
    piece = lax.dynamic_slice_in_dim(out_rows, 64 * y, 64, 0)
    spread = jnp.zeros_like(piece)
    for k in range(1, Y_RING):
        block = lax.dynamic_slice_in_dim(out_rows, 64 * ((y + k) % Y_RING), 64, 0)
        pairs = [((i // 2) * SEQ + i, ((i // 2 + k) % Y_RING) * SEQ + i) for i in range(SEQ)]
        spread = spread + lax.ppermute(block, ("dp", "sp"), pairs)
    own_rows = (d >= Y_RING) | (d == y)
    model = frozen_output_weight.shape[1]
    out_all = gather_rows(
        pack(
            pack_output_kernel,
            (jnp.where(own_rows, piece, spread), sixteen_rows(output_adapter_upper)),
            (64, model + 3 * ADAPTERS),
        )
    )
    out_weight = out_all[:, : model + ADAPTERS]
    out_raise = raising(
        [out_all[:, model + 128 * c : model + 128 * c + 128] for c in (1, 2)], model
    )

    fold = model // 2
    ffn_all = gather_rows(
        pack(
            pack_ffn_kernel,
            (
                place,
                frozen_gate_up_weight,
                gate_up_adapter_lower,
                sixteen_rows(gate_up_adapter_upper),
                frozen_down_weight,
                down_adapter_lower,
                sixteen_rows(down_adapter_upper),
            ),
            (128, fold + 2 * UNITS + 4 * ADAPTERS),
        )
    )
    edge = fold + 2 * UNITS + 2 * ADAPTERS
    gu_raise = raising([ffn_all[:, edge : edge + ADAPTERS]], 2 * UNITS)
    down_raise = raising([ffn_all[:, edge + ADAPTERS :]], model)

    def masked(lowered, mask):
        return jnp.where(mask, lowered, 0.0).astype(bf16)

    def forward(left, weight, raising, mask):
        both = product(left, weight)
        width = raising.shape[1]
        lowered = masked(both[:, width:], mask)
        return both[:, :width] + product(lowered, raising), lowered

    def backward(left, lowered, upstream, weight, raising, mask):
        gradient_lowered = masked(contract_last(upstream, raising), mask)
        grad_raise = contract_first(lowered, upstream)
        grad_lower = contract_first(left, gradient_lowered)
        grad_left = contract_last(jnp.concatenate([upstream, gradient_lowered], axis=1), weight)
        return grad_left, grad_lower, grad_raise

    left_in, cot_own = lax.optimization_barrier((left_in, cotangent))
    cot_below = hop(cot_own, up)
    cot_above = hop(cot_own, down)
    projected, lower_in = input_forward(left_in, mask_all.astype(f32), in_all, in_raise)

    projected, cot_below, cot_above = lax.optimization_barrier((projected, cot_below, cot_above))
    half = tok_count // 2
    cot_far = hop(cot_below[:half], up), hop(cot_above[half:], down)
    taps = jnp.concatenate(
        [
            jnp.concatenate([head_columns(conv_weight[:, :D_SSM]), conv_weight[:, D_SSM:]], axis=1),
            jnp.concatenate([head_columns(conv_bias[:D_SSM]), conv_bias[D_SSM:]])[None],
            jnp.zeros((3, INNER + 2 * STATE), f32),
        ],
        axis=0,
    )
    rate_rows = jnp.pad(
        jnp.stack([head_items(dt_bias), -jnp.exp(head_items(decay_log))]),
        ((0, 6), (0, 128 - HEADS_DEV)),
    )
    skip_rows = jnp.pad(
        jnp.stack([jnp.repeat(head_items(skip_gain), M_HEAD), head_columns(gate_gain)]),
        ((0, 6), (0, 0)),
    )
    gain_pair = lax.dynamic_index_in_dim(
        gate_gain.reshape(12, Y_RING, M_HEAD), y, 1, keepdims=False
    ).reshape(1, -1)
    cosine_table, sine_table = rotary_tables(position)
    gated, scanned, squares, convolved, states = scan_forward(
        seq_lengths, projected, taps, rate_rows, skip_rows
    )
    squares, cot_far = lax.optimization_barrier((squares, cot_far))
    attended, log_totals = attention_forward(seq_lengths, projected, cosine_table, sine_table)
    squares = sum_ring_small(squares.reshape(SEQ, 8, tok_count)[:, 0])
    inverse = lax.rsqrt((squares + hop(squares, side)) / D_SSM + epsilon)
    mixed = jnp.concatenate([attended, gated], axis=1)
    cot_ring = jnp.concatenate([cot_own, cot_above, *cot_far, cot_below], axis=0)

    def to_ring(values):
        doubled = jnp.concatenate([values, values], axis=0)
        rolled = lax.dynamic_slice_in_dim(doubled, X_PAIR * tok_count * y, group_len, 0)
        return rolled.reshape(Y_RING, X_PAIR, tok_count, -1)

    def from_ring(values):
        flat = values.reshape(group_len, -1)
        doubled = jnp.concatenate([flat, flat], axis=0)
        start = X_PAIR * tok_count * ((Y_RING - y) % Y_RING)
        return lax.dynamic_slice_in_dim(doubled, start, group_len, 0)

    ring_len = Y_RING * tok_count
    mixed_ring = to_ring(mixed)
    kept = lax.dynamic_index_in_dim(mixed_ring, x, 1, keepdims=False).reshape(ring_len, SLICE)
    other = lax.dynamic_index_in_dim(mixed_ring, 1 - x, 1, keepdims=False).reshape(ring_len, SLICE)
    received = hop(other, side)
    low = jnp.where(x == 0, kept, received)
    high = jnp.where(x == 0, received, kept)
    gated_pair = jnp.concatenate([low[:, HEAD:], high[:, HEAD:]], axis=1).astype(f32)
    inverse_ring = lax.dynamic_index_in_dim(
        to_ring(inverse.reshape(-1, 1)), x, 1, keepdims=False
    ).reshape(ring_len, 1)
    left_out = jnp.concatenate(
        [low[:, :HEAD], high[:, :HEAD], (gated_pair * inverse_ring * gain_pair).astype(bf16)],
        axis=1,
    )
    branch_part, lower_out = forward(left_out, out_weight, out_raise, mask_ring)
    (branch,) = scatter_ring(branch_part)
    residual = hidden + branch
    normed_ffn, ffn_norm_back = jax.vjp(partial(rms_scale, scale_gain=ffn_gain), residual)
    left_gu = gather_ring(normed_ffn.astype(bf16))
    left_down, grad_gate_half, grad_up_half, grad_gu_part, lower_gu, scaled_gu, scaled_down = (
        ffn_forward_backward(
            left_gu, cot_ring, mask_ring.astype(f32), ffn_all, gu_raise, down_raise
        )
    )
    left_down, ffn_all = lax.optimization_barrier((left_down, ffn_all))
    folded = ffn_all[:, :fold].reshape(DP, 2, 64, fold)
    lowers = ffn_all[:, fold + 2 * UNITS + ADAPTERS : edge].reshape(DP, 2, 64, ADAPTERS)
    down_weight = jnp.concatenate(
        [
            folded[:, 0].reshape(UNITS, -1),
            folded[:, 1].reshape(UNITS, -1),
            lowers[:, 0].reshape(UNITS, -1),
        ],
        axis=1,
    )
    ffn_part, lower_down = forward(left_down, down_weight, down_raise, mask_ring)
    grad_a_down = contract_first(left_down, scaled_down)
    grad_b_down = contract_first(lower_down, cot_ring)
    grad_a_gu = contract_first(left_gu, scaled_gu)
    grad_b_gu = contract_first(
        lower_gu, jnp.concatenate([grad_gate_half, grad_up_half], axis=1)
    )
    (grad_left_gu,) = scatter_ring(grad_gu_part)
    (grad_resid_norm,) = ffn_norm_back(grad_left_gu)
    grad_residual = cotangent.astype(f32) + grad_resid_norm
    grad_ring = gather_ring(grad_residual.astype(bf16))
    grad_mixed, grad_a_out, grad_b_out = backward(
        left_out, lower_out, grad_ring, out_weight, out_raise, mask_ring
    )
    early = jnp.concatenate(
        [
            grad_a_out.astype(bf16).reshape(DP, -1, 128),
            blocks_of(grad_b_out.astype(bf16)),
            grad_a_gu.astype(bf16).reshape(DP, -1, 128),
            blocks_of(grad_b_gu.astype(bf16)),
            grad_a_down.astype(bf16).reshape(DP, -1, 128),
            blocks_of(grad_b_down.astype(bf16)),
        ],
        axis=1,
    )
    grad_mixed = grad_mixed.astype(bf16)
    low = jnp.concatenate([grad_mixed[:, :HEAD], grad_mixed[:, 2 * HEAD : 2 * HEAD + INNER]], axis=1)
    high = jnp.concatenate([grad_mixed[:, HEAD : 2 * HEAD], grad_mixed[:, 2 * HEAD + INNER :]], axis=1)
    kept = jnp.where(x == 0, low, high)
    received, grad_mixed = lax.optimization_barrier(
        (hop(jnp.where(x == 0, high, low), side), grad_mixed)
    )
    first = jnp.where(x == 0, kept, received).reshape(Y_RING, 1, tok_count, SLICE)
    second = jnp.where(x == 0, received, kept).reshape(Y_RING, 1, tok_count, SLICE)
    head_grads, early, ffn_part = lax.optimization_barrier(
        (from_ring(jnp.concatenate([first, second], axis=1)), halve_cores(early, d), ffn_part)
    )
    early = halve_neighbours(early, d)
    (ffn,) = scatter_ring(ffn_part)
    layer_out = (residual + ffn).astype(bf16)
    slope_ring = jnp.sum(
        grad_mixed[:, 2 * HEAD :].astype(f32) * gain_pair * gated_pair, axis=1
    ).reshape(Y_RING, tok_count)
    slope_own = sum_ring_small(
        lax.dynamic_slice_in_dim(
            jnp.concatenate([slope_ring, slope_ring], axis=0), (Y_RING - y) % Y_RING, Y_RING, 0
        )
    )
    slope_mate = hop(slope_own, side)
    slope = jnp.stack(
        [jnp.where(x == 0, slope_own, slope_mate), jnp.where(x == 0, slope_mate, slope_own)],
        axis=1,
    ).reshape(SEQ, tok_count)
    scales = jnp.stack(
        [inverse.reshape(-1), (inverse * inverse * inverse * slope / D_SSM).reshape(-1)], axis=1
    )
    grad_qkv = attention_backward(
        seq_lengths, projected, cosine_table, sine_table, head_grads, log_totals
    )
    grad_qkv, early = lax.optimization_barrier((grad_qkv, early))
    early = scatter_shards(early, Z_RINGS)
    grad_projected = scan_backward(
        seq_lengths,
        projected,
        convolved,
        scanned,
        states,
        head_grads,
        scales,
        grad_qkv,
        taps,
        rate_rows,
        skip_rows,
    )
    grad_projected, layer_out = lax.optimization_barrier((grad_projected, layer_out))
    grad_left_part, late = input_backward(
        grad_projected, left_in, lower_in, mask_all.astype(f32), in_all, in_raise
    )
    grad_left_part, early = lax.optimization_barrier((grad_left_part, early))
    late = halve_cores(late, d)
    grad_left_parts, late = lax.optimization_barrier(
        (exchange_seq(grad_left_part), scatter_shards(late, CHIPS))
    )
    grad_left = jnp.sum(grad_left_parts.astype(f32), axis=0)
    (grad_hidden_norm,) = norm_back(grad_left)
    grad_tokens = (grad_residual + grad_hidden_norm).astype(bf16)

    a_in_own = late[:128]
    b_in_own = row_from_blocks(late[128:240])
    a_out_block = early[:64].astype(bf16)
    b_out_own = early[64:192]
    a_gu_own = early[192:320]
    b_gu_own = early[320:448]
    a_down_own = early[448:512]
    b_down_own = early[512:640]
    zero_rows = jnp.zeros((256, 128), f32)
    a_out_own = lax.dynamic_update_slice_in_dim(
        zero_rows, jnp.where(own_rows, early[:64], 0.0), 64 * y, 0
    )
    for k in range(1, Y_RING):
        pairs = [(((i // 2 + k) % Y_RING) * SEQ + i, (i // 2) * SEQ + i) for i in range(SEQ)]
        moved = lax.ppermute(a_out_block, ("dp", "sp"), pairs)
        a_out_own = a_out_own + lax.dynamic_update_slice_in_dim(
            zero_rows, moved.astype(f32), 64 * ((y + k) % Y_RING), 0
        )
    a_down_own = lax.dynamic_update_slice_in_dim(zero_rows, a_down_own, 64 * y, 0)
    b_gu_full = lax.dynamic_update_slice_in_dim(
        jnp.zeros((8, 2 * DP, Y_RING, 64), f32),
        row_from_blocks(b_gu_own).reshape(8, 2 * DP, 1, 64),
        y,
        2,
    ).reshape(512, 128)

    def spread_heads(part, width):
        return lax.dynamic_update_slice(
            jnp.zeros((8, 12, Y_RING, width), f32),
            part.reshape(8, HEADS_DEV, 1, width),
            (0, HEADS_DEV * x, y, 0),
        ).reshape(8, -1)

    kv_width = H_KV * HEAD
    b_in_full = jnp.concatenate(
        [
            lax.dynamic_update_slice_in_dim(
                jnp.zeros((8, EDGE_INNER), f32), b_in_own[:, COL_Q:COL_INNER], s * HEAD, 1
            ),
            spread_heads(b_in_own[:, COL_INNER:COL_GATE], M_HEAD),
            lax.dynamic_update_slice_in_dim(
                jnp.zeros((8, kv_width), f32), b_in_own[:, COL_K:COL_V], kv_head * HEAD, 1
            ),
            lax.dynamic_update_slice_in_dim(
                jnp.zeros((8, kv_width), f32), b_in_own[:, COL_V:COL_BC], kv_head * HEAD, 1
            ),
            b_in_own[:, COL_BC:COL_STEP],
            spread_heads(b_in_own[:, COL_GATE:COL_K], M_HEAD),
            spread_heads(b_in_own[:, COL_STEP : COL_STEP + HEADS_DEV], 1),
            jnp.zeros((8, 80), f32),
        ],
        axis=1,
    )
    full = jnp.concatenate(
        [
            a_in_own,
            b_in_full.reshape(-1, 128),
            a_out_own,
            b_out_own,
            a_gu_own,
            b_gu_full,
            a_down_own,
            b_down_own,
        ],
        axis=0,
    )
    full = jnp.pad(full, ((0, (-full.shape[0]) % 128), (0, 0)))
    full = gather_seq(scatter_seq(full).astype(bf16)).astype(f32)
    out_a_in = full[:128]
    out_b_in = full[128:648].reshape(8, -1)[:, : EDGE_STEP + M_HEADS]
    full = full[648:]
    out_a_out = full[:256]
    out_b_out = row_from_blocks(full[256:384])
    out_a_gu = full[384:512]
    out_b_gu = full[512:1024].reshape(8, -1)
    out_a_down = full[1024:1280]
    out_b_down = row_from_blocks(full[1280:1408])
    return (
        layer_out,
        grad_tokens,
        out_a_in,
        out_b_in,
        out_a_out,
        out_b_out,
        out_a_gu,
        out_b_gu,
        out_a_down,
        out_b_down,
    )


def solution(mesh):
    rows = P("dp", None)
    both = P(("dp", "sp"), None)
    in_specs = (both, both) + (rows,) * 2 + (P(),) * 8 + (rows,) * 12
    out_specs = (both, both) + (rows,) * 8
    return jax.shard_map(
        per_device, mesh=mesh, in_specs=in_specs, out_specs=out_specs, check_vma=False
    )
```

```python
from functools import partial

import jax
import jax.numpy as jnp
from jax import lax
from jax.experimental import pallas as pl
from jax.experimental.pallas import tpu as pltpu
from jax.sharding import PartitionSpec as P

H_Q = 8
H_KV = 2
HEAD = 128
M_HEADS = 48
M_HEAD = 64
CONV = 4
ADAPTER_RANK = 16
ADAPTER_SETS = 8
SPAN = 128
STATE = 256
D_SSM = 3072
SHARED = 1024
ADAPTERS = ADAPTER_RANK * ADAPTER_SETS

Y_RING = 4
X_PAIR = 2
SEQ = 8
DP = 16
HEADS_DEV = 6
INNER = HEADS_DEV * M_HEAD
SLICE = HEAD + INNER
MIX = X_PAIR * SLICE
UNITS = 1024

COL_Q = 0
COL_INNER = COL_Q + HEAD
COL_GATE = COL_INNER + INNER
COL_K = COL_GATE + INNER
COL_V = COL_K + HEAD
COL_BC = COL_V + HEAD
COL_STEP = COL_BC + 2 * STATE
IN_COLS = COL_STEP + 128

EDGE_INNER = H_Q * HEAD
EDGE_SHARED = EDGE_INNER + D_SSM
EDGE_GATE = EDGE_SHARED + SHARED
EDGE_STEP = EDGE_GATE + D_SSM

CONVOLVED = INNER + 2 * STATE
VMEM_ALL = 56 * 1024 * 1024

epsilon = 1e-05
rope_base = 100000000000.0
masked_score = -1e30
highest = lax.Precision.HIGHEST
bf16 = jnp.bfloat16
f32 = jnp.float32


def rms_scale(vectors, scale_gain):
    return (
        vectors
        * lax.rsqrt(jnp.mean(vectors * vectors, axis=-1, keepdims=True) + epsilon)
        * scale_gain
    )


def silu_value(vectors):
    return vectors * jax.nn.sigmoid(vectors)


def swiglu(gate_and_up):
    half_width = gate_and_up.shape[1] // 2
    return silu_value(gate_and_up[:, :half_width]) * gate_and_up[:, half_width:]


def rotary_tables(position):
    lanes = jnp.arange(HEAD)
    half_width = HEAD // 2
    frequency = rope_base ** (-((lanes % half_width).astype(f32) * 2.0 / HEAD))
    angle = position.astype(f32)[:, None] * frequency[None, :]
    return jnp.cos(angle), jnp.where(lanes < half_width, -1.0, 1.0) * jnp.sin(angle)


def product(left, right):
    return jnp.dot(left, right, preferred_element_type=f32)


def contract_last(left, right):
    return lax.dot_general(left, right, (((1,), (1,)), ((), ())), preferred_element_type=f32)


def contract_first(left, right):
    return lax.dot_general(left, right, (((0,), (0,)), ((), ())), preferred_element_type=f32)


def hop(value, target):
    return lax.ppermute(value, "sp", [(i, target(i)) for i in range(SEQ)])


def up(i):
    return (i + X_PAIR) % SEQ


def down(i):
    return (i - X_PAIR) % SEQ


def side(i):
    return i ^ 1


def gather_ring(block):
    half = block.shape[0] // 2
    below = hop(block, up)
    above = hop(block, down)
    far_first = hop(below[:half], up)
    far_second = hop(above[half:], down)
    return jnp.concatenate([block, above, far_first, far_second, below], axis=0)


def scatter_ring(partial_rows, *after):
    n = partial_rows.shape[0] // Y_RING
    half = n // 2
    far = partial_rows[2 * n : 3 * n].astype(bf16)
    from_below = hop(far[:half], up)
    from_above = hop(far[half:], down)
    from_below, from_above, *after = lax.optimization_barrier((from_below, from_above, *after))
    partial_rows = partial_rows.astype(f32)
    to_up = partial_rows[n : 2 * n]
    to_up = jnp.concatenate([to_up[:half] + from_below.astype(f32), to_up[half:]], axis=0)
    to_down = partial_rows[3 * n :]
    to_down = jnp.concatenate([to_down[:half], to_down[half:] + from_above.astype(f32)], axis=0)
    low = hop(to_up.astype(bf16), up).astype(f32)
    high = hop(to_down.astype(bf16), down).astype(f32)
    return partial_rows[:n] + low + high, *after


def halved(stack, own, axis, target):
    kept = lax.dynamic_index_in_dim(stack, own, axis, keepdims=False)
    sent = lax.dynamic_index_in_dim(stack, 1 - own, axis, keepdims=False)
    received = lax.ppermute(sent, "dp", [(i, target(i)) for i in range(DP)])
    return (kept.astype(f32) + received.astype(f32)).astype(bf16)


def halve_cores(stack, d):
    return halved(stack.reshape(8, 2, -1, 128), d % 2, 1, lambda i: i ^ 1)


def halve_neighbours(stack, d):
    return halved(stack.reshape(2, 4, -1, 128), d // 8, 0, lambda i: (i + 8) % DP)


CHIPS = [[2 * i + c for i in range(DP // 2)] for c in range(2)]
Z_RINGS = [[8 * n + 2 * z + c for z in range(4)] for n in range(2) for c in range(2)]


def scatter_shards(stack, groups):
    return lax.psum_scatter(
        stack.reshape(-1, 128), "dp", scatter_dimension=0, axis_index_groups=groups, tiled=True
    ).astype(f32)


def gather_seq(block):
    copies = jnp.broadcast_to(block[None], (SEQ,) + block.shape)
    return lax.all_to_all(copies, "sp", split_axis=0, concat_axis=0).reshape(
        (SEQ * block.shape[0],) + block.shape[1:]
    )


def exchange_seq(partial_rows):
    pieces = partial_rows.astype(bf16).reshape((SEQ, -1) + partial_rows.shape[1:])
    return lax.all_to_all(pieces, "sp", split_axis=0, concat_axis=0)


def scatter_seq(partial_rows):
    return jnp.sum(exchange_seq(partial_rows).astype(f32), axis=0)


def gather_rings(block, y, x):
    n = block.shape[0]
    half = n // 2
    mate = hop(block, side)
    above = hop(block, down)
    below = hop(block, up)
    mate_above = hop(mate, down)
    mate_below = hop(mate, up)
    out = jnp.zeros((SEQ * n,) + block.shape[1:], block.dtype)
    for rows, distance, column, shift in (
        (block, 0, x, 0),
        (above, 1, x, 0),
        (below, 3, x, 0),
        (mate, 0, 1 - x, 0),
        (hop(below[:half], up), 2, x, 0),
        (hop(above[half:], down), 2, x, half),
        (mate_above, 1, 1 - x, 0),
        (mate_below, 3, 1 - x, 0),
        (hop(mate_below[:half], up), 2, 1 - x, 0),
        (hop(mate_above[half:], down), 2, 1 - x, half),
    ):
        start = n * (X_PAIR * ((y + distance) % Y_RING) + column) + shift
        out = lax.dynamic_update_slice_in_dim(out, rows, start, 0)
    return out


def sum_ring_small(value):
    total = value
    for offset in range(X_PAIR, SEQ, X_PAIR):
        total = total + hop(value, lambda i, offset=offset: (i + offset) % SEQ)
    return total


def blocks_of(matrix):
    n = matrix.shape[1] // 128
    return matrix.reshape(DP, 8, n, 128).transpose(0, 2, 1, 3).reshape(DP, 8 * n, 128)


def row_from_blocks(stacked):
    n = stacked.shape[0] // 8
    return stacked.reshape(n, 8, 128).transpose(1, 0, 2).reshape(8, 128 * n)


def sixteen_rows(rows):
    return jnp.pad(rows, ((0, 16 - rows.shape[0]), (0, 0)))


def pick_columns(block, y):
    rows = lax.broadcasted_iota(jnp.int32, (512, 128), 0)
    lanes = lax.broadcasted_iota(jnp.int32, (512, 128), 1)
    wanted = jnp.where(lanes < M_HEAD, lanes, lanes + 256 - M_HEAD) + M_HEAD * y
    return product(block, (rows == wanted).astype(bf16))


def pack_input_kernel(place_ref, weight_ref, lower_ref, upper_ref, out_ref):
    s = place_ref[0]
    y = s // X_PAIR
    x = s % X_PAIR
    kv_head = s // (H_Q // H_KV)

    def at(column):
        return pl.ds(pl.multiple_of(column, 128), 128)

    def share(ref):
        def heads(edge):
            return [
                pick_columns(
                    ref[:, pl.ds(pl.multiple_of(edge + 256 * (HEADS_DEV * x + 2 * pair), 128), 512)], y
                )
                for pair in range(HEADS_DEV // 2)
            ]

        step_rows = lax.broadcasted_iota(jnp.int32, (M_HEADS, 128), 0)
        step_lanes = lax.broadcasted_iota(jnp.int32, (M_HEADS, 128), 1)
        picked = (step_rows == Y_RING * (HEADS_DEV * x + step_lanes) + y) & (step_lanes < HEADS_DEV)
        return (
            [ref[:, at(HEAD * s)].astype(f32)]
            + heads(EDGE_INNER)
            + heads(EDGE_GATE)
            + [
                ref[:, at(EDGE_SHARED + HEAD * kv_head)].astype(f32),
                ref[:, at(EDGE_SHARED + HEAD * (H_KV + kv_head))].astype(f32),
            ]
            + [
                ref[:, EDGE_SHARED + 2 * H_KV * HEAD + 128 * i : EDGE_SHARED + 2 * H_KV * HEAD + 128 * i + 128].astype(f32)
                for i in range(2 * STATE // 128)
            ]
            + [product(ref[:, EDGE_STEP:], picked.astype(bf16))]
        )

    for i, piece in enumerate(share(weight_ref)):
        out_ref[:, 128 * i : 128 * i + 128] = piece.astype(bf16)
    out_ref[:, IN_COLS : IN_COLS + ADAPTERS] = lower_ref[...]
    upper = [piece[:8] for piece in share(upper_ref)]
    upper.append(jnp.zeros((128 - 8 * len(upper), 128), f32))
    out_ref[:, IN_COLS + ADAPTERS :] = jnp.concatenate(upper, axis=0).astype(bf16)


def pack_ffn_kernel(
    place_ref, gu_ref, gu_lower_ref, gu_upper_ref, down_ref, down_lower_ref, down_upper_ref, out_ref
):
    y = place_ref[0] // X_PAIR
    fold = down_ref.shape[1] // 2
    rows = pl.ds(pl.multiple_of(64 * y, 64), 64)
    out_ref[:64, :fold] = down_ref[rows, :fold]
    out_ref[64:, :fold] = down_ref[rows, fold:]
    pairs = 2 * UNITS // 128
    for i in range(pairs):
        out_ref[:, fold + 128 * i : fold + 128 * i + 128] = pick_columns(
            gu_ref[:, 512 * i : 512 * i + 512], y
        ).astype(bf16)
    edge = fold + 2 * UNITS
    out_ref[:, edge : edge + 128] = gu_lower_ref[...]
    edge += 128
    out_ref[:64, edge : edge + 128] = down_lower_ref[rows, :]
    out_ref[64:, edge : edge + 128] = jnp.zeros((64, 128), bf16)
    edge += 128
    out_ref[:, edge : edge + 128] = jnp.concatenate(
        [pick_columns(gu_upper_ref[:, 512 * i : 512 * i + 512], y)[:8] for i in range(pairs)], axis=0
    ).astype(bf16)
    edge += 128
    out_ref[:, edge:] = jnp.concatenate(
        [down_upper_ref[:, 128 * i : 128 * i + 128].astype(f32)[:8] for i in range(2 * fold // 128)],
        axis=0,
    ).astype(bf16)


def fold_upper(upper_ref, out_ref, column):
    for c in range(2):
        out_ref[:, column + 128 * c : column + 128 * c + 128] = jnp.concatenate(
            [
                upper_ref[:, 1024 * c + 128 * i : 1024 * c + 128 * i + 128].astype(f32)[:8]
                for i in range(8)
            ],
            axis=0,
        ).astype(bf16)


def pack_output_kernel(rows_ref, upper_ref, out_ref):
    width = rows_ref.shape[1]
    out_ref[:, :width] = rows_ref[...]
    fold_upper(upper_ref, out_ref, width)


def raising_kernel(*refs):
    out_ref = refs[-1]
    column = 0
    for ref in refs[:-1]:
        stacked = ref[...].astype(f32)
        depth = stacked.shape[0] // DP
        for block in range(min(depth // 8, out_ref.shape[1] // 128)):
            out_ref[:, column : column + 128] = jnp.concatenate(
                [
                    stacked[depth * shard + 8 * block : depth * shard + 8 * block + 8]
                    for shard in range(DP)
                ],
                axis=0,
            ).astype(bf16)
            column += 128


def raising(stacks, width):
    return pl.pallas_call(
        raising_kernel,
        in_specs=[pl.BlockSpec(memory_space=pltpu.VMEM)] * len(stacks),
        out_specs=pl.BlockSpec(memory_space=pltpu.VMEM),
        out_shape=jax.ShapeDtypeStruct((ADAPTERS, width), bf16),
        compiler_params=pltpu.CompilerParams(vmem_limit_bytes=32 * 1024 * 1024),
    )(*stacks)


def pack(kernel, arrays, shape):
    return pl.pallas_call(
        kernel,
        in_specs=[
            pl.BlockSpec(memory_space=pltpu.SMEM if a.ndim == 1 else pltpu.VMEM) for a in arrays
        ],
        out_specs=pl.BlockSpec(memory_space=pltpu.VMEM),
        out_shape=jax.ShapeDtypeStruct(shape, bf16),
        compiler_params=pltpu.CompilerParams(vmem_limit_bytes=32 * 1024 * 1024),
    )(*arrays)


def lane_index(shape):
    return lax.broadcasted_iota(jnp.int32, shape, 1)


def row_index(shape):
    return lax.broadcasted_iota(jnp.int32, shape, 0)


def over_heads(per_head):
    rows = per_head.shape[0]
    low = lane_index((rows, 128)) < M_HEAD
    return jnp.concatenate(
        [
            jnp.where(low, per_head[:, 2 * pair : 2 * pair + 1], per_head[:, 2 * pair + 1 : 2 * pair + 2])
            for pair in range(HEADS_DEV // 2)
        ],
        axis=1,
    )


def head_sums(values):
    member = (row_index((INNER, 128)) // M_HEAD == lane_index((INNER, 128))).astype(bf16)
    coarse = values.astype(bf16)
    fine = (values - coarse.astype(f32)).astype(bf16)
    return product(coarse, member) + product(fine, member)


def span_terms(convolved, step_block, rate_rows, first_len, start):
    shifted = step_block + rate_rows[0:1]
    rates = jnp.log1p(jnp.exp(-jnp.abs(shifted))) + jnp.maximum(shifted, 0.0)
    log_decay = rates * rate_rows[1:2]
    rows = row_index((SPAN, SPAN))
    lanes = lane_index((SPAN, SPAN))
    below = rows >= lanes
    cumulative = jnp.dot(
        below.astype(f32), log_decay, precision=highest, preferred_element_type=f32
    )
    seg_rows = (rows + start >= first_len).astype(jnp.int32)
    seg_lanes = (lanes + start >= first_len).astype(jnp.int32)
    allowed = below & (seg_rows == seg_lanes)
    last_seg = (start + SPAN - 1 >= first_len).astype(jnp.int32)
    previous = (start - 1 >= first_len).astype(jnp.int32)
    total = cumulative[SPAN - 1 : SPAN]
    entry = jnp.where(seg_rows == previous, jnp.exp(cumulative), 0.0)
    tail = jnp.where(seg_rows == last_seg, jnp.exp(total - cumulative), 0.0)
    keep = jnp.where(last_seg == previous, jnp.exp(total), 0.0)
    activated = convolved * jax.nn.sigmoid(convolved)
    x_in = activated[:, :INNER]
    in_state = activated[:, INNER : INNER + STATE]
    out_state = activated[:, INNER + STATE :]
    return shifted, rates, cumulative, allowed, entry, tail, keep, x_in, in_state, out_state


def decay_of(cumulative, across, allowed, head):
    gap = cumulative[:, head : head + 1] - across[head : head + 1]
    return jnp.exp(jnp.where(allowed, gap, masked_score))


def scan_forward_kernel(
    lengths_ref,
    proj_ref,
    taps_ref,
    rate_rows_ref,
    skip_ref,
    gated_ref,
    scanned_ref,
    squares_ref,
    convolved_ref,
    states_ref,
    state,
    last_rows,
):
    step = pl.program_id(0)
    start = step * SPAN
    first_len = lengths_ref[0, 0]

    @pl.when(step == 0)
    def _():
        state[...] = jnp.zeros_like(state)
        last_rows[...] = jnp.zeros_like(last_rows)

    signal = jnp.concatenate(
        [proj_ref[:, COL_INNER:COL_GATE], proj_ref[:, COL_BC:COL_STEP]], axis=1
    ).astype(f32)
    row = start + row_index((SPAN, 1))
    position = row - jnp.where(row >= first_len, first_len, 0)
    convolved = taps_ref[4:5] + taps_ref[3:4] * signal
    before = last_rows[...]
    top = row_index((8, 1))
    for offset in range(1, CONV):
        moved = pltpu.roll(signal, offset, 0)
        edge = jnp.where(top < offset, pltpu.roll(before, offset, 0), moved[:8])
        moved = jnp.concatenate([edge, moved[8:]], axis=0)
        convolved = convolved + taps_ref[3 - offset : 4 - offset] * jnp.where(
            position >= offset, moved, 0.0
        )
    last_rows[...] = signal[SPAN - 8 :]
    convolved_ref[...] = convolved
    step_block = proj_ref[:, COL_STEP:].astype(f32)
    _, rates, cumulative, allowed, entry, tail, keep, x_in, in_state, out_state = span_terms(
        convolved, step_block, rate_rows_ref[...], first_len, start
    )
    across = cumulative.T
    in_half = in_state.astype(bf16)
    out_half = out_state.astype(bf16)
    state_now = state[...]
    state_half = state_now.astype(bf16)
    states_ref[0] = state_half
    mixing = contract_last(out_half, in_half)
    rates_wide = over_heads(rates)
    weighted = (x_in * rates_wide).astype(bf16)
    low = lane_index((SPAN, 128)) < M_HEAD
    within = []
    for pair in range(HEADS_DEV // 2):
        block = weighted[:, 128 * pair : 128 * pair + 128]
        sides = [
            product(
                (mixing * decay_of(cumulative, across, allowed, 2 * pair + i)).astype(bf16), block
            )
            for i in range(2)
        ]
        within.append(jnp.where(low, sides[0], sides[1]))
    result = (
        jnp.concatenate(within, axis=1)
        + product(out_half, state_half) * over_heads(entry)
        + skip_ref[0:1] * x_in
    )
    scanned = result.astype(bf16)
    scanned_ref[...] = scanned
    gate = proj_ref[:, COL_GATE:COL_K].astype(f32)
    gated = scanned.astype(f32) * (gate * jax.nn.sigmoid(gate))
    gated_ref[...] = gated.astype(bf16)
    squares_ref[...] = lax.dot_general(
        jnp.ones((8, INNER), f32),
        gated * gated,
        (((1,), (1,)), ((), ())),
        precision=highest,
        preferred_element_type=f32,
    )
    state[...] = state_now * over_heads(keep) + contract_first(
        in_half, (x_in * over_heads(tail * rates)).astype(bf16)
    )


def scan_backward_kernel(
    lengths_ref,
    proj_ref,
    convolved_ref,
    scanned_ref,
    states_ref,
    upstream_ref,
    scales_ref,
    grad_query_ref,
    grad_key_ref,
    grad_value_ref,
    taps_ref,
    rate_rows_ref,
    skip_ref,
    out_ref,
    grad_state,
    next_rows,
):
    step = pl.num_programs(0) - 1 - pl.program_id(0)
    start = step * SPAN
    first_len = lengths_ref[0, 0]

    @pl.when(pl.program_id(0) == 0)
    def _():
        grad_state[...] = jnp.zeros_like(grad_state)
        next_rows[...] = jnp.zeros_like(next_rows)

    convolved = convolved_ref[...]
    step_block = proj_ref[:, COL_STEP:].astype(f32)
    rate_rows = rate_rows_ref[...]
    shifted, rates, cumulative, allowed, entry, tail, keep, x_in, in_state, out_state = span_terms(
        convolved, step_block, rate_rows, first_len, start
    )
    across = cumulative.T
    in_half = in_state.astype(bf16)
    out_half = out_state.astype(bf16)
    state_half = states_ref[0]

    gate = proj_ref[:, COL_GATE:COL_K].astype(f32)
    gate_sigmoid = jax.nn.sigmoid(gate)
    gate_silu = gate * gate_sigmoid
    scanned = scanned_ref[...].astype(f32)
    upstream = upstream_ref[:, HEAD:].astype(f32) * skip_ref[1:2]
    grad_gated = scales_ref[:, 0:1] * upstream - scales_ref[:, 1:2] * (scanned * gate_silu)
    out_ref[:, COL_GATE:COL_K] = (
        grad_gated * scanned * (gate_sigmoid * (1.0 + gate * (1.0 - gate_sigmoid)))
    ).astype(bf16)
    grad_half = (grad_gated * gate_silu).astype(bf16)
    grad_result = grad_half.astype(f32)

    mixing = contract_last(out_half, in_half)
    rates_wide = over_heads(rates)
    entry_wide = over_heads(entry)
    tail_wide = over_heads(tail)
    keep_wide = over_heads(keep)
    weighted = (x_in * rates_wide).astype(bf16)
    lane = lane_index((SPAN, 128))
    low = lane < M_HEAD
    grad_mixing = jnp.zeros((SPAN, SPAN), f32)
    grad_cumulative = jnp.zeros((SPAN, 128), f32)
    grad_across = jnp.zeros((SPAN, 128), f32)
    head_row = row_index((SPAN, 128))
    grad_weighted = []
    for pair in range(HEADS_DEV // 2):
        block = weighted[:, 128 * pair : 128 * pair + 128]
        grad_block = grad_half[:, 128 * pair : 128 * pair + 128]
        sides = []
        for i in range(2):
            head = 2 * pair + i
            decay = decay_of(cumulative, across, allowed, head)
            spread = mixing * decay
            sides.append(contract_first(spread.astype(bf16), grad_block))
            mine = low if i == 0 else jnp.logical_not(low)
            grad_spread = contract_last(jnp.where(mine, grad_block, jnp.zeros_like(grad_block)), block)
            grad_mixing = grad_mixing + grad_spread * decay
            grad_gap = grad_spread * spread
            grad_cumulative = jnp.where(
                lane == head, jnp.sum(grad_gap, axis=1, keepdims=True), grad_cumulative
            )
            grad_across = jnp.where(
                head_row == head, jnp.sum(grad_gap, axis=0, keepdims=True), grad_across
            )
        grad_weighted.append(jnp.where(low, sides[0], sides[1]))
    grad_weighted = jnp.concatenate(grad_weighted, axis=1)
    grad_cumulative = grad_cumulative - grad_across.T

    grad_next = grad_state[...]
    grad_next_half = grad_next.astype(bf16)
    grad_entered = (grad_result * entry_wide).astype(bf16)
    from_state = product(out_half, state_half)
    to_state = product(in_half, grad_next_half)
    tail_rates = tail_wide * rates_wide
    grad_mixing_half = grad_mixing.astype(bf16)
    grad_out_state = product(grad_mixing_half, in_half) + contract_last(grad_entered, state_half)
    grad_in_state = contract_first(grad_mixing_half, out_half) + contract_last(
        (x_in * tail_rates).astype(bf16), grad_next_half
    )
    sums = head_sums(
        jnp.concatenate(
            [
                grad_result * from_state,
                to_state * x_in,
                grad_weighted * x_in,
                jnp.broadcast_to(
                    jnp.sum(grad_next * state_half.astype(f32), axis=0, keepdims=True), (8, INNER)
                ),
            ],
            axis=0,
        )
    )
    grad_entry = sums[:SPAN]
    grad_tail = sums[SPAN : 2 * SPAN]
    grad_rates = sums[2 * SPAN : 3 * SPAN] + grad_tail * tail
    from_tail = grad_tail * tail * rates
    grad_total = (
        jnp.sum(from_tail, axis=0, keepdims=True) + sums[3 * SPAN : 3 * SPAN + 1] * keep
    )
    grad_cumulative = grad_cumulative + grad_entry * entry - from_tail
    grad_cumulative = grad_cumulative + jnp.where(head_row == SPAN - 1, grad_total, 0.0)
    above = (row_index((SPAN, SPAN)) <= lane_index((SPAN, SPAN))).astype(f32)
    grad_decay = jnp.dot(above, grad_cumulative, precision=highest, preferred_element_type=f32)
    grad_rates = grad_rates + grad_decay * rate_rows[1:2]
    out_ref[:, COL_STEP:] = jnp.where(
        lane < HEADS_DEV, grad_rates * jax.nn.sigmoid(shifted), 0.0
    ).astype(bf16)
    grad_x = grad_weighted * rates_wide + to_state * tail_rates + skip_ref[0:1] * grad_result
    grad_state[...] = grad_next * keep_wide + contract_first(out_half, grad_entered)

    conv_sigmoid = jax.nn.sigmoid(convolved)
    grad_conv = jnp.concatenate([grad_x, grad_in_state, grad_out_state], axis=1) * (
        conv_sigmoid * (1.0 + convolved * (1.0 - conv_sigmoid))
    )
    row = start + row_index((SPAN, 1))
    position = row - jnp.where(row >= first_len, first_len, 0)
    later_row = start + SPAN + row_index((8, 1))
    later_position = later_row - jnp.where(later_row >= first_len, first_len, 0)
    later = next_rows[...]
    bottom = row_index((8, 1))
    grad_signal = taps_ref[3:4] * grad_conv
    for offset in range(1, CONV):
        moved = pltpu.roll(jnp.where(position >= offset, grad_conv, 0.0), SPAN - offset, 0)
        edge = pltpu.roll(jnp.where(later_position >= offset, later, 0.0), 8 - offset, 0)
        edge = jnp.where(bottom >= 8 - offset, edge, moved[SPAN - 8 :])
        moved = jnp.concatenate([moved[: SPAN - 8], edge], axis=0)
        grad_signal = grad_signal + taps_ref[3 - offset : 4 - offset] * moved
    next_rows[...] = grad_conv[:8]
    out_ref[:, COL_INNER:COL_GATE] = grad_signal[:, :INNER].astype(bf16)
    out_ref[:, COL_BC:COL_STEP] = grad_signal[:, INNER:].astype(bf16)
    out_ref[:, :COL_INNER] = grad_query_ref[...]
    out_ref[:, COL_K:COL_V] = grad_key_ref[...]
    out_ref[:, COL_V:COL_BC] = grad_value_ref[...]


def whole(shape):
    return pl.BlockSpec(shape, lambda i: (0,) * len(shape))


smem = pl.BlockSpec(memory_space=pltpu.SMEM)


def scan_forward(lengths, proj, taps, rate_rows, skip_rows):
    length_all = proj.shape[0]
    spans = length_all // SPAN

    def rows(width):
        return pl.BlockSpec((SPAN, width), lambda i: (i, 0))

    return pl.pallas_call(
        scan_forward_kernel,
        grid=(spans,),
        in_specs=[smem, rows(IN_COLS), whole(taps.shape), whole(rate_rows.shape), whole(skip_rows.shape)],
        out_specs=[
            rows(INNER),
            rows(INNER),
            pl.BlockSpec((8, SPAN), lambda i: (i, 0)),
            rows(CONVOLVED),
            pl.BlockSpec((1, STATE, INNER), lambda i: (i, 0, 0)),
        ],
        out_shape=[
            jax.ShapeDtypeStruct((length_all, INNER), bf16),
            jax.ShapeDtypeStruct((length_all, INNER), bf16),
            jax.ShapeDtypeStruct((8 * spans, SPAN), f32),
            jax.ShapeDtypeStruct((length_all, CONVOLVED), f32),
            jax.ShapeDtypeStruct((spans, STATE, INNER), bf16),
        ],
        scratch_shapes=[pltpu.VMEM((STATE, INNER), f32), pltpu.VMEM((8, CONVOLVED), f32)],
        compiler_params=pltpu.CompilerParams(vmem_limit_bytes=VMEM_ALL),
        cost_estimate=pl.CostEstimate(flops=10**10, bytes_accessed=10**7, transcendentals=10**6),
        name="scan_forward",
    )(lengths, proj, taps, rate_rows, skip_rows)


def scan_backward(
    lengths, proj, convolved, scanned, states, upstream, scales, grad_qkv, taps, rate_rows, skip_rows
):
    length_all = proj.shape[0]
    spans = length_all // SPAN

    def rows(width):
        return pl.BlockSpec((SPAN, width), lambda i: (spans - 1 - i, 0))

    return pl.pallas_call(
        scan_backward_kernel,
        grid=(spans,),
        in_specs=[
            smem,
            rows(IN_COLS),
            rows(CONVOLVED),
            rows(INNER),
            pl.BlockSpec((1, STATE, INNER), lambda i: (spans - 1 - i, 0, 0)),
            rows(HEAD + INNER),
            rows(2),
            rows(HEAD),
            rows(HEAD),
            rows(HEAD),
            whole(taps.shape),
            whole(rate_rows.shape),
            whole(skip_rows.shape),
        ],
        out_specs=rows(IN_COLS),
        out_shape=jax.ShapeDtypeStruct((length_all, IN_COLS), bf16),
        scratch_shapes=[pltpu.VMEM((STATE, INNER), f32), pltpu.VMEM((8, CONVOLVED), f32)],
        compiler_params=pltpu.CompilerParams(vmem_limit_bytes=VMEM_ALL),
        cost_estimate=pl.CostEstimate(flops=17 * 10**9, bytes_accessed=10**7, transcendentals=10**6),
        name="scan_backward",
    )(lengths, proj, convolved, scanned, states, upstream, scales, *grad_qkv, taps, rate_rows, skip_rows)


QUERY_ROWS = 256
score_scale = HEAD ** (-0.5)


def turn(values, cosine, sine):
    return values * cosine + pltpu.roll(values, HEAD // 2, 1) * sine


def allowed_scores(query_rot, key_rot, first_row, first_len):
    scores = contract_last(query_rot, key_rot) * score_scale
    rows = first_row + row_index(scores.shape)
    lanes = lane_index(scores.shape)
    allowed = (lanes <= rows) & ((lanes >= first_len) | (rows < first_len))
    return jnp.where(allowed, scores, masked_score)


def attention_forward_kernel(
    lengths_ref, query_ref, key_ref, value_ref, cosine_ref, sine_ref, out_ref, totals_ref
):
    first_len = lengths_ref[0, 0]
    length_all = query_ref.shape[0]
    key_rot = turn(key_ref[...].astype(f32), cosine_ref[...], sine_ref[...]).astype(bf16)
    for first in range(0, length_all, QUERY_ROWS):
        block = slice(first, first + QUERY_ROWS)
        seen = first + QUERY_ROWS
        query_rot = turn(
            query_ref[block].astype(f32), cosine_ref[block], sine_ref[block]
        ).astype(bf16)
        scores = allowed_scores(query_rot, key_rot[:seen], first, first_len)
        peak = jnp.max(scores, axis=1, keepdims=True)
        exponent = jnp.exp(scores - peak)
        total = jnp.sum(exponent, axis=1, keepdims=True)
        probs = (exponent * (1.0 / total)).astype(bf16)
        out_ref[block] = product(probs, value_ref[:seen]).astype(bf16)
        totals_ref[block] = peak + jnp.log(total)


def attention_backward_kernel(
    lengths_ref,
    query_ref,
    key_ref,
    value_ref,
    cosine_ref,
    sine_ref,
    upstream_ref,
    totals_ref,
    grad_query_ref,
    grad_key_ref,
    grad_value_ref,
    key_sum,
    value_sum,
):
    first_len = lengths_ref[0, 0]
    length_all = query_ref.shape[0]
    key_rot = turn(key_ref[...].astype(f32), cosine_ref[...], sine_ref[...]).astype(bf16)
    key_sum[...] = jnp.zeros_like(key_sum)
    value_sum[...] = jnp.zeros_like(value_sum)
    for first in range(0, length_all, QUERY_ROWS):
        block = slice(first, first + QUERY_ROWS)
        seen = first + QUERY_ROWS
        cosine = cosine_ref[block]
        sine = sine_ref[block]
        query_rot = turn(query_ref[block].astype(f32), cosine, sine).astype(bf16)
        probs = jnp.exp(
            allowed_scores(query_rot, key_rot[:seen], first, first_len) - totals_ref[block]
        )
        upstream = upstream_ref[block]
        grad_probs = contract_last(upstream, value_ref[:seen])
        delta = jnp.sum(probs * grad_probs, axis=1, keepdims=True)
        grad_scores = (probs * (grad_probs - delta)).astype(bf16)
        grad_query_ref[block] = turn(
            product(grad_scores, key_rot[:seen]) * score_scale, cosine, -sine
        ).astype(bf16)
        key_sum[:seen] += contract_first(grad_scores, query_rot)
        value_sum[:seen] += contract_first(probs.astype(bf16), upstream)
    grad_key_ref[...] = turn(
        key_sum[...] * score_scale, cosine_ref[...], -sine_ref[...]
    ).astype(bf16)
    grad_value_ref[...] = value_sum[...].astype(bf16)


def head_block(length_all, column):
    return pl.BlockSpec((length_all, HEAD), lambda i: (0, column // HEAD))


def attention_forward(lengths, proj, cosine, sine):
    length_all = proj.shape[0]
    block = head_block(length_all, 0)
    return pl.pallas_call(
        attention_forward_kernel,
        grid=(1,),
        in_specs=[
            smem,
            block,
            head_block(length_all, COL_K),
            head_block(length_all, COL_V),
            block,
            block,
        ],
        out_specs=[block, pl.BlockSpec((length_all, 1), lambda i: (0, 0))],
        out_shape=[
            jax.ShapeDtypeStruct((length_all, HEAD), bf16),
            jax.ShapeDtypeStruct((length_all, 1), f32),
        ],
        compiler_params=pltpu.CompilerParams(vmem_limit_bytes=VMEM_ALL),
        name="attention_forward",
    )(lengths, proj, proj, proj, cosine, sine)


def attention_backward(lengths, proj, cosine, sine, upstream, totals):
    length_all = proj.shape[0]
    block = head_block(length_all, 0)
    return pl.pallas_call(
        attention_backward_kernel,
        grid=(1,),
        in_specs=[
            smem,
            block,
            head_block(length_all, COL_K),
            head_block(length_all, COL_V),
            block,
            block,
            block,
            pl.BlockSpec((length_all, 1), lambda i: (0, 0)),
        ],
        out_specs=[block, block, block],
        out_shape=[jax.ShapeDtypeStruct((length_all, HEAD), bf16)] * 3,
        scratch_shapes=[pltpu.VMEM((length_all, HEAD), f32)] * 2,
        compiler_params=pltpu.CompilerParams(vmem_limit_bytes=VMEM_ALL),
        name="attention_backward",
    )(lengths, proj, proj, proj, cosine, sine, upstream, totals)


VMEM_LIMIT = 48 * 1024 * 1024


def input_forward_kernel(left_ref, mask_ref, weight_ref, lower_ref, raise_ref, out_ref, lowered_ref):
    @pl.when(pl.program_id(0) == 0)
    def _():
        lowered_ref[...] = (product(left_ref[...], lower_ref[...]) * mask_ref[...]).astype(bf16)

    out_ref[...] = (
        product(left_ref[...], weight_ref[...]) + product(lowered_ref[...], raise_ref[...])
    ).astype(bf16)


def fixed(shape, *place):
    return pl.BlockSpec(shape, lambda i: place)


def input_forward(left, mask, gathered, raising_all):
    rows, depth = left.shape
    tile = 256
    return pl.pallas_call(
        input_forward_kernel,
        grid=(IN_COLS // tile,),
        in_specs=[
            fixed((rows, depth), 0, 0),
            fixed((rows, ADAPTERS), 0, 0),
            pl.BlockSpec((depth, tile), lambda i: (0, i)),
            fixed((depth, ADAPTERS), 0, IN_COLS // ADAPTERS),
            pl.BlockSpec((ADAPTERS, tile), lambda i: (0, i)),
        ],
        out_specs=[
            pl.BlockSpec((rows, tile), lambda i: (0, i)),
            fixed((rows, ADAPTERS), 0, 0),
        ],
        out_shape=[
            jax.ShapeDtypeStruct((rows, IN_COLS), bf16),
            jax.ShapeDtypeStruct((rows, ADAPTERS), bf16),
        ],
        compiler_params=pltpu.CompilerParams(vmem_limit_bytes=VMEM_ALL),
        cost_estimate=pl.CostEstimate(flops=9 * 10**9, bytes_accessed=10**7, transcendentals=0),
        name="input_forward",
    )(left, mask, gathered, gathered, raising_all)


def input_backward_kernel(
    upstream_ref, left_ref, lowered_ref, mask_ref, weight_ref, raise_ref, out_ref, late_ref, scaled
):
    step = pl.program_id(0)

    @pl.when(step == 0)
    def _():
        scaled[...] = (contract_last(upstream_ref[...], raise_ref[...]) * mask_ref[...]).astype(bf16)
        grad_raise = contract_first(lowered_ref[...], upstream_ref[...])
        for shard in range(DP):
            late_ref[shard, 128:] = jnp.concatenate(
                [
                    grad_raise[8 * shard : 8 * shard + 8, 128 * i : 128 * i + 128]
                    for i in range(IN_COLS // 128)
                ]
                + [jnp.zeros((16, 128), f32)],
                axis=0,
            ).astype(bf16)

    out_ref[...] = (
        contract_last(upstream_ref[...], weight_ref[:, :IN_COLS])
        + contract_last(scaled[...], weight_ref[:, IN_COLS : IN_COLS + ADAPTERS])
    ).astype(bf16)
    grad_lower = contract_first(left_ref[...], scaled[...]).astype(bf16)
    shards = grad_lower.shape[0] // 128
    for shard in range(shards):
        late_ref[shards * step + shard, :128] = grad_lower[128 * shard : 128 * shard + 128]


def input_backward(upstream, left, lowered, mask, gathered, raising_all):
    rows, depth = left.shape
    tile = 512
    return pl.pallas_call(
        input_backward_kernel,
        grid=(depth // tile,),
        in_specs=[
            fixed((rows, IN_COLS), 0, 0),
            pl.BlockSpec((rows, tile), lambda i: (0, i)),
            fixed((rows, ADAPTERS), 0, 0),
            fixed((rows, ADAPTERS), 0, 0),
            pl.BlockSpec((tile, gathered.shape[1]), lambda i: (i, 0)),
            fixed((ADAPTERS, IN_COLS), 0, 0),
        ],
        out_specs=[
            pl.BlockSpec((rows, tile), lambda i: (0, i)),
            fixed((DP, 256, 128), 0, 0, 0),
        ],
        out_shape=[
            jax.ShapeDtypeStruct((rows, depth), bf16),
            jax.ShapeDtypeStruct((DP, 256, 128), bf16),
        ],
        scratch_shapes=[pltpu.VMEM((rows, ADAPTERS), bf16)],
        compiler_params=pltpu.CompilerParams(vmem_limit_bytes=VMEM_ALL),
        cost_estimate=pl.CostEstimate(flops=10**10, bytes_accessed=10**7, transcendentals=0),
        name="input_backward",
    )(upstream, left, lowered, mask, gathered, raising_all)


def ffn_kernel(
    left_ref,
    cotangent_ref,
    mask_ref,
    gate_ref,
    up_ref,
    lower_ref,
    raise_gate_ref,
    raise_up_ref,
    down_ref,
    lower_down_ref,
    raise_down_ref,
    left_down_ref,
    grad_gate_ref,
    grad_up_ref,
    grad_left_ref,
    lowered_ref,
    scaled_ref,
    scaled_down_ref,
    grad_left,
    grad_lowered,
):
    step = pl.program_id(0)
    model = left_ref.shape[1]

    @pl.when(step == 0)
    def _():
        lowered_ref[...] = (product(left_ref[...], lower_ref[...]) * mask_ref[...]).astype(bf16)
        scaled_down_ref[...] = (
            contract_last(cotangent_ref[...], raise_down_ref[...]) * mask_ref[...]
        ).astype(bf16)
        grad_left[...] = jnp.zeros_like(grad_left)
        grad_lowered[...] = jnp.zeros_like(grad_lowered)

    lowered = lowered_ref[...]
    gate = product(left_ref[...], gate_ref[...]) + product(lowered, raise_gate_ref[...])
    up = product(left_ref[...], up_ref[...]) + product(lowered, raise_up_ref[...])
    shards = range(0, down_ref.shape[0], 128)
    grad_act = contract_last(
        scaled_down_ref[...],
        jnp.concatenate([lower_down_ref[row : row + 64] for row in shards], axis=0),
    )
    for c in range(2):
        grad_act = grad_act + contract_last(
            cotangent_ref[:, c * model // 2 : (c + 1) * model // 2],
            jnp.concatenate([down_ref[row + 64 * c : row + 64 * c + 64] for row in shards], axis=0),
        )
    sigmoid = jax.nn.sigmoid(gate)
    silu = gate * sigmoid
    left_down_ref[...] = (silu * up).astype(bf16)
    grad_up = (grad_act * silu).astype(bf16)
    grad_gate = (grad_act * up * (sigmoid * (1.0 + gate * (1.0 - sigmoid)))).astype(bf16)
    grad_gate_ref[...] = grad_gate
    grad_up_ref[...] = grad_up
    grad_left[...] += contract_last(grad_gate, gate_ref[...]) + contract_last(grad_up, up_ref[...])
    grad_lowered[...] += contract_last(grad_gate, raise_gate_ref[...]) + contract_last(
        grad_up, raise_up_ref[...]
    )

    @pl.when(step == pl.num_programs(0) - 1)
    def _():
        scaled = (grad_lowered[...] * mask_ref[...]).astype(bf16)
        scaled_ref[...] = scaled
        grad_left_ref[...] = (grad_left[...] + contract_last(scaled, lower_ref[...])).astype(bf16)


def ffn_forward_backward(left, cotangent, mask, gathered, gu_raise, down_raise):
    rows, model = left.shape
    tile = 512
    tiles = UNITS // tile
    fold = model // 2
    first = fold // tile
    lower = (fold + 2 * UNITS) // ADAPTERS
    stacked = tile // 64 * 128
    whole_rows = fixed((rows, model), 0, 0)
    adapter_rows = fixed((rows, ADAPTERS), 0, 0)
    return pl.pallas_call(
        ffn_kernel,
        grid=(tiles,),
        in_specs=[
            whole_rows,
            whole_rows,
            adapter_rows,
            pl.BlockSpec((model, tile), lambda i: (0, first + i)),
            pl.BlockSpec((model, tile), lambda i: (0, first + tiles + i)),
            fixed((model, ADAPTERS), 0, lower),
            pl.BlockSpec((ADAPTERS, tile), lambda i: (0, i)),
            pl.BlockSpec((ADAPTERS, tile), lambda i: (0, tiles + i)),
            pl.BlockSpec((stacked, fold), lambda i: (i, 0)),
            pl.BlockSpec((stacked, ADAPTERS), lambda i: (i, lower + 1)),
            fixed((ADAPTERS, model), 0, 0),
        ],
        out_specs=[pl.BlockSpec((rows, tile), lambda i: (0, i))] * 3
        + [whole_rows, adapter_rows, adapter_rows, adapter_rows],
        out_shape=[jax.ShapeDtypeStruct((rows, UNITS), bf16)] * 3
        + [jax.ShapeDtypeStruct((rows, model), bf16)]
        + [jax.ShapeDtypeStruct((rows, ADAPTERS), bf16)] * 3,
        scratch_shapes=[pltpu.VMEM((rows, model), f32), pltpu.VMEM((rows, ADAPTERS), f32)],
        compiler_params=pltpu.CompilerParams(vmem_limit_bytes=VMEM_LIMIT),
        cost_estimate=pl.CostEstimate(flops=12 * 10**9, bytes_accessed=10**7, transcendentals=10**6),
        name="ffn",
    )(
        left,
        cotangent,
        mask,
        gathered,
        gathered,
        gathered,
        gu_raise,
        gu_raise,
        gathered,
        gathered,
        down_raise,
    )


def per_device(
    tokens,
    cotangent,
    seq_lengths,
    adapter_ids,
    norm_gain,
    ffn_gain,
    gate_gain,
    conv_weight,
    conv_bias,
    dt_bias,
    decay_log,
    skip_gain,
    frozen_input_weight,
    input_adapter_lower,
    input_adapter_upper,
    frozen_output_weight,
    output_adapter_lower,
    output_adapter_upper,
    frozen_gate_up_weight,
    gate_up_adapter_lower,
    gate_up_adapter_upper,
    frozen_down_weight,
    down_adapter_lower,
    down_adapter_upper,
):
    s = lax.axis_index("sp")
    d = lax.axis_index("dp")
    y = s // X_PAIR
    x = s % X_PAIR
    tok_count = tokens.shape[0]
    group_len = tok_count * SEQ
    first_len = seq_lengths[0, 0]
    set_ids = adapter_ids[0]

    def adapter_mask(token_index):
        resident = jnp.where(token_index >= first_len, set_ids[1], set_ids[0])
        return jnp.arange(ADAPTERS)[None, :] // ADAPTER_RANK == resident[:, None]

    group_index = jnp.arange(group_len)
    segment = (group_index >= first_len).astype(jnp.int32)
    position = group_index - first_len * segment
    mask_all = adapter_mask(group_index)
    ring_blocks = X_PAIR * ((y + jnp.arange(Y_RING)) % Y_RING) + x
    ring_index = (ring_blocks[:, None] * tok_count + jnp.arange(tok_count)[None, :]).reshape(-1)
    mask_ring = adapter_mask(ring_index)

    def head_columns(values):
        lead = values.shape[:-1]
        grouped = values.reshape(lead + (12, Y_RING, M_HEAD))
        grouped = lax.dynamic_slice_in_dim(grouped, HEADS_DEV * x, HEADS_DEV, len(lead))
        grouped = lax.dynamic_index_in_dim(grouped, y, len(lead) + 1, keepdims=False)
        return grouped.reshape(lead + (INNER,))

    def head_items(values):
        lead = values.shape[:-1]
        grouped = values.reshape(lead + (12, Y_RING))
        grouped = lax.dynamic_slice_in_dim(grouped, HEADS_DEV * x, HEADS_DEV, len(lead))
        return lax.dynamic_index_in_dim(grouped, y, len(lead) + 1, keepdims=False)

    kv_head = s // (H_Q // H_KV)

    def gather_rows(rows):
        return lax.all_gather(rows, "dp", axis=0, tiled=True)

    place = jnp.reshape(s, (1,)).astype(jnp.int32)
    in_all = gather_rows(
        pack(
            pack_input_kernel,
            (place, frozen_input_weight, input_adapter_lower, sixteen_rows(input_adapter_upper)),
            (128, IN_COLS + 2 * ADAPTERS),
        )
    )
    in_raise = raising([in_all[:, IN_COLS + ADAPTERS :]], IN_COLS)

    hidden = tokens.astype(f32)
    normed, norm_back = jax.vjp(partial(rms_scale, scale_gain=norm_gain), hidden)
    normed, frozen_output_weight, frozen_down_weight = lax.optimization_barrier(
        (normed.astype(bf16), frozen_output_weight, frozen_down_weight)
    )
    left_in = gather_rings(normed, y, x)

    out_rows = jnp.concatenate([frozen_output_weight, output_adapter_lower], axis=1)
    piece = lax.dynamic_slice_in_dim(out_rows, 64 * y, 64, 0)
    spread = jnp.zeros_like(piece)
    for k in range(1, Y_RING):
        block = lax.dynamic_slice_in_dim(out_rows, 64 * ((y + k) % Y_RING), 64, 0)
        pairs = [((i // 2) * SEQ + i, ((i // 2 + k) % Y_RING) * SEQ + i) for i in range(SEQ)]
        spread = spread + lax.ppermute(block, ("dp", "sp"), pairs)
    own_rows = (d >= Y_RING) | (d == y)
    model = frozen_output_weight.shape[1]
    out_all = gather_rows(
        pack(
            pack_output_kernel,
            (jnp.where(own_rows, piece, spread), sixteen_rows(output_adapter_upper)),
            (64, model + 3 * ADAPTERS),
        )
    )
    out_weight = out_all[:, : model + ADAPTERS]
    out_raise = raising(
        [out_all[:, model + 128 * c : model + 128 * c + 128] for c in (1, 2)], model
    )

    fold = model // 2
    ffn_all = gather_rows(
        pack(
            pack_ffn_kernel,
            (
                place,
                frozen_gate_up_weight,
                gate_up_adapter_lower,
                sixteen_rows(gate_up_adapter_upper),
                frozen_down_weight,
                down_adapter_lower,
                sixteen_rows(down_adapter_upper),
            ),
            (128, fold + 2 * UNITS + 4 * ADAPTERS),
        )
    )
    edge = fold + 2 * UNITS + 2 * ADAPTERS
    gu_raise = raising([ffn_all[:, edge : edge + ADAPTERS]], 2 * UNITS)
    down_raise = raising([ffn_all[:, edge + ADAPTERS :]], model)

    def masked(lowered, mask):
        return jnp.where(mask, lowered, 0.0).astype(bf16)

    def forward(left, weight, raising, mask):
        both = product(left, weight)
        width = raising.shape[1]
        lowered = masked(both[:, width:], mask)
        return both[:, :width] + product(lowered, raising), lowered

    def backward(left, lowered, upstream, weight, raising, mask):
        gradient_lowered = masked(contract_last(upstream, raising), mask)
        grad_raise = contract_first(lowered, upstream)
        grad_lower = contract_first(left, gradient_lowered)
        grad_left = contract_last(jnp.concatenate([upstream, gradient_lowered], axis=1), weight)
        return grad_left, grad_lower, grad_raise

    left_in, cot_own = lax.optimization_barrier((left_in, cotangent))
    cot_below = hop(cot_own, up)
    cot_above = hop(cot_own, down)
    projected, lower_in = input_forward(left_in, mask_all.astype(f32), in_all, in_raise)

    projected, cot_below, cot_above = lax.optimization_barrier((projected, cot_below, cot_above))
    half = tok_count // 2
    cot_far = hop(cot_below[:half], up), hop(cot_above[half:], down)
    taps = jnp.concatenate(
        [
            jnp.concatenate([head_columns(conv_weight[:, :D_SSM]), conv_weight[:, D_SSM:]], axis=1),
            jnp.concatenate([head_columns(conv_bias[:D_SSM]), conv_bias[D_SSM:]])[None],
            jnp.zeros((3, INNER + 2 * STATE), f32),
        ],
        axis=0,
    )
    rate_rows = jnp.pad(
        jnp.stack([head_items(dt_bias), -jnp.exp(head_items(decay_log))]),
        ((0, 6), (0, 128 - HEADS_DEV)),
    )
    skip_rows = jnp.pad(
        jnp.stack([jnp.repeat(head_items(skip_gain), M_HEAD), head_columns(gate_gain)]),
        ((0, 6), (0, 0)),
    )
    gain_pair = lax.dynamic_index_in_dim(
        gate_gain.reshape(12, Y_RING, M_HEAD), y, 1, keepdims=False
    ).reshape(1, -1)
    cosine_table, sine_table = rotary_tables(position)
    gated, scanned, squares, convolved, states = scan_forward(
        seq_lengths, projected, taps, rate_rows, skip_rows
    )
    squares, cot_far = lax.optimization_barrier((squares, cot_far))
    attended, log_totals = attention_forward(seq_lengths, projected, cosine_table, sine_table)
    squares = sum_ring_small(squares.reshape(SEQ, 8, tok_count)[:, 0])
    inverse = lax.rsqrt((squares + hop(squares, side)) / D_SSM + epsilon)
    mixed = jnp.concatenate([attended, gated], axis=1)
    cot_ring = jnp.concatenate([cot_own, cot_above, *cot_far, cot_below], axis=0)

    def to_ring(values):
        doubled = jnp.concatenate([values, values], axis=0)
        rolled = lax.dynamic_slice_in_dim(doubled, X_PAIR * tok_count * y, group_len, 0)
        return rolled.reshape(Y_RING, X_PAIR, tok_count, -1)

    def from_ring(values):
        flat = values.reshape(group_len, -1)
        doubled = jnp.concatenate([flat, flat], axis=0)
        start = X_PAIR * tok_count * ((Y_RING - y) % Y_RING)
        return lax.dynamic_slice_in_dim(doubled, start, group_len, 0)

    ring_len = Y_RING * tok_count
    mixed_ring = to_ring(mixed)
    kept = lax.dynamic_index_in_dim(mixed_ring, x, 1, keepdims=False).reshape(ring_len, SLICE)
    other = lax.dynamic_index_in_dim(mixed_ring, 1 - x, 1, keepdims=False).reshape(ring_len, SLICE)
    received = hop(other, side)
    low = jnp.where(x == 0, kept, received)
    high = jnp.where(x == 0, received, kept)
    gated_pair = jnp.concatenate([low[:, HEAD:], high[:, HEAD:]], axis=1).astype(f32)
    inverse_ring = lax.dynamic_index_in_dim(
        to_ring(inverse.reshape(-1, 1)), x, 1, keepdims=False
    ).reshape(ring_len, 1)
    left_out = jnp.concatenate(
        [low[:, :HEAD], high[:, :HEAD], (gated_pair * inverse_ring * gain_pair).astype(bf16)],
        axis=1,
    )
    branch_part, lower_out = forward(left_out, out_weight, out_raise, mask_ring)
    (branch,) = scatter_ring(branch_part)
    residual = hidden + branch
    normed_ffn, ffn_norm_back = jax.vjp(partial(rms_scale, scale_gain=ffn_gain), residual)
    left_gu = gather_ring(normed_ffn.astype(bf16))
    left_down, grad_gate_half, grad_up_half, grad_gu_part, lower_gu, scaled_gu, scaled_down = (
        ffn_forward_backward(
            left_gu, cot_ring, mask_ring.astype(f32), ffn_all, gu_raise, down_raise
        )
    )
    grad_a_gu = contract_first(left_gu, scaled_gu)
    grad_b_gu = contract_first(
        lower_gu, jnp.concatenate([grad_gate_half, grad_up_half], axis=1)
    )
    (grad_left_gu,) = scatter_ring(grad_gu_part)
    grad_left_gu, left_down, ffn_all = lax.optimization_barrier((grad_left_gu, left_down, ffn_all))
    folded = ffn_all[:, :fold].reshape(DP, 2, 64, fold)
    lowers = ffn_all[:, fold + 2 * UNITS + ADAPTERS : edge].reshape(DP, 2, 64, ADAPTERS)
    down_weight = jnp.concatenate(
        [
            folded[:, 0].reshape(UNITS, -1),
            folded[:, 1].reshape(UNITS, -1),
            lowers[:, 0].reshape(UNITS, -1),
        ],
        axis=1,
    )
    ffn_part, lower_down = forward(left_down, down_weight, down_raise, mask_ring)
    grad_a_down = contract_first(left_down, scaled_down)
    grad_b_down = contract_first(lower_down, cot_ring)
    (grad_resid_norm,) = ffn_norm_back(grad_left_gu)
    grad_residual = cotangent.astype(f32) + grad_resid_norm
    grad_ring = gather_ring(grad_residual.astype(bf16))
    grad_mixed, grad_a_out, grad_b_out = backward(
        left_out, lower_out, grad_ring, out_weight, out_raise, mask_ring
    )
    early = jnp.concatenate(
        [
            grad_a_out.astype(bf16).reshape(DP, -1, 128),
            blocks_of(grad_b_out.astype(bf16)),
            grad_a_gu.astype(bf16).reshape(DP, -1, 128),
            blocks_of(grad_b_gu.astype(bf16)),
            grad_a_down.astype(bf16).reshape(DP, -1, 128),
            blocks_of(grad_b_down.astype(bf16)),
        ],
        axis=1,
    )
    grad_mixed = grad_mixed.astype(bf16)
    low = jnp.concatenate([grad_mixed[:, :HEAD], grad_mixed[:, 2 * HEAD : 2 * HEAD + INNER]], axis=1)
    high = jnp.concatenate([grad_mixed[:, HEAD : 2 * HEAD], grad_mixed[:, 2 * HEAD + INNER :]], axis=1)
    kept = jnp.where(x == 0, low, high)
    received, grad_mixed = lax.optimization_barrier(
        (hop(jnp.where(x == 0, high, low), side), grad_mixed)
    )
    first = jnp.where(x == 0, kept, received).reshape(Y_RING, 1, tok_count, SLICE)
    second = jnp.where(x == 0, received, kept).reshape(Y_RING, 1, tok_count, SLICE)
    head_grads, early, ffn_part = lax.optimization_barrier(
        (from_ring(jnp.concatenate([first, second], axis=1)), halve_cores(early, d), ffn_part)
    )
    early = halve_neighbours(early, d)
    (ffn,) = scatter_ring(ffn_part)
    layer_out = (residual + ffn).astype(bf16)
    slope_ring = jnp.sum(
        grad_mixed[:, 2 * HEAD :].astype(f32) * gain_pair * gated_pair, axis=1
    ).reshape(Y_RING, tok_count)
    slope_own = sum_ring_small(
        lax.dynamic_slice_in_dim(
            jnp.concatenate([slope_ring, slope_ring], axis=0), (Y_RING - y) % Y_RING, Y_RING, 0
        )
    )
    slope_mate = hop(slope_own, side)
    slope = jnp.stack(
        [jnp.where(x == 0, slope_own, slope_mate), jnp.where(x == 0, slope_mate, slope_own)],
        axis=1,
    ).reshape(SEQ, tok_count)
    scales = jnp.stack(
        [inverse.reshape(-1), (inverse * inverse * inverse * slope / D_SSM).reshape(-1)], axis=1
    )
    grad_qkv = attention_backward(
        seq_lengths, projected, cosine_table, sine_table, head_grads, log_totals
    )
    grad_qkv, early = lax.optimization_barrier((grad_qkv, early))
    early = scatter_shards(early, Z_RINGS)
    grad_projected = scan_backward(
        seq_lengths,
        projected,
        convolved,
        scanned,
        states,
        head_grads,
        scales,
        grad_qkv,
        taps,
        rate_rows,
        skip_rows,
    )
    grad_projected, layer_out = lax.optimization_barrier((grad_projected, layer_out))
    grad_left_part, late = input_backward(
        grad_projected, left_in, lower_in, mask_all.astype(f32), in_all, in_raise
    )
    grad_left_part, early = lax.optimization_barrier((grad_left_part, early))
    late = halve_cores(late, d)
    grad_left_parts, late = lax.optimization_barrier(
        (exchange_seq(grad_left_part), scatter_shards(late, CHIPS))
    )
    grad_left = jnp.sum(grad_left_parts.astype(f32), axis=0)
    (grad_hidden_norm,) = norm_back(grad_left)
    grad_tokens = (grad_residual + grad_hidden_norm).astype(bf16)

    a_in_own = late[:128]
    b_in_own = row_from_blocks(late[128:240])
    a_out_block = early[:64].astype(bf16)
    b_out_own = early[64:192]
    a_gu_own = early[192:320]
    b_gu_own = early[320:448]
    a_down_own = early[448:512]
    b_down_own = early[512:640]
    zero_rows = jnp.zeros((256, 128), f32)
    a_out_own = lax.dynamic_update_slice_in_dim(
        zero_rows, jnp.where(own_rows, early[:64], 0.0), 64 * y, 0
    )
    for k in range(1, Y_RING):
        pairs = [(((i // 2 + k) % Y_RING) * SEQ + i, (i // 2) * SEQ + i) for i in range(SEQ)]
        moved = lax.ppermute(a_out_block, ("dp", "sp"), pairs)
        a_out_own = a_out_own + lax.dynamic_update_slice_in_dim(
            zero_rows, moved.astype(f32), 64 * ((y + k) % Y_RING), 0
        )
    a_down_own = lax.dynamic_update_slice_in_dim(zero_rows, a_down_own, 64 * y, 0)
    b_gu_full = lax.dynamic_update_slice_in_dim(
        jnp.zeros((8, 2 * DP, Y_RING, 64), f32),
        row_from_blocks(b_gu_own).reshape(8, 2 * DP, 1, 64),
        y,
        2,
    ).reshape(512, 128)

    def spread_heads(part, width):
        return lax.dynamic_update_slice(
            jnp.zeros((8, 12, Y_RING, width), f32),
            part.reshape(8, HEADS_DEV, 1, width),
            (0, HEADS_DEV * x, y, 0),
        ).reshape(8, -1)

    kv_width = H_KV * HEAD
    b_in_full = jnp.concatenate(
        [
            lax.dynamic_update_slice_in_dim(
                jnp.zeros((8, EDGE_INNER), f32), b_in_own[:, COL_Q:COL_INNER], s * HEAD, 1
            ),
            spread_heads(b_in_own[:, COL_INNER:COL_GATE], M_HEAD),
            lax.dynamic_update_slice_in_dim(
                jnp.zeros((8, kv_width), f32), b_in_own[:, COL_K:COL_V], kv_head * HEAD, 1
            ),
            lax.dynamic_update_slice_in_dim(
                jnp.zeros((8, kv_width), f32), b_in_own[:, COL_V:COL_BC], kv_head * HEAD, 1
            ),
            b_in_own[:, COL_BC:COL_STEP],
            spread_heads(b_in_own[:, COL_GATE:COL_K], M_HEAD),
            spread_heads(b_in_own[:, COL_STEP : COL_STEP + HEADS_DEV], 1),
            jnp.zeros((8, 80), f32),
        ],
        axis=1,
    )
    full = jnp.concatenate(
        [
            a_in_own,
            b_in_full.reshape(-1, 128),
            a_out_own,
            b_out_own,
            a_gu_own,
            b_gu_full,
            a_down_own,
            b_down_own,
        ],
        axis=0,
    )
    full = jnp.pad(full, ((0, (-full.shape[0]) % 128), (0, 0)))
    full = gather_seq(scatter_seq(full).astype(bf16)).astype(f32)
    out_a_in = full[:128]
    out_b_in = full[128:648].reshape(8, -1)[:, : EDGE_STEP + M_HEADS]
    full = full[648:]
    out_a_out = full[:256]
    out_b_out = row_from_blocks(full[256:384])
    out_a_gu = full[384:512]
    out_b_gu = full[512:1024].reshape(8, -1)
    out_a_down = full[1024:1280]
    out_b_down = row_from_blocks(full[1280:1408])
    return (
        layer_out,
        grad_tokens,
        out_a_in,
        out_b_in,
        out_a_out,
        out_b_out,
        out_a_gu,
        out_b_gu,
        out_a_down,
        out_b_down,
    )


def solution(mesh):
    rows = P("dp", None)
    both = P(("dp", "sp"), None)
    in_specs = (both, both) + (rows,) * 2 + (P(),) * 8 + (rows,) * 12
    out_specs = (both, both) + (rows,) * 8
    return jax.shard_map(
        per_device, mesh=mesh, in_specs=in_specs, out_specs=out_specs, check_vma=False
    )
```
